32 devices in a mesh: img: 4 (over y, x), tile: 8 (over z, core).
Axes of the slice: x: 2, y: 2, z: 4, core: 2. Of those that a mesh axis runs over, the one named last changes fastest.
Arguments:
- patches: bfloat16 [32, 32, 32, 768], P(('img', 'tile')), may hold values from -6 to 6
- norm_gain: float32 [768], replicated, may hold values from 0.1 to 1.9
- norm_bias: float32 [768], replicated, may hold values from -3 to 3
- up_weight: bfloat16 [768, 3072], replicated, may hold values from -0.21875 to 0.21875
- up_bias: float32 [3072], replicated, may hold values from -3 to 3
- down_weight: bfloat16 [3072, 768], replicated, may hold values from -0.109375 to 0.109375
- down_bias: float32 [768], replicated, may hold values from -3 to 3
- final_gain: float32 [768], replicated, may hold values from 0.1 to 1.9
- final_bias: float32 [768], replicated, may hold values from -3 to 3
- head_weight: bfloat16 [768, 512], replicated, may hold values from -0.21875 to 0.21875
- gauss_rows: bfloat16 [65536, 512], P(('img', 'tile')), may hold values from -48 to 48
- tile_lists: int32 [32, 32, 128], P('img', 'tile'), may hold values from 0 to 65535, as said below
- alphas: float32 [32, 32, 32, 128], P('img', 'tile'), may hold values from 0.002 to 0.05
Outputs:
- rendered: bfloat16 [32, 32, 32, 512], P('img', 'tile')
- feature_grad: float32 [65536, 512], P(('img', 'tile'))
The draws below stay inside these ranges and needn't reach their ends.
Inputs may be any that keep to these rules, and one draw needn't show every extreme that they name: `tile_lists`: among the 4096 entries of the tiles held by one device (one index of img and of tile), at most 256 name Gaussians held by any one device, the holder of id g being index g // 2048 of img+tile.
All inputs are finite; a program needn't handle non-finite values.
Results may differ from the reference program's by a relative error of at most 0.0049.
Values may be sent and summed in bfloat16 or wider, within the bound.
No kernel may reach another device: no remote copies, remote signals or barrier semaphores. Data moves between devices by JAX's collectives and lax.ppermute only.
A program may use at most 128 MiB of HBM per device.

```python
import math
import jax
import jax.numpy as jnp
from jax import lax

D = 768
FF = 3072
FEAT = 512
VIEW_DEV = 1
G_DEV = 2048
TILES_V = 32
TPIX = 32
LIST = 128
VIEWS = 32
NG = 65536
CAP = 256
N_IMG = 4
N_TILE = 8
DEVICES = 32


def draw_tile_lists(key, part):
    entries = VIEW_DEV * TILES_V * LIST
    slots = DEVICES * CAP
    common = jax.random.randint(jax.random.fold_in(key, 1), (), 0, DEVICES)
    label = jnp.arange(slots, dtype=jnp.int32) // CAP
    serial = jnp.arange(slots, dtype=jnp.int32)

    def one_device(device):
        dev_key = jax.random.fold_in(key, 100 + device)
        first, second, third = jax.random.split(dev_key, 3)
        scores = jax.random.randint(first, (slots,), 0, (1 << 30) // slots) * slots + serial
        scores = jnp.where(label == common, serial - slots, scores)
        order = jnp.argsort(scores, stable=True)
        chosen = label[order[:entries]]
        shuffle = jax.random.permutation(second, entries)
        owners = chosen[shuffle]
        local_rows = jax.random.randint(third, (entries,), 0, G_DEV)
        return owners * G_DEV + local_rows
    blocks = jax.vmap(one_device)(jnp.arange(DEVICES, dtype=jnp.int32))
    blocks = blocks.reshape(N_IMG, N_TILE, VIEW_DEV * N_TILE, TILES_V // N_TILE, LIST)
    blocks = blocks.transpose(0, 2, 1, 3, 4).reshape(VIEW_DEV * N_IMG * N_TILE, TILES_V, LIST)
    return blocks.astype(jnp.int32)


def block_scale(own_key, shape, cuts, least, top_value):
    loudness = 1.0
    for position, blocks in cuts:
        draws = jax.random.uniform(jax.random.fold_in(jax.random.fold_in(own_key, 6), position), (blocks,), jnp.float32, least / len(cuts), top_value / len(cuts))
        loudness = loudness * jnp.repeat(jnp.exp(draws), shape[position] // blocks).reshape((-1,) + (1,) * (len(shape) - 1 - position))
    return loudness


def scatter_about(rng, dims, scale, limit, cuts=(), kind=jnp.bfloat16):
    values = jax.random.normal(rng, dims, jnp.float32) * scale
    if len(cuts) > 0:
        values = block_scale(rng, dims, cuts, -0.22, 0.18) * values
    return jnp.clip(values, min=-limit, max=limit).astype(kind)


def setup_inputs(seed: int = 0) -> dict:
    keys = jax.random.split(jax.random.key(seed), 14)
    patches = scatter_about(keys[0], (VIEWS, TILES_V, TPIX, D), 1.0, 6.0, ((0, 32),))
    norm_gain = jnp.clip(1.0 + 0.18 * jax.random.normal(keys[1], (D,), jnp.float32), 0.1, 1.9)
    norm_bias = scatter_about(keys[2], (D,), 0.5, 3.0, (), jnp.float32)
    up_weight = scatter_about(keys[3], (D, FF), D ** -0.5, 0.21875)
    up_bias = scatter_about(keys[4], (FF,), 0.5, 3.0, (), jnp.float32)
    down_weight = scatter_about(keys[5], (FF, D), FF ** -0.5, 0.109375)
    down_bias = scatter_about(keys[6], (D,), 0.5, 3.0, (), jnp.float32)
    final_gain = jnp.clip(1.0 + 0.18 * jax.random.normal(keys[7], (D,), jnp.float32), 0.1, 1.9)
    final_bias = scatter_about(keys[8], (D,), 0.5, 3.0, (), jnp.float32)
    head_weight = scatter_about(keys[9], (D, FEAT), D ** -0.5, 0.21875)
    gauss_rows = scatter_about(keys[10], (NG, FEAT), 8.0, 48.0, ((0, 32),))
    tile_lists = draw_tile_lists(jax.random.fold_in(keys[13], 71), 0)
    alphas = jnp.clip(jnp.exp(math.log(0.05) - 3.218876 * jax.random.uniform(keys[12], (VIEWS, TILES_V, TPIX, LIST), jnp.float32) ** block_scale(keys[12], (VIEWS, TILES_V, TPIX, LIST), ((0, 4), (1, 8)), -0.2, 0.2)), 0.002, 0.05)
    return dict(patches=patches, norm_gain=norm_gain, norm_bias=norm_bias, up_weight=up_weight, up_bias=up_bias, down_weight=down_weight, down_bias=down_bias, final_gain=final_gain, final_bias=final_bias, head_weight=head_weight, gauss_rows=gauss_rows, tile_lists=tile_lists, alphas=alphas)


def layer_norm(rows, gain, bias):
    mean = lax.optimization_barrier(jnp.mean(rows, axis=-1, keepdims=True))
    centred = rows - mean
    var = lax.optimization_barrier(jnp.mean(centred * centred, axis=-1, keepdims=True))
    return centred * lax.rsqrt(var + 1e-05) * gain + bias

def encode(rows, norm_gain, norm_bias, up_weight, up_bias, down_weight, down_bias, final_gain, final_bias, head_weight):
    wide = rows.astype(jnp.float32)
    normed = layer_norm(wide, norm_gain, norm_bias).astype(jnp.bfloat16)
    inner = jnp.dot(normed, up_weight, preferred_element_type=jnp.float32) + up_bias
    act = (inner * jax.nn.sigmoid(1.702 * inner)).astype(jnp.bfloat16)
    block_out = wide + jnp.dot(act, down_weight, preferred_element_type=jnp.float32) + down_bias
    final = layer_norm(block_out, final_gain, final_bias).astype(jnp.bfloat16)
    embed = jnp.dot(final, head_weight, preferred_element_type=jnp.float32)
    scale = lax.rsqrt(lax.optimization_barrier(jnp.mean(embed * embed, axis=-1, keepdims=True)) + 1e-06)
    return (embed * scale).astype(jnp.bfloat16)

def reference(patches, norm_gain, norm_bias, up_weight, up_bias, down_weight, down_bias, final_gain, final_bias, head_weight, gauss_rows, tile_lists, alphas):

    def per_view(grad_sum, view):
        rows_view = lax.dynamic_index_in_dim(patches, view, 0, keepdims=False)
        target = encode(rows_view.reshape(TILES_V * TPIX, D), norm_gain, norm_bias, up_weight, up_bias, down_weight, down_bias, final_gain, final_bias, head_weight)
        target = target.reshape(TILES_V, TPIX, FEAT)
        ids_view = lax.dynamic_index_in_dim(tile_lists, view, 0, keepdims=False)
        alpha_view = lax.dynamic_index_in_dim(alphas, view, 0, keepdims=False)
        fetched = gauss_rows[ids_view.reshape(-1)].reshape(TILES_V, LIST, FEAT)
        logs = jnp.log1p(-alpha_view)
        trans = jnp.exp(jnp.cumsum(logs, axis=-1) - logs)
        weight = (alpha_view * trans).astype(jnp.bfloat16)
        color = jnp.einsum('tpl,tlf->tpf', weight.astype(jnp.float32), fetched.astype(jnp.float32))
        diff = (color - target.astype(jnp.float32)).astype(jnp.bfloat16)
        term = jnp.einsum('tpl,tpf->tlf', weight.astype(jnp.float32), diff.astype(jnp.float32)).astype(jnp.bfloat16)
        grad_sum = grad_sum.at[ids_view.reshape(-1)].add(term.reshape(TILES_V * LIST, FEAT).astype(jnp.float32))
        return (grad_sum, color.astype(jnp.bfloat16))
    start = jnp.zeros((NG, FEAT), jnp.float32)
    feature_grad, rendered = lax.scan(per_view, start, jnp.arange(VIEWS, dtype=jnp.int32))
    return (rendered, feature_grad)
```

```python
import functools

import jax
import jax.numpy as jnp
from jax import lax
from jax.experimental import pallas as pl
from jax.experimental.pallas import tpu as pltpu
from jax.sharding import PartitionSpec as P

F32 = jnp.float32
BF16 = jnp.bfloat16
I32 = jnp.int32
VMEM_BYTES = 50 * 1024 * 1024
LANES = (((1,), (1,)), ((), ()))
ROWS = (((0,), (0,)), ((), ()))


def params():
    return pltpu.CompilerParams(vmem_limit_bytes=VMEM_BYTES)


def index_kernel(peers, cap, rows_held, ids_ref, req_ref, own_ref, rank_ref):
    tiles, length = ids_ref.shape
    earlier = lax.broadcasted_iota(I32, (length, length), 0)
    later = lax.broadcasted_iota(I32, (length, length), 1)
    upper = (earlier < later).astype(BF16)
    every = jnp.ones((length, length), BF16)
    peer_id = lax.broadcasted_iota(I32, (peers, length), 0)
    slot_id = lax.broadcasted_iota(I32, (cap, length), 0)
    hots = []
    for t in range(tiles):
        owner = ids_ref[t : t + 1, :] // rows_held
        own_ref[t : t + 1, :] = owner
        hots.append((jnp.broadcast_to(owner, (peers, length)) == peer_id).astype(F32))
    stack = jnp.concatenate(hots, 0).astype(BF16)
    within = jnp.dot(stack, upper, preferred_element_type=F32)
    totals = jnp.dot(stack, every, preferred_element_type=F32)
    offset = jnp.zeros((peers, length), F32)
    found = jnp.zeros((2 * peers, cap), F32)
    for t in range(tiles):
        own_rows = slice(t * peers, (t + 1) * peers)
        rank = jnp.sum(hots[t] * (within[own_rows] + offset), axis=0, keepdims=True).astype(I32)
        offset = offset + totals[own_rows]
        rank_ref[t : t + 1, :] = rank
        ids = ids_ref[t : t + 1, :]
        row = ids - (ids // rows_held) * rows_held + 1
        high = (row >> 6).astype(F32)
        low = (row & 63).astype(F32)
        digits = jnp.concatenate([hots[t] * high, hots[t] * low], 0).astype(BF16)
        slots = (jnp.broadcast_to(rank, (cap, length)) == slot_id).astype(F32).astype(BF16)
        found = found + lax.dot_general(digits, slots, LANES, preferred_element_type=F32)
    req_ref[...] = (found[:peers] * 64.0 + found[peers:]).astype(I32) - 1


def index(ids, peers, cap, rows_held):
    like = jax.ShapeDtypeStruct(ids.shape, I32)
    return pl.pallas_call(
        functools.partial(index_kernel, peers, cap, rows_held),
        out_shape=(jax.ShapeDtypeStruct((peers, cap), I32), like, like),
        compiler_params=params(),
        cost_estimate=pl.CostEstimate(flops=10**9, bytes_accessed=10**7, transcendentals=0),
        name="index",
    )(ids)


def weights_kernel(alpha_ref, out_ref):
    alpha = alpha_ref[...]
    length = alpha.shape[1]
    logs = jnp.log1p(-alpha)
    earlier = lax.broadcasted_iota(I32, (length, length), 0)
    later = lax.broadcasted_iota(I32, (length, length), 1)
    upper = (earlier < later).astype(F32)
    before = jnp.dot(logs, upper, preferred_element_type=F32, precision=lax.Precision.HIGHEST)
    out_ref[...] = (alpha * jnp.exp(before)).astype(BF16)


def weights(alphas):
    return pl.pallas_call(
        weights_kernel,
        out_shape=jax.ShapeDtypeStruct(alphas.shape, BF16),
        compiler_params=params(),
        cost_estimate=pl.CostEstimate(flops=10**9, bytes_accessed=10**7, transcendentals=0),
        name="weights",
    )(alphas)


def spread_kernel(near, cap, own_ref, rank_ref, weight_ref, out_ref):
    t = pl.program_id(0)
    own = own_ref[pl.ds(t, 1), :]
    rank = rank_ref[pl.ds(t, 1), :]
    weight = weight_ref[...].astype(F32)
    cells, length = weight.shape
    by_owner = jnp.concatenate([jnp.where(own == o, weight, 0.0) for o in range(near)], 0).astype(BF16)
    slot_id = lax.broadcasted_iota(I32, (cap, length), 0)
    slots = (jnp.broadcast_to(rank, (cap, length)) == slot_id).astype(F32).astype(BF16)
    moved = lax.dot_general(by_owner, slots, LANES, preferred_element_type=F32).astype(BF16)
    if cap % 128 == 0:
        for o in range(near):
            out_ref[:, o * cap : (o + 1) * cap] = moved[o * cells : (o + 1) * cells]
    else:
        out_ref[...] = jnp.concatenate([moved[o * cells : (o + 1) * cells] for o in range(near)], 1)


def spread(own, rank, weight, near, cap):
    tiles, length = own.shape
    cells = weight.shape[0] // tiles
    whole = pl.BlockSpec((tiles, length), lambda t: (0, 0))
    return pl.pallas_call(
        functools.partial(spread_kernel, near, cap),
        grid=(tiles,),
        in_specs=[whole, whole, pl.BlockSpec((cells, length), lambda t: (t, 0))],
        out_specs=pl.BlockSpec((cells, near * cap), lambda t: (t, 0)),
        out_shape=jax.ShapeDtypeStruct((weight.shape[0], near * cap), BF16),
        compiler_params=params(),
        cost_estimate=pl.CostEstimate(flops=15 * 10**9, bytes_accessed=10**7, transcendentals=0),
        name="spread",
    )(own, rank, weight)


def gather_kernel(group, cap, asked_ref, rows_ref, out_ref):
    first = pl.program_id(0) * group
    asked = asked_ref[...]
    peer = lax.broadcasted_iota(I32, asked.shape, 1)
    held = rows_ref.shape[0]
    row_id = lax.broadcasted_iota(I32, (cap, held), 1)
    picks = []
    for q in range(group):
        column = jnp.sum(jnp.where(peer == first + q, asked, 0), axis=1, keepdims=True)
        picks.append((jnp.broadcast_to(column, (cap, held)) == row_id).astype(F32).astype(BF16))
    pick = jnp.concatenate(picks, 0)
    out_ref[...] = jnp.dot(pick, rows_ref[...], preferred_element_type=F32).astype(BF16)


def gather(asked, rows):
    near, cap = asked.shape
    held, feat = rows.shape
    group = max(1, min(near, 1024 // cap))
    return pl.pallas_call(
        functools.partial(gather_kernel, group, cap),
        grid=(near // group,),
        in_specs=[pl.BlockSpec((cap, near), lambda i: (0, 0)), pl.BlockSpec((held, feat), lambda i: (0, 0))],
        out_specs=pl.BlockSpec((group * cap, feat), lambda i: (i, 0)),
        out_shape=jax.ShapeDtypeStruct((near * cap, feat), BF16),
        compiler_params=params(),
        cost_estimate=pl.CostEstimate(flops=10**10, bytes_accessed=10**7, transcendentals=0),
        name="gather",
    )(asked.T, rows)


def blend_kernel(weight_ref, rows_ref, out_ref):
    out_ref[...] = jnp.dot(weight_ref[...], rows_ref[...], preferred_element_type=F32).astype(BF16)


def blend_rest_kernel(weight_ref, rows_ref, part_ref, target_ref, color_ref, diff_ref):
    color = jnp.dot(weight_ref[...], rows_ref[...], preferred_element_type=F32) + part_ref[...].astype(F32)
    color_ref[...] = color.astype(BF16)
    diff_ref[...] = (color - target_ref[...].astype(F32)).astype(BF16)


def blend(weight, rows, part=None, target=None):
    cells, slots = weight.shape
    feat = rows.shape[1]
    block = min(cells, 512)
    cell_block = pl.BlockSpec((block, feat), lambda i: (i, 0))
    out = jax.ShapeDtypeStruct((cells, feat), BF16)
    in_specs = [pl.BlockSpec((block, slots), lambda i: (i, 0)), pl.BlockSpec((slots, feat), lambda i: (0, 0))]
    rest = part is not None
    return pl.pallas_call(
        blend_rest_kernel if rest else blend_kernel,
        grid=(cells // block,),
        in_specs=in_specs + [cell_block] * (2 * rest),
        out_specs=(cell_block, cell_block) if rest else cell_block,
        out_shape=(out, out) if rest else out,
        compiler_params=params(),
        cost_estimate=pl.CostEstimate(flops=8 * 10**9, bytes_accessed=10**7, transcendentals=0),
        name="blend",
    )(weight, rows, *((part, target) if rest else ()))


def terms_kernel(weight_ref, diff_ref, out_ref):
    out_ref[...] = lax.dot_general(weight_ref[...], diff_ref[...], ROWS, preferred_element_type=F32).astype(BF16)


def terms(weight, diff):
    cells, slots = weight.shape
    feat = diff.shape[1]
    block = min(slots, 1024)
    return pl.pallas_call(
        terms_kernel,
        grid=(slots // block,),
        in_specs=[pl.BlockSpec((cells, block), lambda i: (0, i)), pl.BlockSpec((cells, feat), lambda i: (0, 0))],
        out_specs=pl.BlockSpec((block, feat), lambda i: (i, 0)),
        out_shape=jax.ShapeDtypeStruct((slots, feat), BF16),
        compiler_params=params(),
        cost_estimate=pl.CostEstimate(flops=8 * 10**9, bytes_accessed=10**7, transcendentals=0),
        name="terms",
    )(weight, diff)


def add_rows_kernel(asked_ref, terms_ref, *rest):
    out_ref = rest[-1]
    block = out_ref.shape[0]
    near, cap = asked_ref.shape
    row_id = lax.broadcasted_iota(I32, (block, cap), 0) + pl.program_id(0) * block
    picks = []
    for o in range(near):
        asked = jnp.broadcast_to(asked_ref[o : o + 1, :], (block, cap))
        picks.append((asked == row_id).astype(F32).astype(BF16))
    total = jnp.dot(jnp.concatenate(picks, 1), terms_ref[...], preferred_element_type=F32)
    out_ref[...] = total if len(rest) == 1 else total + rest[0][...]


def add_rows(asked, arrived, held, before=None):
    near, cap = asked.shape
    feat = arrived.shape[1]
    block = min(held, 512)
    row_block = pl.BlockSpec((block, feat), lambda i: (i, 0))
    more = before is not None
    in_specs = [pl.BlockSpec((near, cap), lambda i: (0, 0)), pl.BlockSpec((near * cap, feat), lambda i: (0, 0))]
    return pl.pallas_call(
        add_rows_kernel,
        grid=(held // block,),
        in_specs=in_specs + [row_block] * more,
        out_specs=row_block,
        out_shape=jax.ShapeDtypeStruct((held, feat), F32),
        compiler_params=params(),
        cost_estimate=pl.CostEstimate(flops=10**10, bytes_accessed=10**7, transcendentals=0),
        name="add_rows",
    )(asked, arrived, *((before,) if more else ()))


def layer_norm(rows, gain, bias):
    mean = jnp.mean(rows, axis=-1, keepdims=True)
    centred = rows - mean
    var = jnp.mean(centred * centred, axis=-1, keepdims=True)
    return centred * lax.rsqrt(var + 1e-05) * gain + bias


def on_device(
    patches,
    norm_gain,
    norm_bias,
    up_weight,
    up_bias,
    down_weight,
    down_bias,
    final_gain,
    final_bias,
    head_weight,
    gauss_rows,
    tile_lists,
    alphas,
):
    view_count, tiles_view, cells, width = patches.shape
    feat = head_weight.shape[1]
    n_img = lax.axis_size("img")
    n_tile = lax.axis_size("tile")
    peers = n_img * n_tile
    both = ("img", "tile")
    held = gauss_rows.shape[0]
    group_views, strip_tiles, list_len = tile_lists.shape
    tiles = group_views * strip_tiles
    cap = 2 * tiles * list_len // peers

    n_half = n_tile // 2
    near = n_img * n_half
    half = lax.axis_index("tile") // n_half
    mirror_of = [(n_half // 2 - 1 - k // 2) * 2 + k % 2 for k in range(n_half)] if n_half % 2 == 0 else list(range(n_half))
    groups = [[i * n_tile + h * n_half + k for i in range(n_img) for k in range(n_half)] for h in range(2)]
    crossing = [
        (i * n_tile + h * n_half + k, i * n_tile + (1 - h) * n_half + mirror_of[k])
        for i in range(n_img)
        for h in range(2)
        for k in range(n_half)
    ]

    def cross(x):
        return lax.ppermute(x, both, crossing)

    def exchange(x):
        return lax.all_to_all(x, both, split_axis=0, concat_axis=0, axis_index_groups=groups, tiled=True)

    def near_owner(own):
        img = own // n_tile
        tile = own - img * n_tile
        place = tile - half * n_half
        return jnp.where((place >= 0) & (place < n_half), img * n_half + place, -1)

    request, own, rank = index(tile_lists.reshape(tiles, list_len), peers, cap, held)
    asked = lax.all_to_all(request, both, split_axis=0, concat_axis=0, tiled=True)
    weight = weights(alphas.reshape(tiles * cells, list_len))
    code_far = cross(own * cap + rank)
    weight_far = cross(weight)

    wide = patches.reshape(-1, width).astype(F32)
    normed = layer_norm(wide, norm_gain, norm_bias).astype(BF16)
    inner = jnp.dot(normed, up_weight, preferred_element_type=F32) + up_bias
    act = (inner * jax.nn.sigmoid(1.702 * inner)).astype(BF16)
    block_out = wide + jnp.dot(act, down_weight, preferred_element_type=F32) + down_bias
    final = layer_norm(block_out, final_gain, final_bias).astype(BF16)
    embed = jnp.dot(final, head_weight, preferred_element_type=F32)
    scale = lax.rsqrt(jnp.mean(embed * embed, axis=-1, keepdims=True) + 1e-06)
    target = (embed * scale).astype(BF16).reshape(view_count, tiles_view, cells, feat)
    target = lax.all_to_all(target, "tile", split_axis=1, concat_axis=0, tiled=True)
    target = target.reshape(tiles * cells, feat)

    asked = asked.reshape(n_img, 2, n_half, cap)
    asked_near = lax.dynamic_index_in_dim(asked, half, 1, keepdims=False).reshape(near, cap)
    asked_far = lax.dynamic_index_in_dim(asked, 1 - half, 1, keepdims=False)
    asked_far = jnp.stack([asked_far[:, mirror_of[k]] for k in range(n_half)], 1).reshape(near, cap)

    rows_far = exchange(gather(asked_far, gauss_rows))
    spread_far = spread(near_owner(code_far // cap), code_far % cap, weight_far, near, cap)
    part = cross(blend(spread_far, rows_far))
    looked = gather(asked_near, gauss_rows)
    looked, rows_far = lax.optimization_barrier((looked, rows_far))
    rows_near = exchange(looked)
    spread_near = spread(near_owner(own), rank, weight, near, cap)
    color, diff = blend(spread_near, rows_near, part, target)

    diff_far = cross(diff)
    back_near = exchange(terms(spread_near, diff))
    term_far = terms(spread_far, diff_far)
    term_far, back_near = lax.optimization_barrier((term_far, back_near))
    back_far = exchange(term_far)
    grad = add_rows(asked_near, back_near, held)
    grad = add_rows(asked_far, back_far, held, grad)
    return (color.reshape(group_views, strip_tiles, cells, feat), grad)


def solution(mesh):
    placed = (
        P(("img", "tile"), None, None, None),
        P(),
        P(),
        P(),
        P(),
        P(),
        P(),
        P(),
        P(),
        P(),
        P(("img", "tile"), None),
        P("img", "tile", None),
        P("img", "tile", None, None),
    )
    return jax.shard_map(
        on_device,
        mesh=mesh,
        in_specs=placed,
        out_specs=(P("img", "tile", None, None), P(("img", "tile"), None)),
        check_vma=False,
    )
```

```python
import functools

import jax
import jax.numpy as jnp
from jax import lax
from jax.experimental import pallas as pl
from jax.experimental.pallas import tpu as pltpu
from jax.sharding import PartitionSpec as P

F32 = jnp.float32
BF16 = jnp.bfloat16
I32 = jnp.int32
VMEM_BYTES = 50 * 1024 * 1024
LANES = (((1,), (1,)), ((), ()))
ROWS = (((0,), (0,)), ((), ()))


def params():
    return pltpu.CompilerParams(vmem_limit_bytes=VMEM_BYTES)


def index_kernel(peers, cap, rows_held, ids_ref, req_ref, own_ref, rank_ref):
    tiles, length = ids_ref.shape
    earlier = lax.broadcasted_iota(I32, (length, length), 0)
    later = lax.broadcasted_iota(I32, (length, length), 1)
    upper = (earlier < later).astype(BF16)
    every = jnp.ones((length, length), BF16)
    peer_id = lax.broadcasted_iota(I32, (peers, length), 0)
    slot_id = lax.broadcasted_iota(I32, (cap, length), 0)
    hots = []
    for t in range(tiles):
        owner = ids_ref[t : t + 1, :] // rows_held
        own_ref[t : t + 1, :] = owner
        hots.append((jnp.broadcast_to(owner, (peers, length)) == peer_id).astype(F32))
    stack = jnp.concatenate(hots, 0).astype(BF16)
    within = jnp.dot(stack, upper, preferred_element_type=F32)
    totals = jnp.dot(stack, every, preferred_element_type=F32)
    offset = jnp.zeros((peers, length), F32)
    found = jnp.zeros((2 * peers, cap), F32)
    for t in range(tiles):
        own_rows = slice(t * peers, (t + 1) * peers)
        rank = jnp.sum(hots[t] * (within[own_rows] + offset), axis=0, keepdims=True).astype(I32)
        offset = offset + totals[own_rows]
        rank_ref[t : t + 1, :] = rank
        ids = ids_ref[t : t + 1, :]
        row = ids - (ids // rows_held) * rows_held + 1
        high = (row >> 6).astype(F32)
        low = (row & 63).astype(F32)
        digits = jnp.concatenate([hots[t] * high, hots[t] * low], 0).astype(BF16)
        slots = (jnp.broadcast_to(rank, (cap, length)) == slot_id).astype(F32).astype(BF16)
        found = found + lax.dot_general(digits, slots, LANES, preferred_element_type=F32)
    req_ref[...] = (found[:peers] * 64.0 + found[peers:]).astype(I32) - 1


def index(ids, peers, cap, rows_held):
    like = jax.ShapeDtypeStruct(ids.shape, I32)
    return pl.pallas_call(
        functools.partial(index_kernel, peers, cap, rows_held),
        out_shape=(jax.ShapeDtypeStruct((peers, cap), I32), like, like),
        compiler_params=params(),
        cost_estimate=pl.CostEstimate(flops=10**9, bytes_accessed=10**7, transcendentals=0),
        name="index",
    )(ids)


def weights_kernel(alpha_ref, out_ref):
    alpha = alpha_ref[...]
    length = alpha.shape[1]
    logs = jnp.log1p(-alpha)
    earlier = lax.broadcasted_iota(I32, (length, length), 0)
    later = lax.broadcasted_iota(I32, (length, length), 1)
    upper = (earlier < later).astype(F32)
    before = jnp.dot(logs, upper, preferred_element_type=F32, precision=lax.Precision.HIGHEST)
    out_ref[...] = (alpha * jnp.exp(before)).astype(BF16)


def weights(alphas):
    return pl.pallas_call(
        weights_kernel,
        out_shape=jax.ShapeDtypeStruct(alphas.shape, BF16),
        compiler_params=params(),
        cost_estimate=pl.CostEstimate(flops=10**9, bytes_accessed=10**7, transcendentals=0),
        name="weights",
    )(alphas)


def spread_kernel(near, cap, own_ref, rank_ref, weight_ref, out_ref):
    t = pl.program_id(0)
    own = own_ref[pl.ds(t, 1), :]
    rank = rank_ref[pl.ds(t, 1), :]
    weight = weight_ref[...].astype(F32)
    cells, length = weight.shape
    by_owner = jnp.concatenate([jnp.where(own == o, weight, 0.0) for o in range(near)], 0).astype(BF16)
    slot_id = lax.broadcasted_iota(I32, (cap, length), 0)
    slots = (jnp.broadcast_to(rank, (cap, length)) == slot_id).astype(F32).astype(BF16)
    moved = lax.dot_general(by_owner, slots, LANES, preferred_element_type=F32).astype(BF16)
    if cap % 128 == 0:
        for o in range(near):
            out_ref[:, o * cap : (o + 1) * cap] = moved[o * cells : (o + 1) * cells]
    else:
        out_ref[...] = jnp.concatenate([moved[o * cells : (o + 1) * cells] for o in range(near)], 1)


def spread(own, rank, weight, near, cap):
    tiles, length = own.shape
    cells = weight.shape[0] // tiles
    whole = pl.BlockSpec((tiles, length), lambda t: (0, 0))
    return pl.pallas_call(
        functools.partial(spread_kernel, near, cap),
        grid=(tiles,),
        in_specs=[whole, whole, pl.BlockSpec((cells, length), lambda t: (t, 0))],
        out_specs=pl.BlockSpec((cells, near * cap), lambda t: (t, 0)),
        out_shape=jax.ShapeDtypeStruct((weight.shape[0], near * cap), BF16),
        compiler_params=params(),
        cost_estimate=pl.CostEstimate(flops=15 * 10**9, bytes_accessed=10**7, transcendentals=0),
        name="spread",
    )(own, rank, weight)


def gather_kernel(group, cap, asked_ref, rows_ref, out_ref):
    first = pl.program_id(0) * group
    asked = asked_ref[...]
    peer = lax.broadcasted_iota(I32, asked.shape, 1)
    held = rows_ref.shape[0]
    row_id = lax.broadcasted_iota(I32, (cap, held), 1)
    picks = []
    for q in range(group):
        column = jnp.sum(jnp.where(peer == first + q, asked, 0), axis=1, keepdims=True)
        picks.append((jnp.broadcast_to(column, (cap, held)) == row_id).astype(F32).astype(BF16))
    pick = jnp.concatenate(picks, 0)
    out_ref[...] = jnp.dot(pick, rows_ref[...], preferred_element_type=F32).astype(BF16)


def gather(asked, rows):
    near, cap = asked.shape
    held, feat = rows.shape
    group = max(1, min(near, 1024 // cap))
    return pl.pallas_call(
        functools.partial(gather_kernel, group, cap),
        grid=(near // group,),
        in_specs=[pl.BlockSpec((cap, near), lambda i: (0, 0)), pl.BlockSpec((held, feat), lambda i: (0, 0))],
        out_specs=pl.BlockSpec((group * cap, feat), lambda i: (i, 0)),
        out_shape=jax.ShapeDtypeStruct((near * cap, feat), BF16),
        compiler_params=params(),
        cost_estimate=pl.CostEstimate(flops=10**10, bytes_accessed=10**7, transcendentals=0),
        name="gather",
    )(asked.T, rows)


def blend_kernel(weight_ref, rows_ref, out_ref):
    out_ref[...] = jnp.dot(weight_ref[...], rows_ref[...], preferred_element_type=F32).astype(BF16)


def blend_rest_kernel(weight_ref, rows_ref, part_ref, target_ref, color_ref, diff_ref):
    color = jnp.dot(weight_ref[...], rows_ref[...], preferred_element_type=F32) + part_ref[...].astype(F32)
    color_ref[...] = color.astype(BF16)
    diff_ref[...] = (color - target_ref[...].astype(F32)).astype(BF16)


def blend(weight, rows, part=None, target=None):
    cells, slots = weight.shape
    feat = rows.shape[1]
    block = min(cells, 512)
    cell_block = pl.BlockSpec((block, feat), lambda i: (i, 0))
    out = jax.ShapeDtypeStruct((cells, feat), BF16)
    in_specs = [pl.BlockSpec((block, slots), lambda i: (i, 0)), pl.BlockSpec((slots, feat), lambda i: (0, 0))]
    rest = part is not None
    return pl.pallas_call(
        blend_rest_kernel if rest else blend_kernel,
        grid=(cells // block,),
        in_specs=in_specs + [cell_block] * (2 * rest),
        out_specs=(cell_block, cell_block) if rest else cell_block,
        out_shape=(out, out) if rest else out,
        compiler_params=params(),
        cost_estimate=pl.CostEstimate(flops=8 * 10**9, bytes_accessed=10**7, transcendentals=0),
        name="blend",
    )(weight, rows, *((part, target) if rest else ()))


def terms_kernel(weight_ref, diff_ref, out_ref):
    out_ref[...] = lax.dot_general(weight_ref[...], diff_ref[...], ROWS, preferred_element_type=F32).astype(BF16)


def terms(weight, diff):
    cells, slots = weight.shape
    feat = diff.shape[1]
    block = min(slots, 1024)
    return pl.pallas_call(
        terms_kernel,
        grid=(slots // block,),
        in_specs=[pl.BlockSpec((cells, block), lambda i: (0, i)), pl.BlockSpec((cells, feat), lambda i: (0, 0))],
        out_specs=pl.BlockSpec((block, feat), lambda i: (i, 0)),
        out_shape=jax.ShapeDtypeStruct((slots, feat), BF16),
        compiler_params=params(),
        cost_estimate=pl.CostEstimate(flops=8 * 10**9, bytes_accessed=10**7, transcendentals=0),
        name="terms",
    )(weight, diff)


def add_rows_kernel(asked_ref, terms_ref, *rest):
    out_ref = rest[-1]
    block = out_ref.shape[0]
    near, cap = asked_ref.shape
    row_id = lax.broadcasted_iota(I32, (block, cap), 0) + pl.program_id(0) * block
    picks = []
    for o in range(near):
        asked = jnp.broadcast_to(asked_ref[o : o + 1, :], (block, cap))
        picks.append((asked == row_id).astype(F32).astype(BF16))
    total = jnp.dot(jnp.concatenate(picks, 1), terms_ref[...], preferred_element_type=F32)
    out_ref[...] = total if len(rest) == 1 else total + rest[0][...]


def add_rows(asked, arrived, held, before=None):
    near, cap = asked.shape
    feat = arrived.shape[1]
    block = min(held, 512)
    row_block = pl.BlockSpec((block, feat), lambda i: (i, 0))
    more = before is not None
    in_specs = [pl.BlockSpec((near, cap), lambda i: (0, 0)), pl.BlockSpec((near * cap, feat), lambda i: (0, 0))]
    return pl.pallas_call(
        add_rows_kernel,
        grid=(held // block,),
        in_specs=in_specs + [row_block] * more,
        out_specs=row_block,
        out_shape=jax.ShapeDtypeStruct((held, feat), F32),
        compiler_params=params(),
        cost_estimate=pl.CostEstimate(flops=10**10, bytes_accessed=10**7, transcendentals=0),
        name="add_rows",
    )(asked, arrived, *((before,) if more else ()))


def layer_norm(rows, gain, bias):
    mean = jnp.mean(rows, axis=-1, keepdims=True)
    centred = rows - mean
    var = jnp.mean(centred * centred, axis=-1, keepdims=True)
    return centred * lax.rsqrt(var + 1e-05) * gain + bias


def on_device(
    patches,
    norm_gain,
    norm_bias,
    up_weight,
    up_bias,
    down_weight,
    down_bias,
    final_gain,
    final_bias,
    head_weight,
    gauss_rows,
    tile_lists,
    alphas,
):
    view_count, tiles_view, cells, width = patches.shape
    feat = head_weight.shape[1]
    n_img = lax.axis_size("img")
    n_tile = lax.axis_size("tile")
    peers = n_img * n_tile
    both = ("img", "tile")
    held = gauss_rows.shape[0]
    group_views, strip_tiles, list_len = tile_lists.shape
    tiles = group_views * strip_tiles
    cap = 2 * tiles * list_len // peers

    n_half = n_tile // 2
    near = n_img * n_half
    half = lax.axis_index("tile") // n_half
    mirror_of = [(n_half // 2 - 1 - k // 2) * 2 + k % 2 for k in range(n_half)] if n_half % 2 == 0 else list(range(n_half))
    groups = [[i * n_tile + h * n_half + k for i in range(n_img) for k in range(n_half)] for h in range(2)]
    crossing = [
        (i * n_tile + h * n_half + k, i * n_tile + (1 - h) * n_half + mirror_of[k])
        for i in range(n_img)
        for h in range(2)
        for k in range(n_half)
    ]

    def cross(x):
        return lax.ppermute(x, both, crossing)

    def exchange(x):
        return lax.all_to_all(x, both, split_axis=0, concat_axis=0, axis_index_groups=groups, tiled=True)

    def near_owner(own):
        img = own // n_tile
        tile = own - img * n_tile
        place = tile - half * n_half
        return jnp.where((place >= 0) & (place < n_half), img * n_half + place, -1)

    request, own, rank = index(tile_lists.reshape(tiles, list_len), peers, cap, held)
    weight = weights(alphas.reshape(tiles * cells, list_len))
    request, code, weight = lax.optimization_barrier((request, own * cap + rank, weight))
    code_far = cross(code)
    weight_far = cross(weight)
    asked = lax.all_to_all(request, both, split_axis=0, concat_axis=0, tiled=True)
    asked, code_far, weight_far = lax.optimization_barrier((asked, code_far, weight_far))

    asked = asked.reshape(n_img, 2, n_half, cap)
    asked_near = lax.dynamic_index_in_dim(asked, half, 1, keepdims=False).reshape(near, cap)
    asked_far = lax.dynamic_index_in_dim(asked, 1 - half, 1, keepdims=False)
    asked_far = jnp.stack([asked_far[:, mirror_of[k]] for k in range(n_half)], 1).reshape(near, cap)

    looked_far = gather(asked_far, gauss_rows)
    looked_far, patches = lax.optimization_barrier((looked_far, patches))
    rows_far = exchange(looked_far)

    wide = patches.reshape(-1, width).astype(F32)
    normed = layer_norm(wide, norm_gain, norm_bias).astype(BF16)
    inner = jnp.dot(normed, up_weight, preferred_element_type=F32) + up_bias
    act = (inner * jax.nn.sigmoid(1.702 * inner)).astype(BF16)
    block_out = wide + jnp.dot(act, down_weight, preferred_element_type=F32) + down_bias
    final = layer_norm(block_out, final_gain, final_bias).astype(BF16)
    embed = jnp.dot(final, head_weight, preferred_element_type=F32)
    scale = lax.rsqrt(jnp.mean(embed * embed, axis=-1, keepdims=True) + 1e-06)
    target = (embed * scale).astype(BF16).reshape(view_count, tiles_view, cells, feat)
    target, asked_near, code_far, weight_far = lax.optimization_barrier((target, asked_near, code_far, weight_far))
    target = lax.all_to_all(target, "tile", split_axis=1, concat_axis=0, tiled=True)
    target = target.reshape(tiles * cells, feat)
    looked_near = gather(asked_near, gauss_rows)
    spread_far = spread(near_owner(code_far // cap), code_far % cap, weight_far, near, cap)

    looked_near, rows_far, spread_far, target, own = lax.optimization_barrier(
        (looked_near, rows_far, spread_far, target, own)
    )
    rows_near = exchange(looked_near)
    part = cross(blend(spread_far, rows_far))
    spread_near = spread(near_owner(own), rank, weight, near, cap)
    part, rows_near, spread_near = lax.optimization_barrier((part, rows_near, spread_near))
    color, diff = blend(spread_near, rows_near, part, target)

    diff_far = cross(diff)
    back_near = exchange(terms(spread_near, diff))
    term_far = terms(spread_far, diff_far)
    term_far, back_near = lax.optimization_barrier((term_far, back_near))
    back_far = exchange(term_far)
    grad = add_rows(asked_near, back_near, held)
    grad = add_rows(asked_far, back_far, held, grad)
    return (color.reshape(group_views, strip_tiles, cells, feat), grad)


def solution(mesh):
    placed = (
        P(("img", "tile"), None, None, None),
        P(),
        P(),
        P(),
        P(),
        P(),
        P(),
        P(),
        P(),
        P(),
        P(("img", "tile"), None),
        P("img", "tile", None),
        P("img", "tile", None, None),
    )
    return jax.shard_map(
        on_device,
        mesh=mesh,
        in_specs=placed,
        out_specs=(P("img", "tile", None, None), P(("img", "tile"), None)),
        check_vma=False,
    )
```

```python
import functools

import jax
import jax.numpy as jnp
from jax import lax
from jax.experimental import pallas as pl
from jax.experimental.pallas import tpu as pltpu
from jax.sharding import PartitionSpec as P

F32 = jnp.float32
BF16 = jnp.bfloat16
I32 = jnp.int32
VMEM_BYTES = 50 * 1024 * 1024
LANES = (((1,), (1,)), ((), ()))
ROWS = (((0,), (0,)), ((), ()))


def params():
    return pltpu.CompilerParams(vmem_limit_bytes=VMEM_BYTES)


def index_kernel(peers, cap, rows_held, ids_ref, req_ref, own_ref, rank_ref):
    tiles, length = ids_ref.shape
    earlier = lax.broadcasted_iota(I32, (length, length), 0)
    later = lax.broadcasted_iota(I32, (length, length), 1)
    upper = (earlier < later).astype(BF16)
    every = jnp.ones((length, length), BF16)
    peer_id = lax.broadcasted_iota(I32, (peers, length), 0)
    slot_id = lax.broadcasted_iota(I32, (cap, length), 0)
    hots = []
    for t in range(tiles):
        owner = ids_ref[t : t + 1, :] // rows_held
        own_ref[t : t + 1, :] = owner.astype(F32).astype(BF16)
        hots.append((jnp.broadcast_to(owner, (peers, length)) == peer_id).astype(F32))
    stack = jnp.concatenate(hots, 0).astype(BF16)
    within = jnp.dot(stack, upper, preferred_element_type=F32)
    totals = jnp.dot(stack, every, preferred_element_type=F32)
    offset = jnp.zeros((peers, length), F32)
    found = jnp.zeros((2 * peers, cap), F32)
    for t in range(tiles):
        own_rows = slice(t * peers, (t + 1) * peers)
        rank = jnp.sum(hots[t] * (within[own_rows] + offset), axis=0, keepdims=True).astype(I32)
        offset = offset + totals[own_rows]
        rank_ref[t : t + 1, :] = rank.astype(F32).astype(BF16)
        ids = ids_ref[t : t + 1, :]
        row = ids - (ids // rows_held) * rows_held + 1
        high = (row >> 6).astype(F32)
        low = (row & 63).astype(F32)
        digits = jnp.concatenate([hots[t] * high, hots[t] * low], 0).astype(BF16)
        slots = (jnp.broadcast_to(rank, (cap, length)) == slot_id).astype(F32).astype(BF16)
        found = found + lax.dot_general(digits, slots, LANES, preferred_element_type=F32)
    req_ref[...] = (found[:peers] * 64.0 + found[peers:]).astype(I32) - 1


def index(ids, peers, cap, rows_held):
    like = jax.ShapeDtypeStruct(ids.shape, BF16)
    return pl.pallas_call(
        functools.partial(index_kernel, peers, cap, rows_held),
        out_shape=(jax.ShapeDtypeStruct((peers, cap), I32), like, like),
        compiler_params=params(),
        cost_estimate=pl.CostEstimate(flops=10**9, bytes_accessed=10**7, transcendentals=0),
        name="index",
    )(ids)


def weights_kernel(alpha_ref, out_ref):
    alpha = alpha_ref[...]
    length = alpha.shape[1]
    logs = jnp.log1p(-alpha)
    earlier = lax.broadcasted_iota(I32, (length, length), 0)
    later = lax.broadcasted_iota(I32, (length, length), 1)
    upper = (earlier < later).astype(F32)
    before = jnp.dot(logs, upper, preferred_element_type=F32, precision=lax.Precision.HIGHEST)
    out_ref[...] = (alpha * jnp.exp(before)).astype(BF16)


def weights(alphas):
    return pl.pallas_call(
        weights_kernel,
        out_shape=jax.ShapeDtypeStruct(alphas.shape, BF16),
        compiler_params=params(),
        cost_estimate=pl.CostEstimate(flops=10**9, bytes_accessed=10**7, transcendentals=0),
        name="weights",
    )(alphas)


def spread_kernel(near, cap, base_ref, own_ref, rank_ref, weight_ref, out_ref):
    tiles, length = own_ref.shape
    cells = weight_ref.shape[0] // tiles
    slot_id = lax.broadcasted_iota(I32, (cap, length), 0)
    for t in range(tiles):
        own = own_ref[t : t + 1, :].astype(I32)
        rank = rank_ref[t : t + 1, :].astype(I32)
        here = slice(t * cells, (t + 1) * cells)
        weight = weight_ref[here, :].astype(F32)
        by_owner = [jnp.where(own == base_ref[o], weight, 0.0) for o in range(near)]
        slots = (jnp.broadcast_to(rank, (cap, length)) == slot_id).astype(F32).astype(BF16)
        moved = lax.dot_general(
            jnp.concatenate(by_owner, 0).astype(BF16), slots, LANES, preferred_element_type=F32
        ).astype(BF16)
        if cap % 128 == 0:
            for o in range(near):
                out_ref[here, o * cap : (o + 1) * cap] = moved[o * cells : (o + 1) * cells]
        else:
            out_ref[here, :] = jnp.concatenate([moved[o * cells : (o + 1) * cells] for o in range(near)], 1)


def spread(owners, own, rank, weight, cap):
    tiles, length = own.shape
    cells = weight.shape[0] // tiles
    near = owners.shape[0]
    step = 16
    lists = pl.BlockSpec((step, length), lambda t: (t, 0))
    return pl.pallas_call(
        functools.partial(spread_kernel, near, cap),
        grid=(tiles // step,),
        in_specs=[pl.BlockSpec(memory_space=pltpu.SMEM), lists, lists, pl.BlockSpec((step * cells, length), lambda t: (t, 0))],
        out_specs=pl.BlockSpec((step * cells, near * cap), lambda t: (t, 0)),
        out_shape=jax.ShapeDtypeStruct((weight.shape[0], near * cap), BF16),
        compiler_params=params(),
        cost_estimate=pl.CostEstimate(flops=7 * 10**9, bytes_accessed=10**7, transcendentals=0),
        name="spread",
    )(owners, own, rank, weight)


def gather_kernel(group, cap, asked_ref, rows_ref, out_ref):
    first = pl.program_id(0) * group
    asked = asked_ref[...]
    peer = lax.broadcasted_iota(I32, asked.shape, 1)
    held = rows_ref.shape[0]
    row_id = lax.broadcasted_iota(I32, (cap, held), 1)
    picks = []
    for q in range(group):
        column = jnp.sum(jnp.where(peer == first + q, asked, 0), axis=1, keepdims=True)
        picks.append((jnp.broadcast_to(column, (cap, held)) == row_id).astype(F32).astype(BF16))
    pick = jnp.concatenate(picks, 0)
    out_ref[...] = jnp.dot(pick, rows_ref[...], preferred_element_type=F32).astype(BF16)


def gather(asked, rows):
    near, cap = asked.shape
    held, feat = rows.shape
    group = max(1, min(near, 1024 // cap))
    return pl.pallas_call(
        functools.partial(gather_kernel, group, cap),
        grid=(near // group,),
        in_specs=[pl.BlockSpec((cap, near), lambda i: (0, 0)), pl.BlockSpec((held, feat), lambda i: (0, 0))],
        out_specs=pl.BlockSpec((group * cap, feat), lambda i: (i, 0)),
        out_shape=jax.ShapeDtypeStruct((near * cap, feat), BF16),
        compiler_params=params(),
        cost_estimate=pl.CostEstimate(flops=10**10, bytes_accessed=10**7, transcendentals=0),
        name="gather",
    )(asked.T, rows)


def blend_kernel(n_parts, weight_ref, rows_ref, *rest):
    color = jnp.dot(weight_ref[...], rows_ref[...], preferred_element_type=F32)
    for part_ref in rest[:n_parts]:
        color = color + part_ref[...].astype(F32)
    if len(rest) == n_parts + 1:
        rest[n_parts][...] = color.astype(BF16)
    else:
        target_ref, color_ref, diff_ref = rest[n_parts:]
        color_ref[...] = color.astype(BF16)
        diff_ref[...] = (color - target_ref[...].astype(F32)).astype(BF16)


def blend(weight, rows, parts=(), target=None):
    cells, slots = weight.shape
    feat = rows.shape[1]
    block = min(cells, 256)
    cell_block = pl.BlockSpec((block, feat), lambda i: (i, 0))
    out = jax.ShapeDtypeStruct((cells, feat), BF16)
    more = tuple(parts) + (() if target is None else (target,))
    return pl.pallas_call(
        functools.partial(blend_kernel, len(parts)),
        grid=(cells // block,),
        in_specs=[pl.BlockSpec((block, slots), lambda i: (i, 0)), pl.BlockSpec((slots, feat), lambda i: (0, 0))]
        + [cell_block] * len(more),
        out_specs=cell_block if target is None else (cell_block, cell_block),
        out_shape=out if target is None else (out, out),
        compiler_params=params(),
        cost_estimate=pl.CostEstimate(flops=4 * 10**9, bytes_accessed=10**7, transcendentals=0),
        name="blend",
    )(weight, rows, *more)


def terms_kernel(weight_ref, *refs):
    diff = refs[0][...]
    for more_ref in refs[1:-1]:
        diff = diff + more_ref[...]
    refs[-1][...] = lax.dot_general(weight_ref[...], diff, ROWS, preferred_element_type=F32).astype(BF16)


def terms(weight, *diffs):
    cells, slots = weight.shape
    feat = diffs[0].shape[1]
    block = min(slots, 1024)
    return pl.pallas_call(
        terms_kernel,
        grid=(slots // block,),
        in_specs=[pl.BlockSpec((cells, block), lambda i: (0, i))]
        + [pl.BlockSpec((cells, feat), lambda i: (0, 0))] * len(diffs),
        out_specs=pl.BlockSpec((block, feat), lambda i: (i, 0)),
        out_shape=jax.ShapeDtypeStruct((slots, feat), BF16),
        compiler_params=params(),
        cost_estimate=pl.CostEstimate(flops=4 * 10**9, bytes_accessed=10**7, transcendentals=0),
        name="terms",
    )(weight, *diffs)


def add_rows_kernel(count, *refs):
    out_ref = refs[-1]
    block = out_ref.shape[0]
    total = None if len(refs) == 2 * count + 1 else refs[2 * count][...]
    for n in range(count):
        asked_ref, terms_ref = refs[n], refs[count + n]
        near, cap = asked_ref.shape
        row_id = lax.broadcasted_iota(I32, (block, cap), 0) + pl.program_id(0) * block
        picks = []
        for o in range(near):
            asked = jnp.broadcast_to(asked_ref[o : o + 1, :], (block, cap))
            picks.append((asked == row_id).astype(F32).astype(BF16))
        got = jnp.dot(jnp.concatenate(picks, 1), terms_ref[...], preferred_element_type=F32)
        total = got if total is None else total + got
    out_ref[...] = total


def add_rows(askeds, arrivals, held, before=None):
    near, cap = askeds[0].shape
    feat = arrivals[0].shape[1]
    count = len(askeds)
    block = min(held, 512)
    row_block = pl.BlockSpec((block, feat), lambda i: (i, 0))
    more = before is not None
    in_specs = [pl.BlockSpec((near, cap), lambda i: (0, 0))] * count
    in_specs += [pl.BlockSpec((near * cap, feat), lambda i: (0, 0))] * count
    return pl.pallas_call(
        functools.partial(add_rows_kernel, count),
        grid=(held // block,),
        in_specs=in_specs + [row_block] * more,
        out_specs=row_block,
        out_shape=jax.ShapeDtypeStruct((held, feat), F32),
        compiler_params=params(),
        cost_estimate=pl.CostEstimate(flops=5 * count * 10**9, bytes_accessed=10**7, transcendentals=0),
        name="add_rows",
    )(*askeds, *arrivals, *((before,) if more else ()))


def layer_norm(rows, gain, bias):
    mean = jnp.mean(rows, axis=-1, keepdims=True)
    centred = rows - mean
    var = jnp.mean(centred * centred, axis=-1, keepdims=True)
    return centred * lax.rsqrt(var + 1e-05) * gain + bias


def on_device(
    patches,
    norm_gain,
    norm_bias,
    up_weight,
    up_bias,
    down_weight,
    down_bias,
    final_gain,
    final_bias,
    head_weight,
    gauss_rows,
    tile_lists,
    alphas,
):
    view_count, tiles_view, cells, width = patches.shape
    feat = head_weight.shape[1]
    n_img = lax.axis_size("img")
    n_tile = lax.axis_size("tile")
    peers = n_img * n_tile
    both = ("img", "tile")
    held = gauss_rows.shape[0]
    group_views, strip_tiles, list_len = tile_lists.shape
    tiles = group_views * strip_tiles
    cap = 2 * tiles * list_len // peers

    wide_layer = n_tile // 4
    near = n_img * wide_layer
    tile = lax.axis_index("tile")
    layer = tile // wide_layer
    low = layer < 2
    outer = (layer == 0) | (layer == 3)
    groups = [[i * n_tile + z * wide_layer + k for i in range(n_img) for k in range(wide_layer)] for z in range(4)]

    def moves(*pairs):
        return [(a * wide_layer + k, b * wide_layer + k) for a, b in pairs for k in range(wide_layer)]

    beside = moves((0, 1), (1, 0), (2, 3), (3, 2))
    middle = moves((1, 2), (2, 1))
    inwards = moves((0, 1), (3, 2))
    outwards = moves((1, 0), (2, 3))

    def move(x, pairs):
        return lax.ppermute(x, "tile", pairs)

    def exchange(x):
        return lax.all_to_all(x, both, split_axis=0, concat_axis=0, axis_index_groups=groups, tiled=True)

    request, own, rank = index(tile_lists.reshape(tiles, list_len), peers, cap, held)
    weight = weights(alphas.reshape(tiles * cells, list_len))
    packed = jnp.concatenate([weight, own, rank], 0)
    request, packed = lax.optimization_barrier((request, packed))
    from_beside = move(packed, beside)
    from_two = move(packed, moves((0, 2), (2, 0), (1, 3), (3, 1)))
    from_three = move(packed, moves((0, 3), (3, 0), (1, 2), (2, 1)))
    asked = lax.all_to_all(request, both, split_axis=0, concat_axis=0, tiled=True)
    asked = asked.reshape(n_img, 4, wide_layer, cap)
    sets = (jnp.where(low, 3, 0), jnp.where(low, 2, 1), layer ^ 1, layer)
    lists = [lax.dynamic_index_in_dim(asked, s, 1, keepdims=False).reshape(near, cap) for s in sets]
    packs = (
        jnp.where(outer, from_three, from_two),
        jnp.where(outer, from_two, from_three),
        from_beside,
        packed,
    )
    owners = (
        jnp.arange(n_img, dtype=I32)[:, None] * n_tile
        + layer * wide_layer
        + jnp.arange(wide_layer, dtype=I32)[None, :]
    ).reshape(near)

    def spread_of(pack):
        n_cells = tiles * cells
        return spread(owners, pack[n_cells : n_cells + tiles], pack[n_cells + tiles :], pack[:n_cells], cap)

    rows = []
    for n in range(4):
        looked = gather(lists[n], gauss_rows)
        if n:
            looked, rows[-1] = lax.optimization_barrier((looked, rows[-1]))
        rows.append(exchange(looked))

    wide = patches.reshape(-1, width).astype(F32)
    normed = layer_norm(wide, norm_gain, norm_bias).astype(BF16)
    inner = jnp.dot(normed, up_weight, preferred_element_type=F32) + up_bias
    act = (inner * jax.nn.sigmoid(1.702 * inner)).astype(BF16)
    block_out = wide + jnp.dot(act, down_weight, preferred_element_type=F32) + down_bias
    final = layer_norm(block_out, final_gain, final_bias).astype(BF16)
    embed = jnp.dot(final, head_weight, preferred_element_type=F32)
    scale = lax.rsqrt(jnp.mean(embed * embed, axis=-1, keepdims=True) + 1e-06)
    strips = (embed * scale).astype(BF16).reshape(n_tile, -1, feat)
    arrived = []
    for n in reversed(range(n_tile)):
        strip = lax.dynamic_index_in_dim(strips, lax.rem(tile + n, n_tile), 0, keepdims=True)
        arrived.append(lax.ppermute(strip, "tile", [(a, (a + n) % n_tile) for a in range(n_tile)]) if n else strip)
    first = lax.rem(2 * n_tile - 1 - tile, n_tile)
    target = lax.dynamic_slice_in_dim(jnp.concatenate(arrived + arrived, 0), first, n_tile, 0)
    target = target.reshape(tiles * cells, feat)

    spreads = [spread_of(pack) for pack in packs]
    part = blend(spreads[0], rows[0])
    far = move(part + move(part, inwards), middle)
    part = blend(spreads[1], rows[1])
    middle_part = move(part + move(part, inwards), middle)
    beside_part = move(blend(spreads[2], rows[2], (far,)), beside)
    color, diff = blend(spreads[3], rows[3], (beside_part, middle_part), target)

    diff_beside = move(diff, beside)
    diff_middle = move(diff, middle)
    far_middle = move(diff_beside, middle)
    diff_out = move(diff_middle, outwards)
    far_out = move(far_middle, outwards)
    back = []
    for n, diffs in ((3, (diff,)), (2, (diff_beside,)), (1, (diff_middle, diff_out)), (0, (far_middle, far_out))):
        term = terms(spreads[n], *diffs)
        if back:
            term, back[-1] = lax.optimization_barrier((term, back[-1]))
        back.append(exchange(term))
    grad = add_rows([lists[3], lists[2], lists[1]], back[:3], held)
    grad = add_rows([lists[0]], back[3:], held, grad)
    return (color.reshape(group_views, strip_tiles, cells, feat), grad)


def solution(mesh):
    placed = (
        P(("img", "tile"), None, None, None),
        P(),
        P(),
        P(),
        P(),
        P(),
        P(),
        P(),
        P(),
        P(),
        P(("img", "tile"), None),
        P("img", "tile", None),
        P("img", "tile", None, None),
    )
    return jax.shard_map(
        on_device,
        mesh=mesh,
        in_specs=placed,
        out_specs=(P("img", "tile", None, None), P(("img", "tile"), None)),
        check_vma=False,
    )
```

```python
import functools

import jax
import jax.numpy as jnp
from jax import lax
from jax.experimental import pallas as pl
from jax.experimental.pallas import tpu as pltpu
from jax.sharding import PartitionSpec as P

F32 = jnp.float32
BF16 = jnp.bfloat16
I32 = jnp.int32
VMEM_BYTES = 50 * 1024 * 1024
LANES = (((1,), (1,)), ((), ()))
ROWS = (((0,), (0,)), ((), ()))


def params():
    return pltpu.CompilerParams(vmem_limit_bytes=VMEM_BYTES)


def index_kernel(peers, cap, rows_held, ids_ref, req_ref, own_ref, rank_ref):
    tiles, length = ids_ref.shape
    earlier = lax.broadcasted_iota(I32, (length, length), 0)
    later = lax.broadcasted_iota(I32, (length, length), 1)
    upper = (earlier < later).astype(BF16)
    every = jnp.ones((length, length), BF16)
    peer_id = lax.broadcasted_iota(I32, (peers, length), 0)
    slot_id = lax.broadcasted_iota(I32, (cap, length), 0)
    hots = []
    for t in range(tiles):
        owner = ids_ref[t : t + 1, :] // rows_held
        own_ref[t : t + 1, :] = owner.astype(F32).astype(BF16)
        hots.append((jnp.broadcast_to(owner, (peers, length)) == peer_id).astype(F32))
    stack = jnp.concatenate(hots, 0).astype(BF16)
    within = jnp.dot(stack, upper, preferred_element_type=F32)
    totals = jnp.dot(stack, every, preferred_element_type=F32)
    offset = jnp.zeros((peers, length), F32)
    found = jnp.zeros((2 * peers, cap), F32)
    for t in range(tiles):
        own_rows = slice(t * peers, (t + 1) * peers)
        rank = jnp.sum(hots[t] * (within[own_rows] + offset), axis=0, keepdims=True).astype(I32)
        offset = offset + totals[own_rows]
        rank_ref[t : t + 1, :] = rank.astype(F32).astype(BF16)
        ids = ids_ref[t : t + 1, :]
        row = ids - (ids // rows_held) * rows_held + 1
        high = (row >> 6).astype(F32)
        low = (row & 63).astype(F32)
        digits = jnp.concatenate([hots[t] * high, hots[t] * low], 0).astype(BF16)
        slots = (jnp.broadcast_to(rank, (cap, length)) == slot_id).astype(F32).astype(BF16)
        found = found + lax.dot_general(digits, slots, LANES, preferred_element_type=F32)
    req_ref[...] = (found[:peers] * 64.0 + found[peers:]).astype(I32) - 1


def index(ids, peers, cap, rows_held):
    like = jax.ShapeDtypeStruct(ids.shape, BF16)
    return pl.pallas_call(
        functools.partial(index_kernel, peers, cap, rows_held),
        out_shape=(jax.ShapeDtypeStruct((peers, cap), I32), like, like),
        compiler_params=params(),
        cost_estimate=pl.CostEstimate(flops=10**9, bytes_accessed=10**7, transcendentals=0),
        name="index",
    )(ids)


def weights_kernel(alpha_ref, out_ref):
    alpha = alpha_ref[...]
    length = alpha.shape[1]
    logs = jnp.log1p(-alpha)
    earlier = lax.broadcasted_iota(I32, (length, length), 0)
    later = lax.broadcasted_iota(I32, (length, length), 1)
    upper = (earlier < later).astype(F32)
    before = jnp.dot(logs, upper, preferred_element_type=F32, precision=lax.Precision.HIGHEST)
    out_ref[...] = (alpha * jnp.exp(before)).astype(BF16)


def weights(alphas):
    return pl.pallas_call(
        weights_kernel,
        out_shape=jax.ShapeDtypeStruct(alphas.shape, BF16),
        compiler_params=params(),
        cost_estimate=pl.CostEstimate(flops=10**9, bytes_accessed=10**7, transcendentals=0),
        name="weights",
    )(alphas)


def spread_kernel(near, cap, base_ref, own_ref, rank_ref, weight_ref, out_ref):
    tiles, length = own_ref.shape
    cells = weight_ref.shape[0] // tiles
    slot_id = lax.broadcasted_iota(I32, (cap, length), 0)
    for t in range(tiles):
        own = own_ref[t : t + 1, :].astype(I32)
        rank = rank_ref[t : t + 1, :].astype(I32)
        here = slice(t * cells, (t + 1) * cells)
        weight = weight_ref[here, :].astype(F32)
        by_owner = [jnp.where(own == base_ref[o], weight, 0.0) for o in range(near)]
        slots = (jnp.broadcast_to(rank, (cap, length)) == slot_id).astype(F32).astype(BF16)
        moved = lax.dot_general(
            jnp.concatenate(by_owner, 0).astype(BF16), slots, LANES, preferred_element_type=F32
        ).astype(BF16)
        if cap % 128 == 0:
            for o in range(near):
                out_ref[here, o * cap : (o + 1) * cap] = moved[o * cells : (o + 1) * cells]
        else:
            out_ref[here, :] = jnp.concatenate([moved[o * cells : (o + 1) * cells] for o in range(near)], 1)


def spread(owners, own, rank, weight, cap):
    tiles, length = own.shape
    cells = weight.shape[0] // tiles
    near = owners.shape[0]
    step = 16
    lists = pl.BlockSpec((step, length), lambda t: (t, 0))
    return pl.pallas_call(
        functools.partial(spread_kernel, near, cap),
        grid=(tiles // step,),
        in_specs=[pl.BlockSpec(memory_space=pltpu.SMEM), lists, lists, pl.BlockSpec((step * cells, length), lambda t: (t, 0))],
        out_specs=pl.BlockSpec((step * cells, near * cap), lambda t: (t, 0)),
        out_shape=jax.ShapeDtypeStruct((weight.shape[0], near * cap), BF16),
        compiler_params=params(),
        cost_estimate=pl.CostEstimate(flops=7 * 10**9, bytes_accessed=10**7, transcendentals=0),
        name="spread",
    )(owners, own, rank, weight)


def gather_kernel(group, cap, asked_ref, rows_ref, out_ref):
    first = pl.program_id(0) * group
    asked = asked_ref[...]
    peer = lax.broadcasted_iota(I32, asked.shape, 1)
    held = rows_ref.shape[0]
    row_id = lax.broadcasted_iota(I32, (cap, held), 1)
    picks = []
    for q in range(group):
        column = jnp.sum(jnp.where(peer == first + q, asked, 0), axis=1, keepdims=True)
        picks.append((jnp.broadcast_to(column, (cap, held)) == row_id).astype(F32).astype(BF16))
    pick = jnp.concatenate(picks, 0)
    out_ref[...] = jnp.dot(pick, rows_ref[...], preferred_element_type=F32).astype(BF16)


def gather(asked, rows):
    near, cap = asked.shape
    held, feat = rows.shape
    group = max(1, min(near, 1024 // cap))
    return pl.pallas_call(
        functools.partial(gather_kernel, group, cap),
        grid=(near // group,),
        in_specs=[pl.BlockSpec((cap, near), lambda i: (0, 0)), pl.BlockSpec((held, feat), lambda i: (0, 0))],
        out_specs=pl.BlockSpec((group * cap, feat), lambda i: (i, 0)),
        out_shape=jax.ShapeDtypeStruct((near * cap, feat), BF16),
        compiler_params=params(),
        cost_estimate=pl.CostEstimate(flops=10**10, bytes_accessed=10**7, transcendentals=0),
        name="gather",
    )(asked.T, rows)


def blend_kernel(n_parts, weight_ref, rows_ref, *rest):
    color = jnp.dot(weight_ref[...], rows_ref[...], preferred_element_type=F32)
    for part_ref in rest[:n_parts]:
        color = color + part_ref[...].astype(F32)
    rest[n_parts][...] = color.astype(BF16)


def last_blend_kernel(n_parts, first_ref, weight_ref, rows_ref, *rest):
    parts, strips = rest[:n_parts], rest[n_parts:-2]
    color_ref, diff_ref = rest[-2:]
    color = jnp.dot(weight_ref[...], rows_ref[...], preferred_element_type=F32)
    for part_ref in parts:
        color = color + part_ref[...].astype(F32)
    color_ref[...] = color.astype(BF16)
    cells = strips[0].shape[0]
    per_step = color.shape[0] // cells
    for k in range(per_step):
        at = lax.rem(first_ref[0] + pl.program_id(0) * per_step + k, len(strips))
        here = slice(k * cells, (k + 1) * cells)
        for n in range(len(strips)):

            @pl.when(at == n)
            def _(n=n):
                diff_ref[here, :] = (color[here] - strips[n][...].astype(F32)).astype(BF16)


def blend(weight, rows, parts=(), first=None, strips=()):
    cells, slots = weight.shape
    feat = rows.shape[1]
    block = min(cells, 256)
    cell_block = pl.BlockSpec((block, feat), lambda i: (i, 0))
    out = jax.ShapeDtypeStruct((cells, feat), BF16)
    last = first is not None
    in_specs = [pl.BlockSpec((block, slots), lambda i: (i, 0)), pl.BlockSpec((slots, feat), lambda i: (0, 0))]
    in_specs += [cell_block] * len(parts)
    args = [weight, rows, *parts]
    if last:
        in_specs = [pl.BlockSpec(memory_space=pltpu.SMEM)] + in_specs
        in_specs += [pl.BlockSpec(strip.shape, lambda i: (0, 0)) for strip in strips]
        args = [first, *args, *strips]
    return pl.pallas_call(
        functools.partial(last_blend_kernel if last else blend_kernel, len(parts)),
        grid=(cells // block,),
        in_specs=in_specs,
        out_specs=(cell_block, cell_block) if last else cell_block,
        out_shape=(out, out) if last else out,
        compiler_params=params(),
        cost_estimate=pl.CostEstimate(flops=4 * 10**9, bytes_accessed=10**7, transcendentals=0),
        name="blend",
    )(*args)


def terms_kernel(weight_ref, *refs):
    diff = refs[0][...]
    for more_ref in refs[1:-1]:
        diff = diff + more_ref[...]
    refs[-1][...] = lax.dot_general(weight_ref[...], diff, ROWS, preferred_element_type=F32).astype(BF16)


def terms(weight, *diffs):
    cells, slots = weight.shape
    feat = diffs[0].shape[1]
    block = min(slots, 1024)
    return pl.pallas_call(
        terms_kernel,
        grid=(slots // block,),
        in_specs=[pl.BlockSpec((cells, block), lambda i: (0, i))]
        + [pl.BlockSpec((cells, feat), lambda i: (0, 0))] * len(diffs),
        out_specs=pl.BlockSpec((block, feat), lambda i: (i, 0)),
        out_shape=jax.ShapeDtypeStruct((slots, feat), BF16),
        compiler_params=params(),
        cost_estimate=pl.CostEstimate(flops=4 * 10**9, bytes_accessed=10**7, transcendentals=0),
        name="terms",
    )(weight, *diffs)


def add_rows_kernel(count, *refs):
    out_ref = refs[-1]
    block = out_ref.shape[0]
    total = None if len(refs) == 2 * count + 1 else refs[2 * count][...]
    for n in range(count):
        asked_ref, terms_ref = refs[n], refs[count + n]
        near, cap = asked_ref.shape
        row_id = lax.broadcasted_iota(I32, (block, cap), 0) + pl.program_id(0) * block
        picks = []
        for o in range(near):
            asked = jnp.broadcast_to(asked_ref[o : o + 1, :], (block, cap))
            picks.append((asked == row_id).astype(F32).astype(BF16))
        got = jnp.dot(jnp.concatenate(picks, 1), terms_ref[...], preferred_element_type=F32)
        total = got if total is None else total + got
    out_ref[...] = total


def add_rows(askeds, arrivals, held, before=None):
    near, cap = askeds[0].shape
    feat = arrivals[0].shape[1]
    count = len(askeds)
    block = min(held, 512)
    row_block = pl.BlockSpec((block, feat), lambda i: (i, 0))
    more = before is not None
    in_specs = [pl.BlockSpec((near, cap), lambda i: (0, 0))] * count
    in_specs += [pl.BlockSpec((near * cap, feat), lambda i: (0, 0))] * count
    return pl.pallas_call(
        functools.partial(add_rows_kernel, count),
        grid=(held // block,),
        in_specs=in_specs + [row_block] * more,
        out_specs=row_block,
        out_shape=jax.ShapeDtypeStruct((held, feat), F32),
        compiler_params=params(),
        cost_estimate=pl.CostEstimate(flops=5 * count * 10**9, bytes_accessed=10**7, transcendentals=0),
        name="add_rows",
    )(*askeds, *arrivals, *((before,) if more else ()))


def layer_norm(rows, gain, bias):
    mean = jnp.mean(rows, axis=-1, keepdims=True)
    centred = rows - mean
    var = jnp.mean(centred * centred, axis=-1, keepdims=True)
    return centred * lax.rsqrt(var + 1e-05) * gain + bias


def on_device(
    patches,
    norm_gain,
    norm_bias,
    up_weight,
    up_bias,
    down_weight,
    down_bias,
    final_gain,
    final_bias,
    head_weight,
    gauss_rows,
    tile_lists,
    alphas,
):
    view_count, tiles_view, cells, width = patches.shape
    feat = head_weight.shape[1]
    n_img = lax.axis_size("img")
    n_tile = lax.axis_size("tile")
    peers = n_img * n_tile
    both = ("img", "tile")
    held = gauss_rows.shape[0]
    group_views, strip_tiles, list_len = tile_lists.shape
    tiles = group_views * strip_tiles
    cap = 2 * tiles * list_len // peers

    wide_layer = n_tile // 4
    near = n_img * wide_layer
    tile = lax.axis_index("tile")
    layer = tile // wide_layer
    low = layer < 2
    outer = (layer == 0) | (layer == 3)
    groups = [[i * n_tile + z * wide_layer + k for i in range(n_img) for k in range(wide_layer)] for z in range(4)]

    def moves(*pairs):
        return [(a * wide_layer + k, b * wide_layer + k) for a, b in pairs for k in range(wide_layer)]

    beside = moves((0, 1), (1, 0), (2, 3), (3, 2))
    middle = moves((1, 2), (2, 1))
    inwards = moves((0, 1), (3, 2))
    outwards = moves((1, 0), (2, 3))

    def move(x, pairs):
        return lax.ppermute(x, "tile", pairs)

    def exchange(x):
        return lax.all_to_all(x, both, split_axis=0, concat_axis=0, axis_index_groups=groups, tiled=True)

    request, own, rank = index(tile_lists.reshape(tiles, list_len), peers, cap, held)
    asked = lax.all_to_all(request, both, split_axis=0, concat_axis=0, tiled=True)
    asked = asked.reshape(n_img, 4, wide_layer, cap)
    sets = (jnp.where(low, 3, 0), jnp.where(low, 2, 1), layer ^ 1, layer)
    lists = [lax.dynamic_index_in_dim(asked, s, 1, keepdims=False).reshape(near, cap) for s in sets]
    owners = (
        jnp.arange(n_img, dtype=I32)[:, None] * n_tile
        + layer * wide_layer
        + jnp.arange(wide_layer, dtype=I32)[None, :]
    ).reshape(near)

    def spread_of(pack):
        n_cells = tiles * cells
        return spread(owners, pack[n_cells : n_cells + tiles], pack[n_cells + tiles :], pack[:n_cells], cap)

    looked = gather(lists[0], gauss_rows)
    looked, patches, alphas = lax.optimization_barrier((looked, patches, alphas))
    rows = [exchange(looked)]
    weight = weights(alphas.reshape(tiles * cells, list_len))
    packed = jnp.concatenate([weight, own, rank], 0)
    from_beside = move(packed, beside)
    from_two = move(packed, moves((0, 2), (2, 0), (1, 3), (3, 1)))
    from_three = move(packed, moves((0, 3), (3, 0), (1, 2), (2, 1)))
    packs = (
        jnp.where(outer, from_three, from_two),
        jnp.where(outer, from_two, from_three),
        from_beside,
        packed,
    )
    spreads = [spread_of(pack) for pack in packs]

    wide = patches.reshape(-1, width).astype(F32)
    normed = layer_norm(wide, norm_gain, norm_bias).astype(BF16)
    inner = jnp.dot(normed, up_weight, preferred_element_type=F32) + up_bias
    act = (inner * jax.nn.sigmoid(1.702 * inner)).astype(BF16)
    block_out = wide + jnp.dot(act, down_weight, preferred_element_type=F32) + down_bias
    final = layer_norm(block_out, final_gain, final_bias).astype(BF16)
    embed = jnp.dot(final, head_weight, preferred_element_type=F32)
    scale = lax.rsqrt(jnp.mean(embed * embed, axis=-1, keepdims=True) + 1e-06)
    target = (embed * scale).astype(BF16).reshape(n_tile, -1, feat)

    looked, rows[0] = lax.optimization_barrier((gather(lists[1], gauss_rows), rows[0]))
    rows.append(exchange(looked))
    part = blend(spreads[0], rows[0])
    moved = move(part, inwards)
    looked, rows[1], part, moved = lax.optimization_barrier((gather(lists[2], gauss_rows), rows[1], part, moved))
    rows.append(exchange(looked))
    far = move(part + moved, middle)
    part = blend(spreads[1], rows[1])
    moved = move(part, inwards)
    looked, rows[2], far = lax.optimization_barrier((gather(lists[3], gauss_rows), rows[2], far))
    rows.append(exchange(looked))
    middle_part = move(part + moved, middle)
    beside_part = move(blend(spreads[2], rows[2], (far,)), beside)

    strips = []
    for n in reversed(range(n_tile)):
        strip = lax.dynamic_index_in_dim(target, lax.rem(tile + n, n_tile), 0, keepdims=False)
        strips.append(lax.ppermute(strip, "tile", [(a, (a + n) % n_tile) for a in range(n_tile)]) if n else strip)
    first = lax.rem(2 * n_tile - 1 - tile, n_tile).astype(I32).reshape(1)
    color, diff = blend(spreads[3], rows[3], (beside_part, middle_part), first, strips)

    diff_beside = move(diff, beside)
    diff_middle = move(diff, middle)
    far_middle = move(diff_beside, middle)
    diff_out = move(diff_middle, outwards)
    far_out = move(far_middle, outwards)
    back = []
    for n, diffs in ((3, (diff,)), (2, (diff_beside,)), (1, (diff_middle, diff_out)), (0, (far_middle, far_out))):
        term = terms(spreads[n], *diffs)
        if back:
            term, back[-1] = lax.optimization_barrier((term, back[-1]))
        back.append(exchange(term))
    grad = add_rows([lists[3], lists[2], lists[1]], back[:3], held)
    grad = add_rows([lists[0]], back[3:], held, grad)
    return (color.reshape(group_views, strip_tiles, cells, feat), grad)


def solution(mesh):
    placed = (
        P(("img", "tile"), None, None, None),
        P(),
        P(),
        P(),
        P(),
        P(),
        P(),
        P(),
        P(),
        P(),
        P(("img", "tile"), None),
        P("img", "tile", None),
        P("img", "tile", None, None),
    )
    return jax.shard_map(
        on_device,
        mesh=mesh,
        in_specs=placed,
        out_specs=(P("img", "tile", None, None), P(("img", "tile"), None)),
        check_vma=False,
    )
```

```python
import functools

import jax
import jax.numpy as jnp
from jax import lax
from jax.experimental import pallas as pl
from jax.experimental.pallas import tpu as pltpu
from jax.sharding import PartitionSpec as P

F32 = jnp.float32
BF16 = jnp.bfloat16
I32 = jnp.int32
VMEM_BYTES = 50 * 1024 * 1024
LANES = (((1,), (1,)), ((), ()))
ROWS = (((0,), (0,)), ((), ()))


def params():
    return pltpu.CompilerParams(vmem_limit_bytes=VMEM_BYTES)


def index_kernel(peers, cap, rows_held, ids_ref, req_ref, own_ref, rank_ref):
    tiles, length = ids_ref.shape
    earlier = lax.broadcasted_iota(I32, (length, length), 0)
    later = lax.broadcasted_iota(I32, (length, length), 1)
    upper = (earlier < later).astype(BF16)
    every = jnp.ones((length, length), BF16)
    peer_id = lax.broadcasted_iota(I32, (peers, length), 0)
    slot_id = lax.broadcasted_iota(I32, (cap, length), 0)
    hots = []
    for t in range(tiles):
        owner = ids_ref[t : t + 1, :] // rows_held
        own_ref[t : t + 1, :] = owner.astype(F32).astype(BF16)
        hots.append((jnp.broadcast_to(owner, (peers, length)) == peer_id).astype(F32))
    stack = jnp.concatenate(hots, 0).astype(BF16)
    within = jnp.dot(stack, upper, preferred_element_type=F32)
    totals = jnp.dot(stack, every, preferred_element_type=F32)
    offset = jnp.zeros((peers, length), F32)
    found = jnp.zeros((2 * peers, cap), F32)
    for t in range(tiles):
        own_rows = slice(t * peers, (t + 1) * peers)
        rank = jnp.sum(hots[t] * (within[own_rows] + offset), axis=0, keepdims=True).astype(I32)
        offset = offset + totals[own_rows]
        rank_ref[t : t + 1, :] = rank.astype(F32).astype(BF16)
        ids = ids_ref[t : t + 1, :]
        row = ids - (ids // rows_held) * rows_held + 1
        high = (row >> 6).astype(F32)
        low = (row & 63).astype(F32)
        digits = jnp.concatenate([hots[t] * high, hots[t] * low], 0).astype(BF16)
        slots = (jnp.broadcast_to(rank, (cap, length)) == slot_id).astype(F32).astype(BF16)
        found = found + lax.dot_general(digits, slots, LANES, preferred_element_type=F32)
    req_ref[...] = (found[:peers] * 64.0 + found[peers:]).astype(I32) - 1


def index(ids, peers, cap, rows_held):
    like = jax.ShapeDtypeStruct(ids.shape, BF16)
    return pl.pallas_call(
        functools.partial(index_kernel, peers, cap, rows_held),
        out_shape=(jax.ShapeDtypeStruct((peers, cap), I32), like, like),
        compiler_params=params(),
        cost_estimate=pl.CostEstimate(flops=10**9, bytes_accessed=10**7, transcendentals=0),
        name="index",
    )(ids)


def weights_kernel(alpha_ref, out_ref):
    alpha = alpha_ref[...]
    length = alpha.shape[1]
    logs = jnp.log1p(-alpha)
    earlier = lax.broadcasted_iota(I32, (length, length), 0)
    later = lax.broadcasted_iota(I32, (length, length), 1)
    upper = (earlier < later).astype(F32)
    before = jnp.dot(logs, upper, preferred_element_type=F32, precision=lax.Precision.HIGHEST)
    out_ref[...] = (alpha * jnp.exp(before)).astype(BF16)


def weights(alphas):
    return pl.pallas_call(
        weights_kernel,
        out_shape=jax.ShapeDtypeStruct(alphas.shape, BF16),
        compiler_params=params(),
        cost_estimate=pl.CostEstimate(flops=10**9, bytes_accessed=10**7, transcendentals=0),
        name="weights",
    )(alphas)


def spread_kernel(near, cap, base_ref, own_ref, rank_ref, weight_ref, out_ref):
    tiles, length = own_ref.shape
    cells = weight_ref.shape[0] // tiles
    slot_id = lax.broadcasted_iota(I32, (cap, length), 0)
    for t in range(tiles):
        own = own_ref[t : t + 1, :].astype(I32)
        rank = rank_ref[t : t + 1, :].astype(I32)
        here = slice(t * cells, (t + 1) * cells)
        weight = weight_ref[here, :].astype(F32)
        by_owner = [jnp.where(own == base_ref[o], weight, 0.0) for o in range(near)]
        slots = (jnp.broadcast_to(rank, (cap, length)) == slot_id).astype(F32).astype(BF16)
        moved = lax.dot_general(
            jnp.concatenate(by_owner, 0).astype(BF16), slots, LANES, preferred_element_type=F32
        ).astype(BF16)
        if cap % 128 == 0:
            for o in range(near):
                out_ref[here, o * cap : (o + 1) * cap] = moved[o * cells : (o + 1) * cells]
        else:
            out_ref[here, :] = jnp.concatenate([moved[o * cells : (o + 1) * cells] for o in range(near)], 1)


def spread(owners, own, rank, weight, cap):
    tiles, length = own.shape
    cells = weight.shape[0] // tiles
    near = owners.shape[0]
    step = 16
    lists = pl.BlockSpec((step, length), lambda t: (t, 0))
    return pl.pallas_call(
        functools.partial(spread_kernel, near, cap),
        grid=(tiles // step,),
        in_specs=[pl.BlockSpec(memory_space=pltpu.SMEM), lists, lists, pl.BlockSpec((step * cells, length), lambda t: (t, 0))],
        out_specs=pl.BlockSpec((step * cells, near * cap), lambda t: (t, 0)),
        out_shape=jax.ShapeDtypeStruct((weight.shape[0], near * cap), BF16),
        compiler_params=params(),
        cost_estimate=pl.CostEstimate(flops=7 * 10**9, bytes_accessed=10**7, transcendentals=0),
        name="spread",
    )(owners, own, rank, weight)


def gather_kernel(group, cap, asked_ref, rows_ref, out_ref):
    first = pl.program_id(0) * group
    asked = asked_ref[...]
    peer = lax.broadcasted_iota(I32, asked.shape, 1)
    held = rows_ref.shape[0]
    row_id = lax.broadcasted_iota(I32, (cap, held), 1)
    picks = []
    for q in range(group):
        column = jnp.sum(jnp.where(peer == first + q, asked, 0), axis=1, keepdims=True)
        picks.append((jnp.broadcast_to(column, (cap, held)) == row_id).astype(F32).astype(BF16))
    pick = jnp.concatenate(picks, 0)
    out_ref[...] = jnp.dot(pick, rows_ref[...], preferred_element_type=F32).astype(BF16)


def gather(asked, rows):
    near, cap = asked.shape
    held, feat = rows.shape
    group = max(1, min(near, 1024 // cap))
    return pl.pallas_call(
        functools.partial(gather_kernel, group, cap),
        grid=(near // group,),
        in_specs=[pl.BlockSpec((cap, near), lambda i: (0, 0)), pl.BlockSpec((held, feat), lambda i: (0, 0))],
        out_specs=pl.BlockSpec((group * cap, feat), lambda i: (i, 0)),
        out_shape=jax.ShapeDtypeStruct((near * cap, feat), BF16),
        compiler_params=params(),
        cost_estimate=pl.CostEstimate(flops=10**10, bytes_accessed=10**7, transcendentals=0),
        name="gather",
    )(asked.T, rows)


def blend_kernel(n_parts, weight_ref, rows_ref, *rest):
    color = jnp.dot(weight_ref[...], rows_ref[...], preferred_element_type=F32)
    for part_ref in rest[:n_parts]:
        color = color + part_ref[...].astype(F32)
    rest[n_parts][...] = color.astype(BF16)


def last_blend_kernel(n_parts, first_ref, weight_ref, rows_ref, *rest):
    parts, strips = rest[:n_parts], rest[n_parts:-2]
    color_ref, diff_ref = rest[-2:]
    color = jnp.dot(weight_ref[...], rows_ref[...], preferred_element_type=F32)
    for part_ref in parts:
        color = color + part_ref[...].astype(F32)
    color_ref[...] = color.astype(BF16)
    cells = strips[0].shape[0]
    per_step = color.shape[0] // cells
    for k in range(per_step):
        at = lax.rem(first_ref[0] + pl.program_id(0) * per_step + k, len(strips))
        here = slice(k * cells, (k + 1) * cells)
        for n in range(len(strips)):

            @pl.when(at == n)
            def _(n=n):
                diff_ref[here, :] = (color[here] - strips[n][...].astype(F32)).astype(BF16)


def blend(weight, rows, parts=(), first=None, strips=()):
    cells, slots = weight.shape
    feat = rows.shape[1]
    block = min(cells, 256)
    cell_block = pl.BlockSpec((block, feat), lambda i: (i, 0))
    out = jax.ShapeDtypeStruct((cells, feat), BF16)
    last = first is not None
    in_specs = [pl.BlockSpec((block, slots), lambda i: (i, 0)), pl.BlockSpec((slots, feat), lambda i: (0, 0))]
    in_specs += [cell_block] * len(parts)
    args = [weight, rows, *parts]
    if last:
        in_specs = [pl.BlockSpec(memory_space=pltpu.SMEM)] + in_specs
        in_specs += [pl.BlockSpec(strip.shape, lambda i: (0, 0)) for strip in strips]
        args = [first, *args, *strips]
    return pl.pallas_call(
        functools.partial(last_blend_kernel if last else blend_kernel, len(parts)),
        grid=(cells // block,),
        in_specs=in_specs,
        out_specs=(cell_block, cell_block) if last else cell_block,
        out_shape=(out, out) if last else out,
        compiler_params=params(),
        cost_estimate=pl.CostEstimate(flops=4 * 10**9, bytes_accessed=10**7, transcendentals=0),
        name="blend",
    )(*args)


def terms_kernel(weight_ref, *refs):
    diff = refs[0][...]
    for more_ref in refs[1:-1]:
        diff = diff + more_ref[...]
    refs[-1][...] = lax.dot_general(weight_ref[...], diff, ROWS, preferred_element_type=F32).astype(BF16)


def terms(weight, *diffs):
    cells, slots = weight.shape
    feat = diffs[0].shape[1]
    block = min(slots, 1024)
    return pl.pallas_call(
        terms_kernel,
        grid=(slots // block,),
        in_specs=[pl.BlockSpec((cells, block), lambda i: (0, i))]
        + [pl.BlockSpec((cells, feat), lambda i: (0, 0))] * len(diffs),
        out_specs=pl.BlockSpec((block, feat), lambda i: (i, 0)),
        out_shape=jax.ShapeDtypeStruct((slots, feat), BF16),
        compiler_params=params(),
        cost_estimate=pl.CostEstimate(flops=4 * 10**9, bytes_accessed=10**7, transcendentals=0),
        name="terms",
    )(weight, *diffs)


def add_rows_kernel(count, *refs):
    out_ref = refs[-1]
    block = out_ref.shape[0]
    total = None if len(refs) == 2 * count + 1 else refs[2 * count][...]
    for n in range(count):
        asked_ref, terms_ref = refs[n], refs[count + n]
        near, cap = asked_ref.shape
        row_id = lax.broadcasted_iota(I32, (block, cap), 0) + pl.program_id(0) * block
        picks = []
        for o in range(near):
            asked = jnp.broadcast_to(asked_ref[o : o + 1, :], (block, cap))
            picks.append((asked == row_id).astype(F32).astype(BF16))
        got = jnp.dot(jnp.concatenate(picks, 1), terms_ref[...], preferred_element_type=F32)
        total = got if total is None else total + got
    out_ref[...] = total


def add_rows(askeds, arrivals, held, before=None):
    near, cap = askeds[0].shape
    feat = arrivals[0].shape[1]
    count = len(askeds)
    block = min(held, 512)
    row_block = pl.BlockSpec((block, feat), lambda i: (i, 0))
    more = before is not None
    in_specs = [pl.BlockSpec((near, cap), lambda i: (0, 0))] * count
    in_specs += [pl.BlockSpec((near * cap, feat), lambda i: (0, 0))] * count
    return pl.pallas_call(
        functools.partial(add_rows_kernel, count),
        grid=(held // block,),
        in_specs=in_specs + [row_block] * more,
        out_specs=row_block,
        out_shape=jax.ShapeDtypeStruct((held, feat), F32),
        compiler_params=params(),
        cost_estimate=pl.CostEstimate(flops=5 * count * 10**9, bytes_accessed=10**7, transcendentals=0),
        name="add_rows",
    )(*askeds, *arrivals, *((before,) if more else ()))


def layer_norm(rows, gain, bias):
    mean = jnp.mean(rows, axis=-1, keepdims=True)
    centred = rows - mean
    var = jnp.mean(centred * centred, axis=-1, keepdims=True)
    return centred * lax.rsqrt(var + 1e-05) * gain + bias


def on_device(
    patches,
    norm_gain,
    norm_bias,
    up_weight,
    up_bias,
    down_weight,
    down_bias,
    final_gain,
    final_bias,
    head_weight,
    gauss_rows,
    tile_lists,
    alphas,
):
    view_count, tiles_view, cells, width = patches.shape
    feat = head_weight.shape[1]
    n_img = lax.axis_size("img")
    n_tile = lax.axis_size("tile")
    peers = n_img * n_tile
    both = ("img", "tile")
    held = gauss_rows.shape[0]
    group_views, strip_tiles, list_len = tile_lists.shape
    tiles = group_views * strip_tiles
    cap = 2 * tiles * list_len // peers

    wide_layer = n_tile // 4
    near = n_img * wide_layer
    tile = lax.axis_index("tile")
    layer = tile // wide_layer
    low = layer < 2
    outer = (layer == 0) | (layer == 3)
    groups = [[i * n_tile + z * wide_layer + k for i in range(n_img) for k in range(wide_layer)] for z in range(4)]

    def moves(*pairs):
        return [(a * wide_layer + k, b * wide_layer + k) for a, b in pairs for k in range(wide_layer)]

    beside = moves((0, 1), (1, 0), (2, 3), (3, 2))
    middle = moves((1, 2), (2, 1))
    inwards = moves((0, 1), (3, 2))
    outwards = moves((1, 0), (2, 3))

    def move(x, pairs):
        return lax.ppermute(x, "tile", pairs)

    def exchange(x):
        return lax.all_to_all(x, both, split_axis=0, concat_axis=0, axis_index_groups=groups, tiled=True)

    request, own, rank = index(tile_lists.reshape(tiles, list_len), peers, cap, held)
    asked = lax.all_to_all(request, both, split_axis=0, concat_axis=0, tiled=True)
    asked = asked.reshape(n_img, 4, wide_layer, cap)
    sets = (jnp.where(low, 3, 0), jnp.where(low, 2, 1), layer ^ 1, layer)
    lists = [lax.dynamic_index_in_dim(asked, s, 1, keepdims=False).reshape(near, cap) for s in sets]
    owners = (
        jnp.arange(n_img, dtype=I32)[:, None] * n_tile
        + layer * wide_layer
        + jnp.arange(wide_layer, dtype=I32)[None, :]
    ).reshape(near)

    def spread_of(pack):
        n_cells = tiles * cells
        return spread(owners, pack[n_cells : n_cells + tiles], pack[n_cells + tiles :], pack[:n_cells], cap)

    def tie(*values):
        return lax.optimization_barrier(values)

    looked, alphas, lists[1] = tie(gather(lists[0], gauss_rows), alphas, lists[1])
    rows_1 = exchange(looked)
    weight = weights(alphas.reshape(tiles * cells, list_len))
    packed = jnp.concatenate([weight, own, rank], 0)
    from_beside = move(packed, beside)
    from_two = move(packed, moves((0, 2), (2, 0), (1, 3), (3, 1)))
    from_three = move(packed, moves((0, 3), (3, 0), (1, 2), (2, 1)))
    spread_1 = spread_of(jnp.where(outer, from_three, from_two))
    looked_2 = gather(lists[1], gauss_rows)
    looked_2, lists[2] = tie(looked_2, lists[2])
    looked_3 = gather(lists[2], gauss_rows)
    looked_2, looked_3, spread_1, rows_1, from_two, from_three, patches = tie(
        looked_2, looked_3, spread_1, rows_1, from_two, from_three, patches
    )

    rows_2 = exchange(looked_2)
    part_1 = blend(spread_1, rows_1)
    moved_1 = move(part_1, inwards)
    spread_2 = spread_of(jnp.where(outer, from_two, from_three))
    wide = patches.reshape(-1, width).astype(F32)
    normed = layer_norm(wide, norm_gain, norm_bias).astype(BF16)
    inner = jnp.dot(normed, up_weight, preferred_element_type=F32) + up_bias
    act = (inner * jax.nn.sigmoid(1.702 * inner)).astype(BF16)
    block_out = wide + jnp.dot(act, down_weight, preferred_element_type=F32) + down_bias
    final = layer_norm(block_out, final_gain, final_bias).astype(BF16)
    embed = jnp.dot(final, head_weight, preferred_element_type=F32)
    scale = lax.rsqrt(jnp.mean(embed * embed, axis=-1, keepdims=True) + 1e-06)
    target = (embed * scale).astype(BF16).reshape(n_tile, -1, feat)
    looked_3, rows_2, part_1, moved_1, target, spread_2, lists[3], from_beside = tie(
        looked_3, rows_2, part_1, moved_1, target, spread_2, lists[3], from_beside
    )

    rows_3 = exchange(looked_3)
    far = move(part_1 + moved_1, middle)
    part_2 = blend(spread_2, rows_2)
    moved_2 = move(part_2, inwards)
    strips = []
    for n in reversed(range(n_tile)):
        strip = lax.dynamic_index_in_dim(target, lax.rem(tile + n, n_tile), 0, keepdims=False)
        strips.append(lax.ppermute(strip, "tile", [(a, (a + n) % n_tile) for a in range(n_tile)]) if n else strip)
    spread_3 = spread_of(from_beside)
    looked_4 = gather(lists[3], gauss_rows)
    looked_4, rows_3, far, spread_3, packed, *strips = tie(looked_4, rows_3, far, spread_3, packed, *strips)

    rows_4 = exchange(looked_4)
    part_3 = blend(spread_3, rows_3, (far,))
    beside_part = move(part_3, beside)
    part_2, moved_2, part_3, packed = tie(part_2, moved_2, part_3, packed)
    middle_part = move(part_2 + moved_2, middle)
    spread_4 = spread_of(packed)
    first = lax.rem(2 * n_tile - 1 - tile, n_tile).astype(I32).reshape(1)
    color, diff = blend(spread_4, rows_4, (beside_part, middle_part), first, strips)
    spreads = (spread_1, spread_2, spread_3, spread_4)

    diff_beside = move(diff, beside)
    diff_middle = move(diff, middle)
    far_middle = move(diff_beside, middle)
    diff_out = move(diff_middle, outwards)
    far_out = move(far_middle, outwards)
    back = []
    for n, diffs in ((3, (diff,)), (2, (diff_beside,)), (1, (diff_middle, diff_out)), (0, (far_middle, far_out))):
        term = terms(spreads[n], *diffs)
        if back:
            term, back[-1] = lax.optimization_barrier((term, back[-1]))
        back.append(exchange(term))
    grad = add_rows([lists[3], lists[2], lists[1]], back[:3], held)
    grad = add_rows([lists[0]], back[3:], held, grad)
    return (color.reshape(group_views, strip_tiles, cells, feat), grad)


def solution(mesh):
    placed = (
        P(("img", "tile"), None, None, None),
        P(),
        P(),
        P(),
        P(),
        P(),
        P(),
        P(),
        P(),
        P(),
        P(("img", "tile"), None),
        P("img", "tile", None),
        P("img", "tile", None, None),
    )
    return jax.shard_map(
        on_device,
        mesh=mesh,
        in_specs=placed,
        out_specs=(P("img", "tile", None, None), P(("img", "tile"), None)),
        check_vma=False,
    )
```

```python
import functools

import jax
import jax.numpy as jnp
from jax import lax
from jax.experimental import pallas as pl
from jax.experimental.pallas import tpu as pltpu
from jax.sharding import PartitionSpec as P

F32 = jnp.float32
BF16 = jnp.bfloat16
I32 = jnp.int32
VMEM_BYTES = 50 * 1024 * 1024
LANES = (((1,), (1,)), ((), ()))
ROWS = (((0,), (0,)), ((), ()))


def params():
    return pltpu.CompilerParams(vmem_limit_bytes=VMEM_BYTES)


def index_kernel(peers, cap, rows_held, ids_ref, req_ref, own_ref, rank_ref):
    tiles, length = ids_ref.shape
    earlier = lax.broadcasted_iota(I32, (length, length), 0)
    later = lax.broadcasted_iota(I32, (length, length), 1)
    upper = (earlier < later).astype(BF16)
    every = jnp.ones((length, length), BF16)
    peer_id = lax.broadcasted_iota(I32, (peers, length), 0)
    slot_id = lax.broadcasted_iota(I32, (cap, length), 0)
    hots = []
    for t in range(tiles):
        owner = ids_ref[t : t + 1, :] // rows_held
        own_ref[t : t + 1, :] = owner.astype(F32).astype(BF16)
        hots.append((jnp.broadcast_to(owner, (peers, length)) == peer_id).astype(F32))
    stack = jnp.concatenate(hots, 0).astype(BF16)
    within = jnp.dot(stack, upper, preferred_element_type=F32)
    totals = jnp.dot(stack, every, preferred_element_type=F32)
    offset = jnp.zeros((peers, length), F32)
    found = jnp.zeros((2 * peers, cap), F32)
    for t in range(tiles):
        own_rows = slice(t * peers, (t + 1) * peers)
        rank = jnp.sum(hots[t] * (within[own_rows] + offset), axis=0, keepdims=True).astype(I32)
        offset = offset + totals[own_rows]
        rank_ref[t : t + 1, :] = rank.astype(F32).astype(BF16)
        ids = ids_ref[t : t + 1, :]
        row = ids - (ids // rows_held) * rows_held + 1
        high = (row >> 6).astype(F32)
        low = (row & 63).astype(F32)
        digits = jnp.concatenate([hots[t] * high, hots[t] * low], 0).astype(BF16)
        slots = (jnp.broadcast_to(rank, (cap, length)) == slot_id).astype(F32).astype(BF16)
        found = found + lax.dot_general(digits, slots, LANES, preferred_element_type=F32)
    req_ref[...] = (found[:peers] * 64.0 + found[peers:]).astype(I32) - 1


def index(ids, peers, cap, rows_held):
    like = jax.ShapeDtypeStruct(ids.shape, BF16)
    return pl.pallas_call(
        functools.partial(index_kernel, peers, cap, rows_held),
        out_shape=(jax.ShapeDtypeStruct((peers, cap), I32), like, like),
        compiler_params=params(),
        cost_estimate=pl.CostEstimate(flops=10**9, bytes_accessed=10**7, transcendentals=0),
        name="index",
    )(ids)


def weights_kernel(alpha_ref, out_ref):
    alpha = alpha_ref[...]
    length = alpha.shape[1]
    logs = jnp.log1p(-alpha)
    earlier = lax.broadcasted_iota(I32, (length, length), 0)
    later = lax.broadcasted_iota(I32, (length, length), 1)
    upper = (earlier < later).astype(F32)
    before = jnp.dot(logs, upper, preferred_element_type=F32, precision=lax.Precision.HIGHEST)
    out_ref[...] = (alpha * jnp.exp(before)).astype(BF16)


def weights(alphas):
    return pl.pallas_call(
        weights_kernel,
        out_shape=jax.ShapeDtypeStruct(alphas.shape, BF16),
        compiler_params=params(),
        cost_estimate=pl.CostEstimate(flops=10**9, bytes_accessed=10**7, transcendentals=0),
        name="weights",
    )(alphas)


def spread_kernel(near, cap, base_ref, own_ref, rank_ref, weight_ref, out_ref):
    tiles, length = own_ref.shape
    cells = weight_ref.shape[0] // tiles
    slot_id = lax.broadcasted_iota(I32, (cap, length), 0)
    for t in range(tiles):
        own = own_ref[t : t + 1, :].astype(I32)
        rank = rank_ref[t : t + 1, :].astype(I32)
        here = slice(t * cells, (t + 1) * cells)
        weight = weight_ref[here, :].astype(F32)
        by_owner = [jnp.where(own == base_ref[o], weight, 0.0) for o in range(near)]
        slots = (jnp.broadcast_to(rank, (cap, length)) == slot_id).astype(F32).astype(BF16)
        moved = lax.dot_general(
            jnp.concatenate(by_owner, 0).astype(BF16), slots, LANES, preferred_element_type=F32
        ).astype(BF16)
        if cap % 128 == 0:
            for o in range(near):
                out_ref[here, o * cap : (o + 1) * cap] = moved[o * cells : (o + 1) * cells]
        else:
            out_ref[here, :] = jnp.concatenate([moved[o * cells : (o + 1) * cells] for o in range(near)], 1)


def spread(owners, own, rank, weight, cap):
    tiles, length = own.shape
    cells = weight.shape[0] // tiles
    near = owners.shape[0]
    step = 16
    lists = pl.BlockSpec((step, length), lambda t: (t, 0))
    return pl.pallas_call(
        functools.partial(spread_kernel, near, cap),
        grid=(tiles // step,),
        in_specs=[pl.BlockSpec(memory_space=pltpu.SMEM), lists, lists, pl.BlockSpec((step * cells, length), lambda t: (t, 0))],
        out_specs=pl.BlockSpec((step * cells, near * cap), lambda t: (t, 0)),
        out_shape=jax.ShapeDtypeStruct((weight.shape[0], near * cap), BF16),
        compiler_params=params(),
        cost_estimate=pl.CostEstimate(flops=7 * 10**9, bytes_accessed=10**7, transcendentals=0),
        name="spread",
    )(owners, own, rank, weight)


def gather_kernel(group, cap, asked_ref, rows_ref, out_ref):
    first = pl.program_id(0) * group
    asked = asked_ref[...]
    peer = lax.broadcasted_iota(I32, asked.shape, 1)
    held = rows_ref.shape[0]
    row_id = lax.broadcasted_iota(I32, (cap, held), 1)
    picks = []
    for q in range(group):
        column = jnp.sum(jnp.where(peer == first + q, asked, 0), axis=1, keepdims=True)
        picks.append((jnp.broadcast_to(column, (cap, held)) == row_id).astype(F32).astype(BF16))
    pick = jnp.concatenate(picks, 0)
    out_ref[...] = jnp.dot(pick, rows_ref[...], preferred_element_type=F32).astype(BF16)


def gather(asked, rows):
    near, cap = asked.shape
    held, feat = rows.shape
    group = max(1, min(near, 1024 // cap))
    return pl.pallas_call(
        functools.partial(gather_kernel, group, cap),
        grid=(near // group,),
        in_specs=[pl.BlockSpec((cap, near), lambda i: (0, 0)), pl.BlockSpec((held, feat), lambda i: (0, 0))],
        out_specs=pl.BlockSpec((group * cap, feat), lambda i: (i, 0)),
        out_shape=jax.ShapeDtypeStruct((near * cap, feat), BF16),
        compiler_params=params(),
        cost_estimate=pl.CostEstimate(flops=10**10, bytes_accessed=10**7, transcendentals=0),
        name="gather",
    )(asked.T, rows)


def blend_kernel(n_parts, weight_ref, rows_ref, *rest):
    color = jnp.dot(weight_ref[...], rows_ref[...], preferred_element_type=F32)
    for part_ref in rest[:n_parts]:
        color = color + part_ref[...].astype(F32)
    rest[n_parts][...] = color.astype(BF16)


def last_blend_kernel(n_parts, first_ref, weight_ref, rows_ref, *rest):
    parts, target_ref = rest[:n_parts], rest[n_parts]
    color_ref, diff_ref = rest[-2:]
    color = jnp.dot(weight_ref[...], rows_ref[...], preferred_element_type=F32)
    for part_ref in parts:
        color = color + part_ref[...].astype(F32)
    color_ref[...] = color.astype(BF16)
    strips, cells = target_ref.shape[:2]
    per_step = color.shape[0] // cells
    for k in range(per_step):
        at = lax.rem(first_ref[0] + pl.program_id(0) * per_step + k, strips)
        here = slice(k * cells, (k + 1) * cells)
        diff_ref[here, :] = (color[here] - target_ref[at].astype(F32)).astype(BF16)


def blend(weight, rows, parts=(), first=None, target=None):
    cells, slots = weight.shape
    feat = rows.shape[1]
    block = min(cells, 256)
    cell_block = pl.BlockSpec((block, feat), lambda i: (i, 0))
    out = jax.ShapeDtypeStruct((cells, feat), BF16)
    last = first is not None
    in_specs = [pl.BlockSpec((block, slots), lambda i: (i, 0)), pl.BlockSpec((slots, feat), lambda i: (0, 0))]
    in_specs += [cell_block] * len(parts)
    args = [weight, rows, *parts]
    if last:
        in_specs = [pl.BlockSpec(memory_space=pltpu.SMEM)] + in_specs + [pl.BlockSpec(target.shape, lambda i: (0, 0, 0))]
        args = [first, *args, target]
    return pl.pallas_call(
        functools.partial(last_blend_kernel if last else blend_kernel, len(parts)),
        grid=(cells // block,),
        in_specs=in_specs,
        out_specs=(cell_block, cell_block) if last else cell_block,
        out_shape=(out, out) if last else out,
        compiler_params=params(),
        cost_estimate=pl.CostEstimate(flops=4 * 10**9, bytes_accessed=10**7, transcendentals=0),
        name="blend",
    )(*args)


def terms_kernel(weight_ref, *refs):
    diff = refs[0][...]
    for more_ref in refs[1:-1]:
        diff = diff + more_ref[...]
    refs[-1][...] = lax.dot_general(weight_ref[...], diff, ROWS, preferred_element_type=F32).astype(BF16)


def terms(weight, *diffs):
    cells, slots = weight.shape
    feat = diffs[0].shape[1]
    block = min(slots, 1024)
    return pl.pallas_call(
        terms_kernel,
        grid=(slots // block,),
        in_specs=[pl.BlockSpec((cells, block), lambda i: (0, i))]
        + [pl.BlockSpec((cells, feat), lambda i: (0, 0))] * len(diffs),
        out_specs=pl.BlockSpec((block, feat), lambda i: (i, 0)),
        out_shape=jax.ShapeDtypeStruct((slots, feat), BF16),
        compiler_params=params(),
        cost_estimate=pl.CostEstimate(flops=4 * 10**9, bytes_accessed=10**7, transcendentals=0),
        name="terms",
    )(weight, *diffs)


def add_rows_kernel(count, *refs):
    out_ref = refs[-1]
    block = out_ref.shape[0]
    total = None if len(refs) == 2 * count + 1 else refs[2 * count][...]
    for n in range(count):
        asked_ref, terms_ref = refs[n], refs[count + n]
        near, cap = asked_ref.shape
        row_id = lax.broadcasted_iota(I32, (block, cap), 0) + pl.program_id(0) * block
        picks = []
        for o in range(near):
            asked = jnp.broadcast_to(asked_ref[o : o + 1, :], (block, cap))
            picks.append((asked == row_id).astype(F32).astype(BF16))
        got = jnp.dot(jnp.concatenate(picks, 1), terms_ref[...], preferred_element_type=F32)
        total = got if total is None else total + got
    out_ref[...] = total


def add_rows(askeds, arrivals, held, before=None):
    near, cap = askeds[0].shape
    feat = arrivals[0].shape[1]
    count = len(askeds)
    block = min(held, 512)
    row_block = pl.BlockSpec((block, feat), lambda i: (i, 0))
    more = before is not None
    in_specs = [pl.BlockSpec((near, cap), lambda i: (0, 0))] * count
    in_specs += [pl.BlockSpec((near * cap, feat), lambda i: (0, 0))] * count
    return pl.pallas_call(
        functools.partial(add_rows_kernel, count),
        grid=(held // block,),
        in_specs=in_specs + [row_block] * more,
        out_specs=row_block,
        out_shape=jax.ShapeDtypeStruct((held, feat), F32),
        compiler_params=params(),
        cost_estimate=pl.CostEstimate(flops=5 * count * 10**9, bytes_accessed=10**7, transcendentals=0),
        name="add_rows",
    )(*askeds, *arrivals, *((before,) if more else ()))


def layer_norm(rows, gain, bias):
    mean = jnp.mean(rows, axis=-1, keepdims=True)
    centred = rows - mean
    var = jnp.mean(centred * centred, axis=-1, keepdims=True)
    return centred * lax.rsqrt(var + 1e-05) * gain + bias


def encode_kernel(strips, *refs):
    gain, bias, up, up_bias, down, down_bias, last_gain, last_bias, head = refs[strips:-1]
    out_ref = refs[-1]
    hidden = up.shape[1]
    step = 768 if hidden % 768 == 0 else hidden
    group = max(1, strips // 2)
    for first in range(0, strips, group):
        wide = jnp.concatenate([ref[...] for ref in refs[first : first + group]], 0).astype(F32)
        normed = layer_norm(wide, gain[...], bias[...]).astype(BF16)
        block_out = wide + down_bias[...]
        for k in range(0, hidden, step):
            inner = jnp.dot(normed, up[:, k : k + step], preferred_element_type=F32) + up_bias[:, k : k + step]
            act = (inner * jax.nn.sigmoid(1.702 * inner)).astype(BF16)
            block_out = block_out + jnp.dot(act, down[k : k + step, :], preferred_element_type=F32)
        final = layer_norm(block_out, last_gain[...], last_bias[...]).astype(BF16)
        embed = jnp.dot(final, head[...], preferred_element_type=F32)
        scale = lax.rsqrt(jnp.mean(embed * embed, axis=-1, keepdims=True) + 1e-06)
        target = (embed * scale).astype(BF16)
        cells = target.shape[0] // group
        for n in range(group):
            out_ref[first + n] = target[n * cells : (n + 1) * cells]


def encode(strips, *weights_and_biases):
    args = [w.reshape(1, -1) if w.ndim == 1 else w for w in weights_and_biases]
    cells = strips[0].shape[0]
    return pl.pallas_call(
        functools.partial(encode_kernel, len(strips)),
        out_shape=jax.ShapeDtypeStruct((len(strips), cells, args[-1].shape[1]), BF16),
        compiler_params=params(),
        cost_estimate=pl.CostEstimate(flops=2 * 10**10, bytes_accessed=10**7, transcendentals=0),
        name="encode",
    )(*strips, *args)


def on_device(
    patches,
    norm_gain,
    norm_bias,
    up_weight,
    up_bias,
    down_weight,
    down_bias,
    final_gain,
    final_bias,
    head_weight,
    gauss_rows,
    tile_lists,
    alphas,
):
    view_count, tiles_view, cells, width = patches.shape
    feat = head_weight.shape[1]
    n_img = lax.axis_size("img")
    n_tile = lax.axis_size("tile")
    peers = n_img * n_tile
    both = ("img", "tile")
    held = gauss_rows.shape[0]
    group_views, strip_tiles, list_len = tile_lists.shape
    tiles = group_views * strip_tiles
    cap = 2 * tiles * list_len // peers

    wide_layer = n_tile // 4
    near = n_img * wide_layer
    tile = lax.axis_index("tile")
    layer = tile // wide_layer
    low = layer < 2
    outer = (layer == 0) | (layer == 3)
    groups = [[i * n_tile + z * wide_layer + k for i in range(n_img) for k in range(wide_layer)] for z in range(4)]

    def moves(*pairs):
        return [(a * wide_layer + k, b * wide_layer + k) for a, b in pairs for k in range(wide_layer)]

    beside = moves((0, 1), (1, 0), (2, 3), (3, 2))
    middle = moves((1, 2), (2, 1))
    inwards = moves((0, 1), (3, 2))
    outwards = moves((1, 0), (2, 3))

    def move(x, pairs):
        return lax.ppermute(x, "tile", pairs)

    def exchange(x):
        return lax.all_to_all(x, both, split_axis=0, concat_axis=0, axis_index_groups=groups, tiled=True)

    def tie(*values):
        return lax.optimization_barrier(values)

    request, own, rank = index(tile_lists.reshape(tiles, list_len), peers, cap, held)
    asked = lax.all_to_all(request, both, split_axis=0, concat_axis=0, tiled=True)
    patches = patches.reshape(n_tile, -1, width)
    strips = []
    for n in reversed(range(n_tile)):
        strip = lax.dynamic_index_in_dim(patches, lax.rem(tile + n, n_tile), 0, keepdims=False)
        strips.append(move(strip, [(a, (a + n) % n_tile) for a in range(n_tile)]) if n else strip)
    first = lax.rem(2 * n_tile - 1 - tile, n_tile).astype(I32).reshape(1)
    asked = asked.reshape(n_img, 4, wide_layer, cap)
    sets = (jnp.where(low, 3, 0), jnp.where(low, 2, 1), layer ^ 1, layer)
    lists = [lax.dynamic_index_in_dim(asked, s, 1, keepdims=False).reshape(near, cap) for s in sets]
    owners = (
        jnp.arange(n_img, dtype=I32)[:, None] * n_tile
        + layer * wide_layer
        + jnp.arange(wide_layer, dtype=I32)[None, :]
    ).reshape(near)

    def spread_of(pack):
        n_cells = tiles * cells
        return spread(owners, pack[n_cells : n_cells + tiles], pack[n_cells + tiles :], pack[:n_cells], cap)

    looked, alphas, lists[1] = tie(gather(lists[0], gauss_rows), alphas, lists[1])
    rows_1 = exchange(looked)
    weight = weights(alphas.reshape(tiles * cells, list_len))
    packed = jnp.concatenate([weight, own, rank], 0)
    from_beside = move(packed, beside)
    from_two = move(packed, moves((0, 2), (2, 0), (1, 3), (3, 1)))
    from_three = move(packed, moves((0, 3), (3, 0), (1, 2), (2, 1)))
    spread_1 = spread_of(jnp.where(outer, from_three, from_two))
    looked_2 = gather(lists[1], gauss_rows)
    looked_2, lists[2] = tie(looked_2, lists[2])
    looked_3 = gather(lists[2], gauss_rows)
    looked_2, looked_3, spread_1, rows_1, from_two, from_three, *strips = tie(
        looked_2, looked_3, spread_1, rows_1, from_two, from_three, *strips
    )

    rows_2 = exchange(looked_2)
    part_1 = blend(spread_1, rows_1)
    moved_1 = move(part_1, inwards)
    part_1, *strips = tie(part_1, *strips)
    target = encode(
        strips, norm_gain, norm_bias, up_weight, up_bias, down_weight, down_bias, final_gain, final_bias, head_weight
    )
    looked_3, rows_2, part_1, moved_1, target, lists[3], from_beside, from_two = tie(
        looked_3, rows_2, part_1, moved_1, target, lists[3], from_beside, from_two
    )

    rows_3 = exchange(looked_3)
    far = move(part_1 + moved_1, middle)
    spread_2 = spread_of(jnp.where(outer, from_two, from_three))
    part_2 = blend(spread_2, rows_2)
    moved_2 = move(part_2, inwards)
    part_2, lists[3], from_beside = tie(part_2, lists[3], from_beside)
    looked_4 = gather(lists[3], gauss_rows)
    spread_3 = spread_of(from_beside)
    looked_4, rows_3, far, spread_3, packed = tie(looked_4, rows_3, far, spread_3, packed)

    rows_4 = exchange(looked_4)
    part_3 = blend(spread_3, rows_3, (far,))
    beside_part = move(part_3, beside)
    part_2, moved_2, part_3, packed = tie(part_2, moved_2, part_3, packed)
    middle_part = move(part_2 + moved_2, middle)
    spread_4 = spread_of(packed)
    color, diff = blend(spread_4, rows_4, (beside_part, middle_part), first, target)
    spreads = (spread_1, spread_2, spread_3, spread_4)

    diff_beside = move(diff, beside)
    diff_middle = move(diff, middle)
    far_middle = move(diff_beside, middle)
    diff_out = move(diff_middle, outwards)
    far_out = move(far_middle, outwards)
    back = []
    for n, diffs in ((3, (diff,)), (2, (diff_beside,)), (1, (diff_middle, diff_out)), (0, (far_middle, far_out))):
        term = terms(spreads[n], *diffs)
        if back:
            term, back[-1] = lax.optimization_barrier((term, back[-1]))
        back.append(exchange(term))
    grad = add_rows([lists[3], lists[2], lists[1]], back[:3], held)
    grad = add_rows([lists[0]], back[3:], held, grad)
    return (color.reshape(group_views, strip_tiles, cells, feat), grad)


def solution(mesh):
    placed = (
        P(("img", "tile"), None, None, None),
        P(),
        P(),
        P(),
        P(),
        P(),
        P(),
        P(),
        P(),
        P(),
        P(("img", "tile"), None),
        P("img", "tile", None),
        P("img", "tile", None, None),
    )
    return jax.shard_map(
        on_device,
        mesh=mesh,
        in_specs=placed,
        out_specs=(P("img", "tile", None, None), P(("img", "tile"), None)),
        check_vma=False,
    )
```

```python
import functools

import jax
import jax.numpy as jnp
from jax import lax
from jax.experimental import pallas as pl
from jax.experimental.pallas import tpu as pltpu
from jax.sharding import PartitionSpec as P

F32 = jnp.float32
BF16 = jnp.bfloat16
I32 = jnp.int32
VMEM_BYTES = 50 * 1024 * 1024
LANES = (((1,), (1,)), ((), ()))
ROWS = (((0,), (0,)), ((), ()))


def params():
    return pltpu.CompilerParams(vmem_limit_bytes=VMEM_BYTES)


def index_kernel(peers, cap, rows_held, ids_ref, req_ref, own_ref, rank_ref):
    tiles, length = ids_ref.shape
    earlier = lax.broadcasted_iota(I32, (length, length), 0)
    later = lax.broadcasted_iota(I32, (length, length), 1)
    upper = (earlier < later).astype(BF16)
    every = jnp.ones((length, length), BF16)
    peer_id = lax.broadcasted_iota(I32, (peers, length), 0)
    slot_id = lax.broadcasted_iota(I32, (cap, length), 0)
    hots = []
    for t in range(tiles):
        owner = ids_ref[t : t + 1, :] // rows_held
        own_ref[t : t + 1, :] = owner.astype(F32).astype(BF16)
        hots.append((jnp.broadcast_to(owner, (peers, length)) == peer_id).astype(F32))
    stack = jnp.concatenate(hots, 0).astype(BF16)
    within = jnp.dot(stack, upper, preferred_element_type=F32)
    totals = jnp.dot(stack, every, preferred_element_type=F32)
    offset = jnp.zeros((peers, length), F32)
    found = jnp.zeros((2 * peers, cap), F32)
    for t in range(tiles):
        own_rows = slice(t * peers, (t + 1) * peers)
        rank = jnp.sum(hots[t] * (within[own_rows] + offset), axis=0, keepdims=True).astype(I32)
        offset = offset + totals[own_rows]
        rank_ref[t : t + 1, :] = rank.astype(F32).astype(BF16)
        ids = ids_ref[t : t + 1, :]
        row = ids - (ids // rows_held) * rows_held + 1
        high = (row >> 6).astype(F32)
        low = (row & 63).astype(F32)
        digits = jnp.concatenate([hots[t] * high, hots[t] * low], 0).astype(BF16)
        slots = (jnp.broadcast_to(rank, (cap, length)) == slot_id).astype(F32).astype(BF16)
        found = found + lax.dot_general(digits, slots, LANES, preferred_element_type=F32)
    req_ref[...] = (found[:peers] * 64.0 + found[peers:]).astype(I32) - 1


def index(ids, peers, cap, rows_held):
    like = jax.ShapeDtypeStruct(ids.shape, BF16)
    return pl.pallas_call(
        functools.partial(index_kernel, peers, cap, rows_held),
        out_shape=(jax.ShapeDtypeStruct((peers, cap), I32), like, like),
        compiler_params=params(),
        cost_estimate=pl.CostEstimate(flops=10**9, bytes_accessed=10**7, transcendentals=0),
        name="index",
    )(ids)


def weights_kernel(alpha_ref, out_ref):
    alpha = alpha_ref[...]
    length = alpha.shape[1]
    logs = jnp.log1p(-alpha)
    earlier = lax.broadcasted_iota(I32, (length, length), 0)
    later = lax.broadcasted_iota(I32, (length, length), 1)
    upper = (earlier < later).astype(F32)
    before = jnp.dot(logs, upper, preferred_element_type=F32, precision=lax.Precision.HIGHEST)
    out_ref[...] = (alpha * jnp.exp(before)).astype(BF16)


def weights(alphas):
    return pl.pallas_call(
        weights_kernel,
        out_shape=jax.ShapeDtypeStruct(alphas.shape, BF16),
        compiler_params=params(),
        cost_estimate=pl.CostEstimate(flops=10**9, bytes_accessed=10**7, transcendentals=0),
        name="weights",
    )(alphas)


def spread_kernel(near, cap, base_ref, own_ref, rank_ref, weight_ref, out_ref):
    tiles, length = own_ref.shape
    cells = weight_ref.shape[0] // tiles
    slot_id = lax.broadcasted_iota(I32, (cap, length), 0)
    for t in range(tiles):
        own = own_ref[t : t + 1, :].astype(I32)
        rank = rank_ref[t : t + 1, :].astype(I32)
        here = slice(t * cells, (t + 1) * cells)
        weight = weight_ref[here, :].astype(F32)
        by_owner = [jnp.where(own == base_ref[o], weight, 0.0) for o in range(near)]
        slots = (jnp.broadcast_to(rank, (cap, length)) == slot_id).astype(F32).astype(BF16)
        moved = lax.dot_general(
            jnp.concatenate(by_owner, 0).astype(BF16), slots, LANES, preferred_element_type=F32
        ).astype(BF16)
        if cap % 128 == 0:
            for o in range(near):
                out_ref[here, o * cap : (o + 1) * cap] = moved[o * cells : (o + 1) * cells]
        else:
            out_ref[here, :] = jnp.concatenate([moved[o * cells : (o + 1) * cells] for o in range(near)], 1)


def spread(owners, own, rank, weight, cap):
    tiles, length = own.shape
    cells = weight.shape[0] // tiles
    near = owners.shape[0]
    step = 16
    lists = pl.BlockSpec((step, length), lambda t: (t, 0))
    return pl.pallas_call(
        functools.partial(spread_kernel, near, cap),
        grid=(tiles // step,),
        in_specs=[pl.BlockSpec(memory_space=pltpu.SMEM), lists, lists, pl.BlockSpec((step * cells, length), lambda t: (t, 0))],
        out_specs=pl.BlockSpec((step * cells, near * cap), lambda t: (t, 0)),
        out_shape=jax.ShapeDtypeStruct((weight.shape[0], near * cap), BF16),
        compiler_params=params(),
        cost_estimate=pl.CostEstimate(flops=7 * 10**9, bytes_accessed=10**7, transcendentals=0),
        name="spread",
    )(owners, own, rank, weight)


def gather_kernel(group, cap, asked_ref, rows_ref, out_ref):
    first = pl.program_id(0) * group
    asked = asked_ref[...]
    peer = lax.broadcasted_iota(I32, asked.shape, 1)
    held = rows_ref.shape[0]
    row_id = lax.broadcasted_iota(I32, (cap, held), 1)
    picks = []
    for q in range(group):
        column = jnp.sum(jnp.where(peer == first + q, asked, 0), axis=1, keepdims=True)
        picks.append((jnp.broadcast_to(column, (cap, held)) == row_id).astype(F32).astype(BF16))
    pick = jnp.concatenate(picks, 0)
    out_ref[...] = jnp.dot(pick, rows_ref[...], preferred_element_type=F32).astype(BF16)


def gather(asked, rows):
    near, cap = asked.shape
    held, feat = rows.shape
    group = max(1, min(near, 1024 // cap))
    return pl.pallas_call(
        functools.partial(gather_kernel, group, cap),
        grid=(near // group,),
        in_specs=[pl.BlockSpec((cap, near), lambda i: (0, 0)), pl.BlockSpec((held, feat), lambda i: (0, 0))],
        out_specs=pl.BlockSpec((group * cap, feat), lambda i: (i, 0)),
        out_shape=jax.ShapeDtypeStruct((near * cap, feat), BF16),
        compiler_params=params(),
        cost_estimate=pl.CostEstimate(flops=10**10, bytes_accessed=10**7, transcendentals=0),
        name="gather",
    )(asked.T, rows)


def blend_kernel(n_parts, weight_ref, rows_ref, *rest):
    color = jnp.dot(weight_ref[...], rows_ref[...], preferred_element_type=F32)
    for part_ref in rest[:n_parts]:
        color = color + part_ref[...].astype(F32)
    rest[n_parts][...] = color.astype(BF16)


def last_blend_kernel(n_parts, first_ref, weight_ref, rows_ref, *rest):
    parts, target_ref = rest[:n_parts], rest[n_parts]
    color_ref, diff_ref = rest[-2:]
    color = jnp.dot(weight_ref[...], rows_ref[...], preferred_element_type=F32)
    for part_ref in parts:
        color = color + part_ref[...].astype(F32)
    color_ref[...] = color.astype(BF16)
    strips, cells = target_ref.shape[:2]
    per_step = color.shape[0] // cells
    for k in range(per_step):
        at = lax.rem(first_ref[0] + pl.program_id(0) * per_step + k, strips)
        here = slice(k * cells, (k + 1) * cells)
        diff_ref[here, :] = (color[here] - target_ref[at].astype(F32)).astype(BF16)


def blend(weight, rows, parts=(), first=None, target=None):
    cells, slots = weight.shape
    feat = rows.shape[1]
    block = min(cells, 256)
    cell_block = pl.BlockSpec((block, feat), lambda i: (i, 0))
    out = jax.ShapeDtypeStruct((cells, feat), BF16)
    last = first is not None
    in_specs = [pl.BlockSpec((block, slots), lambda i: (i, 0)), pl.BlockSpec((slots, feat), lambda i: (0, 0))]
    in_specs += [cell_block] * len(parts)
    args = [weight, rows, *parts]
    if last:
        in_specs = [pl.BlockSpec(memory_space=pltpu.SMEM)] + in_specs + [pl.BlockSpec(target.shape, lambda i: (0, 0, 0))]
        args = [first, *args, target]
    return pl.pallas_call(
        functools.partial(last_blend_kernel if last else blend_kernel, len(parts)),
        grid=(cells // block,),
        in_specs=in_specs,
        out_specs=(cell_block, cell_block) if last else cell_block,
        out_shape=(out, out) if last else out,
        compiler_params=params(),
        cost_estimate=pl.CostEstimate(flops=4 * 10**9, bytes_accessed=10**7, transcendentals=0),
        name="blend",
    )(*args)


def terms_kernel(weight_ref, *refs):
    diff = refs[0][...]
    for more_ref in refs[1:-1]:
        diff = diff + more_ref[...]
    refs[-1][...] = lax.dot_general(weight_ref[...], diff, ROWS, preferred_element_type=F32).astype(BF16)


def terms(weight, *diffs):
    cells, slots = weight.shape
    feat = diffs[0].shape[1]
    block = min(slots, 1024)
    return pl.pallas_call(
        terms_kernel,
        grid=(slots // block,),
        in_specs=[pl.BlockSpec((cells, block), lambda i: (0, i))]
        + [pl.BlockSpec((cells, feat), lambda i: (0, 0))] * len(diffs),
        out_specs=pl.BlockSpec((block, feat), lambda i: (i, 0)),
        out_shape=jax.ShapeDtypeStruct((slots, feat), BF16),
        compiler_params=params(),
        cost_estimate=pl.CostEstimate(flops=10**11, bytes_accessed=10**7, transcendentals=0),
        name="terms",
    )(weight, *diffs)


def add_rows_kernel(count, *refs):
    out_ref = refs[-1]
    block = out_ref.shape[0]
    total = None if len(refs) == 2 * count + 1 else refs[2 * count][...]
    for n in range(count):
        asked_ref, terms_ref = refs[n], refs[count + n]
        near, cap = asked_ref.shape
        row_id = lax.broadcasted_iota(I32, (block, cap), 0) + pl.program_id(0) * block
        picks = []
        for o in range(near):
            asked = jnp.broadcast_to(asked_ref[o : o + 1, :], (block, cap))
            picks.append((asked == row_id).astype(F32).astype(BF16))
        got = jnp.dot(jnp.concatenate(picks, 1), terms_ref[...], preferred_element_type=F32)
        total = got if total is None else total + got
    out_ref[...] = total


def add_rows(askeds, arrivals, held, before=None):
    near, cap = askeds[0].shape
    feat = arrivals[0].shape[1]
    count = len(askeds)
    block = min(held, 512)
    row_block = pl.BlockSpec((block, feat), lambda i: (i, 0))
    more = before is not None
    in_specs = [pl.BlockSpec((near, cap), lambda i: (0, 0))] * count
    in_specs += [pl.BlockSpec((near * cap, feat), lambda i: (0, 0))] * count
    return pl.pallas_call(
        functools.partial(add_rows_kernel, count),
        grid=(held // block,),
        in_specs=in_specs + [row_block] * more,
        out_specs=row_block,
        out_shape=jax.ShapeDtypeStruct((held, feat), F32),
        compiler_params=params(),
        cost_estimate=pl.CostEstimate(flops=5 * count * 10**9, bytes_accessed=10**7, transcendentals=0),
        name="add_rows",
    )(*askeds, *arrivals, *((before,) if more else ()))


def layer_norm(rows, gain, bias):
    mean = jnp.mean(rows, axis=-1, keepdims=True)
    centred = rows - mean
    var = jnp.mean(centred * centred, axis=-1, keepdims=True)
    return centred * lax.rsqrt(var + 1e-05) * gain + bias


def encode_kernel(strips, *refs):
    gain, bias, up, up_bias, down, down_bias, last_gain, last_bias, head = refs[strips:-1]
    out_ref = refs[-1]
    hidden = up.shape[1]
    step = 768 if hidden % 768 == 0 else hidden
    group = max(1, strips // 2)
    for first in range(0, strips, group):
        wide = jnp.concatenate([ref[...] for ref in refs[first : first + group]], 0).astype(F32)
        normed = layer_norm(wide, gain[...], bias[...]).astype(BF16)
        block_out = wide + down_bias[...]
        for k in range(0, hidden, step):
            inner = jnp.dot(normed, up[:, k : k + step], preferred_element_type=F32) + up_bias[:, k : k + step]
            act = (inner * jax.nn.sigmoid(1.702 * inner)).astype(BF16)
            block_out = block_out + jnp.dot(act, down[k : k + step, :], preferred_element_type=F32)
        final = layer_norm(block_out, last_gain[...], last_bias[...]).astype(BF16)
        embed = jnp.dot(final, head[...], preferred_element_type=F32)
        scale = lax.rsqrt(jnp.mean(embed * embed, axis=-1, keepdims=True) + 1e-06)
        target = (embed * scale).astype(BF16)
        cells = target.shape[0] // group
        for n in range(group):
            out_ref[first + n] = target[n * cells : (n + 1) * cells]


def encode(strips, *weights_and_biases):
    args = [w.reshape(1, -1) if w.ndim == 1 else w for w in weights_and_biases]
    cells = strips[0].shape[0]
    return pl.pallas_call(
        functools.partial(encode_kernel, len(strips)),
        out_shape=jax.ShapeDtypeStruct((len(strips), cells, args[-1].shape[1]), BF16),
        compiler_params=params(),
        cost_estimate=pl.CostEstimate(flops=2 * 10**10, bytes_accessed=10**7, transcendentals=0),
        name="encode",
    )(*strips, *args)


def on_device(
    patches,
    norm_gain,
    norm_bias,
    up_weight,
    up_bias,
    down_weight,
    down_bias,
    final_gain,
    final_bias,
    head_weight,
    gauss_rows,
    tile_lists,
    alphas,
):
    view_count, tiles_view, cells, width = patches.shape
    feat = head_weight.shape[1]
    n_img = lax.axis_size("img")
    n_tile = lax.axis_size("tile")
    peers = n_img * n_tile
    both = ("img", "tile")
    held = gauss_rows.shape[0]
    group_views, strip_tiles, list_len = tile_lists.shape
    tiles = group_views * strip_tiles
    cap = 2 * tiles * list_len // peers

    wide_layer = n_tile // 4
    near = n_img * wide_layer
    tile = lax.axis_index("tile")
    layer = tile // wide_layer
    low = layer < 2
    outer = (layer == 0) | (layer == 3)
    groups = [[i * n_tile + z * wide_layer + k for i in range(n_img) for k in range(wide_layer)] for z in range(4)]

    def moves(*pairs):
        return [(a * wide_layer + k, b * wide_layer + k) for a, b in pairs for k in range(wide_layer)]

    beside = moves((0, 1), (1, 0), (2, 3), (3, 2))
    middle = moves((1, 2), (2, 1))
    inwards = moves((0, 1), (3, 2))
    outwards = moves((1, 0), (2, 3))

    def move(x, pairs):
        return lax.ppermute(x, "tile", pairs)

    def exchange(x):
        return lax.all_to_all(x, both, split_axis=0, concat_axis=0, axis_index_groups=groups, tiled=True)

    def tie(*values):
        return lax.optimization_barrier(values)

    request, own, rank = index(tile_lists.reshape(tiles, list_len), peers, cap, held)
    asked = lax.all_to_all(request, both, split_axis=0, concat_axis=0, tiled=True)
    patches = patches.reshape(n_tile, -1, width)
    strips = []
    for n in reversed(range(n_tile)):
        strip = lax.dynamic_index_in_dim(patches, lax.rem(tile + n, n_tile), 0, keepdims=False)
        strips.append(move(strip, [(a, (a + n) % n_tile) for a in range(n_tile)]) if n else strip)
    first = lax.rem(2 * n_tile - 1 - tile, n_tile).astype(I32).reshape(1)
    asked = asked.reshape(n_img, 4, wide_layer, cap)
    sets = (jnp.where(low, 3, 0), jnp.where(low, 2, 1), layer ^ 1, layer)
    lists = [lax.dynamic_index_in_dim(asked, s, 1, keepdims=False).reshape(near, cap) for s in sets]
    owners = (
        jnp.arange(n_img, dtype=I32)[:, None] * n_tile
        + layer * wide_layer
        + jnp.arange(wide_layer, dtype=I32)[None, :]
    ).reshape(near)

    def spread_of(pack):
        n_cells = tiles * cells
        return spread(owners, pack[n_cells : n_cells + tiles], pack[n_cells + tiles :], pack[:n_cells], cap)

    looked, alphas, lists[1] = tie(gather(lists[0], gauss_rows), alphas, lists[1])
    rows_1 = exchange(looked)
    weight = weights(alphas.reshape(tiles * cells, list_len))
    packed = jnp.concatenate([weight, own, rank], 0)
    from_two = move(packed, moves((0, 2), (2, 0), (1, 3), (3, 1)))
    from_three = move(packed, moves((0, 3), (3, 0), (1, 2), (2, 1)))
    spread_1 = spread_of(jnp.where(outer, from_three, from_two))
    looked_2 = gather(lists[1], gauss_rows)
    looked_2, lists[2] = tie(looked_2, lists[2])
    looked_3 = gather(lists[2], gauss_rows)
    looked_2, looked_3, spread_1, rows_1, from_two, from_three, packed = tie(
        looked_2, looked_3, spread_1, rows_1, from_two, from_three, packed
    )

    rows_2 = exchange(looked_2)
    part_1 = blend(spread_1, rows_1)
    moved_1 = move(part_1, inwards)
    from_beside = move(packed, beside)
    part_1, *strips = tie(part_1, *strips)
    target = encode(
        strips, norm_gain, norm_bias, up_weight, up_bias, down_weight, down_bias, final_gain, final_bias, head_weight
    )
    looked_3, rows_2, part_1, moved_1, target, lists[3], from_beside, from_two = tie(
        looked_3, rows_2, part_1, moved_1, target, lists[3], from_beside, from_two
    )

    rows_3 = exchange(looked_3)
    far = move(part_1 + moved_1, middle)
    spread_2 = spread_of(jnp.where(outer, from_two, from_three))
    part_2 = blend(spread_2, rows_2)
    moved_2 = move(part_2, inwards)
    part_2, lists[3], from_beside = tie(part_2, lists[3], from_beside)
    looked_4 = gather(lists[3], gauss_rows)
    spread_3 = spread_of(from_beside)
    looked_4, rows_3, far, spread_3, packed = tie(looked_4, rows_3, far, spread_3, packed)

    rows_4 = exchange(looked_4)
    part_3 = blend(spread_3, rows_3, (far,))
    beside_part = move(part_3, beside)
    part_2, moved_2, part_3, packed = tie(part_2, moved_2, part_3, packed)
    middle_part = move(part_2 + moved_2, middle)
    spread_4 = spread_of(packed)
    color, diff = blend(spread_4, rows_4, (beside_part, middle_part), first, target)
    spreads = (spread_1, spread_2, spread_3, spread_4)

    diff_beside = move(diff, beside)
    diff_middle = move(diff, middle)
    far_middle = move(diff_beside, middle)
    diff_out = move(diff_middle, outwards)
    far_out = move(far_middle, outwards)
    back = []
    for n, diffs in ((3, (diff,)), (2, (diff_beside,)), (1, (diff_middle, diff_out)), (0, (far_middle, far_out))):
        term = terms(spreads[n], *diffs)
        if back:
            term, back[-1] = lax.optimization_barrier((term, back[-1]))
        back.append(exchange(term))
    grad = add_rows([lists[3], lists[2], lists[1]], back[:3], held)
    grad = add_rows([lists[0]], back[3:], held, grad)
    return (color.reshape(group_views, strip_tiles, cells, feat), grad)


def solution(mesh):
    placed = (
        P(("img", "tile"), None, None, None),
        P(),
        P(),
        P(),
        P(),
        P(),
        P(),
        P(),
        P(),
        P(),
        P(("img", "tile"), None),
        P("img", "tile", None),
        P("img", "tile", None, None),
    )
    return jax.shard_map(
        on_device,
        mesh=mesh,
        in_specs=placed,
        out_specs=(P("img", "tile", None, None), P(("img", "tile"), None)),
        check_vma=False,
    )
```

```python
import functools

import jax
import jax.numpy as jnp
from jax import lax
from jax.experimental import pallas as pl
from jax.experimental.pallas import tpu as pltpu
from jax.sharding import PartitionSpec as P

F32 = jnp.float32
BF16 = jnp.bfloat16
I32 = jnp.int32
VMEM_BYTES = 50 * 1024 * 1024
LANES = (((1,), (1,)), ((), ()))
ROWS = (((0,), (0,)), ((), ()))


def params():
    return pltpu.CompilerParams(vmem_limit_bytes=VMEM_BYTES)


def index_kernel(peers, cap, rows_held, ids_ref, req_ref, own_ref, rank_ref):
    tiles, length = ids_ref.shape
    earlier = lax.broadcasted_iota(I32, (length, length), 0)
    later = lax.broadcasted_iota(I32, (length, length), 1)
    upper = (earlier < later).astype(BF16)
    every = jnp.ones((length, length), BF16)
    peer_id = lax.broadcasted_iota(I32, (peers, length), 0)
    slot_id = lax.broadcasted_iota(I32, (cap, length), 0)
    hots = []
    for t in range(tiles):
        owner = ids_ref[t : t + 1, :] // rows_held
        own_ref[t : t + 1, :] = owner.astype(F32).astype(BF16)
        hots.append((jnp.broadcast_to(owner, (peers, length)) == peer_id).astype(F32))
    stack = jnp.concatenate(hots, 0).astype(BF16)
    within = jnp.dot(stack, upper, preferred_element_type=F32)
    totals = jnp.dot(stack, every, preferred_element_type=F32)
    offset = jnp.zeros((peers, length), F32)
    found = jnp.zeros((2 * peers, cap), F32)
    for t in range(tiles):
        own_rows = slice(t * peers, (t + 1) * peers)
        rank = jnp.sum(hots[t] * (within[own_rows] + offset), axis=0, keepdims=True).astype(I32)
        offset = offset + totals[own_rows]
        rank_ref[t : t + 1, :] = rank.astype(F32).astype(BF16)
        ids = ids_ref[t : t + 1, :]
        row = ids - (ids // rows_held) * rows_held + 1
        high = (row >> 6).astype(F32)
        low = (row & 63).astype(F32)
        digits = jnp.concatenate([hots[t] * high, hots[t] * low], 0).astype(BF16)
        slots = (jnp.broadcast_to(rank, (cap, length)) == slot_id).astype(F32).astype(BF16)
        found = found + lax.dot_general(digits, slots, LANES, preferred_element_type=F32)
    req_ref[...] = (found[:peers] * 64.0 + found[peers:]).astype(I32) - 1


def index(ids, peers, cap, rows_held):
    like = jax.ShapeDtypeStruct(ids.shape, BF16)
    return pl.pallas_call(
        functools.partial(index_kernel, peers, cap, rows_held),
        out_shape=(jax.ShapeDtypeStruct((peers, cap), I32), like, like),
        compiler_params=params(),
        cost_estimate=pl.CostEstimate(flops=10**9, bytes_accessed=10**7, transcendentals=0),
        name="index",
    )(ids)


def weights_kernel(alpha_ref, out_ref):
    alpha = alpha_ref[...]
    length = alpha.shape[1]
    logs = jnp.log1p(-alpha)
    earlier = lax.broadcasted_iota(I32, (length, length), 0)
    later = lax.broadcasted_iota(I32, (length, length), 1)
    upper = (earlier < later).astype(F32)
    before = jnp.dot(logs, upper, preferred_element_type=F32, precision=lax.Precision.HIGHEST)
    out_ref[...] = (alpha * jnp.exp(before)).astype(BF16)


def weights(alphas):
    return pl.pallas_call(
        weights_kernel,
        out_shape=jax.ShapeDtypeStruct(alphas.shape, BF16),
        compiler_params=params(),
        cost_estimate=pl.CostEstimate(flops=10**8, bytes_accessed=10**6, transcendentals=0),
        name="weights",
    )(alphas)


def spread_kernel(near, cap, base_ref, own_ref, rank_ref, weight_ref, out_ref):
    tiles, length = own_ref.shape
    cells = weight_ref.shape[0] // tiles
    slot_id = lax.broadcasted_iota(I32, (cap, length), 0)
    for t in range(tiles):
        own = own_ref[t : t + 1, :].astype(I32)
        rank = rank_ref[t : t + 1, :].astype(I32)
        here = slice(t * cells, (t + 1) * cells)
        weight = weight_ref[here, :].astype(F32)
        by_owner = [jnp.where(own == base_ref[o], weight, 0.0) for o in range(near)]
        slots = (jnp.broadcast_to(rank, (cap, length)) == slot_id).astype(F32).astype(BF16)
        moved = lax.dot_general(
            jnp.concatenate(by_owner, 0).astype(BF16), slots, LANES, preferred_element_type=F32
        ).astype(BF16)
        if cap % 128 == 0:
            for o in range(near):
                out_ref[here, o * cap : (o + 1) * cap] = moved[o * cells : (o + 1) * cells]
        else:
            out_ref[here, :] = jnp.concatenate([moved[o * cells : (o + 1) * cells] for o in range(near)], 1)


def spread(owners, own, rank, weight, cap):
    tiles, length = own.shape
    cells = weight.shape[0] // tiles
    near = owners.shape[0]
    step = 16
    lists = pl.BlockSpec((step, length), lambda t: (t, 0))
    return pl.pallas_call(
        functools.partial(spread_kernel, near, cap),
        grid=(tiles // step,),
        in_specs=[pl.BlockSpec(memory_space=pltpu.SMEM), lists, lists, pl.BlockSpec((step * cells, length), lambda t: (t, 0))],
        out_specs=pl.BlockSpec((step * cells, near * cap), lambda t: (t, 0)),
        out_shape=jax.ShapeDtypeStruct((weight.shape[0], near * cap), BF16),
        compiler_params=params(),
        cost_estimate=pl.CostEstimate(flops=10**8, bytes_accessed=10**6, transcendentals=0),
        name="spread",
    )(owners, own, rank, weight)


def gather_kernel(group, cap, asked_ref, rows_ref, out_ref):
    first = pl.program_id(0) * group
    asked = asked_ref[...]
    peer = lax.broadcasted_iota(I32, asked.shape, 1)
    held = rows_ref.shape[0]
    row_id = lax.broadcasted_iota(I32, (cap, held), 1)
    picks = []
    for q in range(group):
        column = jnp.sum(jnp.where(peer == first + q, asked, 0), axis=1, keepdims=True)
        picks.append((jnp.broadcast_to(column, (cap, held)) == row_id).astype(F32).astype(BF16))
    pick = jnp.concatenate(picks, 0)
    out_ref[...] = jnp.dot(pick, rows_ref[...], preferred_element_type=F32).astype(BF16)


def gather(asked, rows):
    near, cap = asked.shape
    held, feat = rows.shape
    group = max(1, min(near, 1024 // cap))
    return pl.pallas_call(
        functools.partial(gather_kernel, group, cap),
        grid=(near // group,),
        in_specs=[pl.BlockSpec((cap, near), lambda i: (0, 0)), pl.BlockSpec((held, feat), lambda i: (0, 0))],
        out_specs=pl.BlockSpec((group * cap, feat), lambda i: (i, 0)),
        out_shape=jax.ShapeDtypeStruct((near * cap, feat), BF16),
        compiler_params=params(),
        cost_estimate=pl.CostEstimate(flops=10**8, bytes_accessed=10**6, transcendentals=0),
        name="gather",
    )(asked.T, rows)


def blend_kernel(n_parts, weight_ref, rows_ref, *rest):
    color = jnp.dot(weight_ref[...], rows_ref[...], preferred_element_type=F32)
    for part_ref in rest[:n_parts]:
        color = color + part_ref[...].astype(F32)
    rest[n_parts][...] = color.astype(BF16)


def last_blend_kernel(n_parts, place_ref, weight_ref, rows_ref, *rest):
    parts, target_ref = rest[:n_parts], rest[n_parts]
    color_ref, diff_ref = rest[-2:]
    color = jnp.dot(weight_ref[...], rows_ref[...], preferred_element_type=F32)
    for part_ref in parts:
        color = color + part_ref[...].astype(F32)
    color_ref[...] = color.astype(BF16)
    cells = target_ref.shape[1]
    per_step = color.shape[0] // cells
    for k in range(per_step):
        at = place_ref[pl.program_id(0) * per_step + k]
        here = slice(k * cells, (k + 1) * cells)
        diff_ref[here, :] = (color[here] - target_ref[at].astype(F32)).astype(BF16)


def blend(weight, rows, parts=(), place=None, target=None):
    cells, slots = weight.shape
    feat = rows.shape[1]
    block = min(cells, 256)
    cell_block = pl.BlockSpec((block, feat), lambda i: (i, 0))
    out = jax.ShapeDtypeStruct((cells, feat), BF16)
    last = place is not None
    in_specs = [pl.BlockSpec((block, slots), lambda i: (i, 0)), pl.BlockSpec((slots, feat), lambda i: (0, 0))]
    in_specs += [cell_block] * len(parts)
    args = [weight, rows, *parts]
    if last:
        in_specs = [pl.BlockSpec(memory_space=pltpu.SMEM)] + in_specs + [pl.BlockSpec(target.shape, lambda i: (0, 0, 0))]
        args = [place, *args, target]
    return pl.pallas_call(
        functools.partial(last_blend_kernel if last else blend_kernel, len(parts)),
        grid=(cells // block,),
        in_specs=in_specs,
        out_specs=(cell_block, cell_block) if last else cell_block,
        out_shape=(out, out) if last else out,
        compiler_params=params(),
        cost_estimate=pl.CostEstimate(flops=4 * 10**9, bytes_accessed=10**7, transcendentals=0),
        name="blend",
    )(*args)


def terms_kernel(weight_ref, *refs):
    diff = refs[0][...]
    for more_ref in refs[1:-1]:
        diff = diff + more_ref[...]
    refs[-1][...] = lax.dot_general(weight_ref[...], diff, ROWS, preferred_element_type=F32).astype(BF16)


def terms(weight, *diffs):
    cells, slots = weight.shape
    feat = diffs[0].shape[1]
    block = min(slots, 1024)
    return pl.pallas_call(
        terms_kernel,
        grid=(slots // block,),
        in_specs=[pl.BlockSpec((cells, block), lambda i: (0, i))]
        + [pl.BlockSpec((cells, feat), lambda i: (0, 0))] * len(diffs),
        out_specs=pl.BlockSpec((block, feat), lambda i: (i, 0)),
        out_shape=jax.ShapeDtypeStruct((slots, feat), BF16),
        compiler_params=params(),
        cost_estimate=pl.CostEstimate(flops=10**11, bytes_accessed=10**7, transcendentals=0),
        name="terms",
    )(weight, *diffs)


def add_rows_kernel(count, *refs):
    out_ref = refs[-1]
    block = out_ref.shape[0]
    total = None if len(refs) == 2 * count + 1 else refs[2 * count][...]
    for n in range(count):
        asked_ref, terms_ref = refs[n], refs[count + n]
        near, cap = asked_ref.shape
        row_id = lax.broadcasted_iota(I32, (block, cap), 0) + pl.program_id(0) * block
        picks = []
        for o in range(near):
            asked = jnp.broadcast_to(asked_ref[o : o + 1, :], (block, cap))
            picks.append((asked == row_id).astype(F32).astype(BF16))
        got = jnp.dot(jnp.concatenate(picks, 1), terms_ref[...], preferred_element_type=F32)
        total = got if total is None else total + got
    out_ref[...] = total


def add_rows(askeds, arrivals, held, before=None):
    near, cap = askeds[0].shape
    feat = arrivals[0].shape[1]
    count = len(askeds)
    block = min(held, 512)
    row_block = pl.BlockSpec((block, feat), lambda i: (i, 0))
    more = before is not None
    in_specs = [pl.BlockSpec((near, cap), lambda i: (0, 0))] * count
    in_specs += [pl.BlockSpec((near * cap, feat), lambda i: (0, 0))] * count
    return pl.pallas_call(
        functools.partial(add_rows_kernel, count),
        grid=(held // block,),
        in_specs=in_specs + [row_block] * more,
        out_specs=row_block,
        out_shape=jax.ShapeDtypeStruct((held, feat), F32),
        compiler_params=params(),
        cost_estimate=pl.CostEstimate(flops=5 * count * 10**9, bytes_accessed=10**7, transcendentals=0),
        name="add_rows",
    )(*askeds, *arrivals, *((before,) if more else ()))


def layer_norm(rows, gain, bias):
    mean = jnp.mean(rows, axis=-1, keepdims=True)
    centred = rows - mean
    var = jnp.mean(centred * centred, axis=-1, keepdims=True)
    return centred * lax.rsqrt(var + 1e-05) * gain + bias


def encode_kernel(strips, *refs):
    gain, bias, up, up_bias, down, down_bias, last_gain, last_bias, head = refs[strips:-1]
    out_ref = refs[-1]
    hidden = up.shape[1]
    step = 768 if hidden % 768 == 0 else hidden
    group = max(1, strips // 2)
    for first in range(0, strips, group):
        wide = jnp.concatenate([ref[...] for ref in refs[first : first + group]], 0).astype(F32)
        normed = layer_norm(wide, gain[...], bias[...]).astype(BF16)
        block_out = wide + down_bias[...]
        for k in range(0, hidden, step):
            inner = jnp.dot(normed, up[:, k : k + step], preferred_element_type=F32) + up_bias[:, k : k + step]
            act = (inner * jax.nn.sigmoid(1.702 * inner)).astype(BF16)
            block_out = block_out + jnp.dot(act, down[k : k + step, :], preferred_element_type=F32)
        final = layer_norm(block_out, last_gain[...], last_bias[...]).astype(BF16)
        embed = jnp.dot(final, head[...], preferred_element_type=F32)
        scale = lax.rsqrt(jnp.mean(embed * embed, axis=-1, keepdims=True) + 1e-06)
        target = (embed * scale).astype(BF16)
        cells = target.shape[0] // group
        for n in range(group):
            out_ref[first + n] = target[n * cells : (n + 1) * cells]


def encode(strips, *weights_and_biases):
    args = [w.reshape(1, -1) if w.ndim == 1 else w for w in weights_and_biases]
    cells = strips[0].shape[0]
    return pl.pallas_call(
        functools.partial(encode_kernel, len(strips)),
        out_shape=jax.ShapeDtypeStruct((len(strips), cells, args[-1].shape[1]), BF16),
        compiler_params=params(),
        cost_estimate=pl.CostEstimate(flops=10**11, bytes_accessed=10**7, transcendentals=0),
        name="encode",
    )(*strips, *args)


def on_device(
    patches,
    norm_gain,
    norm_bias,
    up_weight,
    up_bias,
    down_weight,
    down_bias,
    final_gain,
    final_bias,
    head_weight,
    gauss_rows,
    tile_lists,
    alphas,
):
    view_count, tiles_view, cells, width = patches.shape
    feat = head_weight.shape[1]
    n_img = lax.axis_size("img")
    n_tile = lax.axis_size("tile")
    peers = n_img * n_tile
    both = ("img", "tile")
    held = gauss_rows.shape[0]
    group_views, strip_tiles, list_len = tile_lists.shape
    tiles = group_views * strip_tiles
    cap = 2 * tiles * list_len // peers

    wide_layer = n_tile // 4
    near = n_img * wide_layer
    tile = lax.axis_index("tile")
    layer = tile // wide_layer
    low = layer < 2
    outer = (layer == 0) | (layer == 3)
    groups = [[i * n_tile + z * wide_layer + k for i in range(n_img) for k in range(wide_layer)] for z in range(4)]

    def moves(*pairs):
        return [(a * wide_layer + k, b * wide_layer + k) for a, b in pairs for k in range(wide_layer)]

    beside = moves((0, 1), (1, 0), (2, 3), (3, 2))
    middle = moves((1, 2), (2, 1))
    inwards = moves((0, 1), (3, 2))
    outwards = moves((1, 0), (2, 3))

    def move(x, pairs):
        return lax.ppermute(x, "tile", pairs)

    def exchange(x):
        return lax.all_to_all(x, both, split_axis=0, concat_axis=0, axis_index_groups=groups, tiled=True)

    def tie(*values):
        return lax.optimization_barrier(values)

    request, own, rank = index(tile_lists.reshape(tiles, list_len), peers, cap, held)
    request, patches = tie(request, patches)
    asked = lax.all_to_all(request, both, split_axis=0, concat_axis=0, tiled=True)
    chips = n_tile // 2
    core = tile % 2
    chip = tile // 2
    patches = patches.reshape(chips, 2, -1, width)
    others = lax.dynamic_index_in_dim(patches, 1 - core, 1, keepdims=False)
    others = move(others, [(a, a ^ 1) for a in range(n_tile)])
    asked, others = tie(asked, others)
    pairs = jnp.concatenate([lax.dynamic_index_in_dim(patches, core, 1, keepdims=False), others], 1)
    strips = []
    for n in range(chips):
        pair = lax.dynamic_index_in_dim(pairs, lax.rem(chip + n, chips), 0, keepdims=False)
        strips.append(move(pair, [(a, (a + 2 * n) % n_tile) for a in range(n_tile)]) if n else pair)
    view = jnp.arange(n_tile, dtype=I32)
    place = lax.rem(chip + chips - view // 2, chips) * 2 + (view % 2 != core).astype(I32)
    asked = asked.reshape(n_img, 4, wide_layer, cap)
    sets = (jnp.where(low, 3, 0), jnp.where(low, 2, 1), layer ^ 1, layer)
    lists = [lax.dynamic_index_in_dim(asked, s, 1, keepdims=False).reshape(near, cap) for s in sets]
    owners = (
        jnp.arange(n_img, dtype=I32)[:, None] * n_tile
        + layer * wide_layer
        + jnp.arange(wide_layer, dtype=I32)[None, :]
    ).reshape(near)

    def spread_of(pack):
        n_cells = tiles * cells
        return spread(owners, pack[n_cells : n_cells + tiles], pack[n_cells + tiles :], pack[:n_cells], cap)

    looked, lists[1] = tie(gather(lists[0], gauss_rows), lists[1])
    rows_1 = exchange(looked)
    looked_2 = gather(lists[1], gauss_rows)
    looked_2, lists[2], alphas = tie(looked_2, lists[2], alphas)
    weight = weights(alphas.reshape(tiles * cells, list_len))
    packed = jnp.concatenate([weight, own, rank], 0)
    from_two = move(packed, moves((0, 2), (2, 0), (1, 3), (3, 1)))
    from_three = move(packed, moves((0, 3), (3, 0), (1, 2), (2, 1)))
    spread_1 = spread_of(jnp.where(outer, from_three, from_two))
    looked_3 = gather(lists[2], gauss_rows)
    looked_2, looked_3, spread_1, rows_1, from_two, from_three, packed = tie(
        looked_2, looked_3, spread_1, rows_1, from_two, from_three, packed
    )

    rows_2 = exchange(looked_2)
    part_1 = blend(spread_1, rows_1)
    moved_1 = move(part_1, inwards)
    part_1, *strips = tie(part_1, *strips)
    target = encode(
        strips, norm_gain, norm_bias, up_weight, up_bias, down_weight, down_bias, final_gain, final_bias, head_weight
    )
    looked_3, rows_2, part_1, target, lists[3], packed, from_two = tie(
        looked_3, rows_2, part_1, target, lists[3], packed, from_two
    )

    rows_3 = exchange(looked_3)
    from_beside = move(packed, beside)
    far = move(part_1 + moved_1, middle)
    spread_2 = spread_of(jnp.where(outer, from_two, from_three))
    part_2 = blend(spread_2, rows_2)
    moved_2 = move(part_2, inwards)
    part_2, lists[3], from_beside = tie(part_2, lists[3], from_beside)
    looked_4 = gather(lists[3], gauss_rows)
    spread_3 = spread_of(from_beside)
    looked_4, rows_3, far, spread_3, packed = tie(looked_4, rows_3, far, spread_3, packed)

    rows_4 = exchange(looked_4)
    part_3 = blend(spread_3, rows_3, (far,))
    beside_part = move(part_3, beside)
    part_2, moved_2, part_3, packed = tie(part_2, moved_2, part_3, packed)
    middle_part = move(part_2 + moved_2, middle)
    spread_4 = spread_of(packed)
    color, diff = blend(spread_4, rows_4, (beside_part, middle_part), place, target.reshape(n_tile, -1, feat))
    spreads = (spread_1, spread_2, spread_3, spread_4)

    diff_beside = move(diff, beside)
    diff_middle = move(diff, middle)
    far_middle = move(diff_beside, middle)
    diff_out = move(diff_middle, outwards)
    far_out = move(far_middle, outwards)
    back = []
    for n, diffs in ((3, (diff,)), (2, (diff_beside,)), (1, (diff_middle, diff_out)), (0, (far_middle, far_out))):
        term = terms(spreads[n], *diffs)
        if back:
            term, back[-1] = lax.optimization_barrier((term, back[-1]))
        back.append(exchange(term))
    grad = add_rows([lists[3], lists[2], lists[1]], back[:3], held)
    grad = add_rows([lists[0]], back[3:], held, grad)
    return (color.reshape(group_views, strip_tiles, cells, feat), grad)


def solution(mesh):
    placed = (
        P(("img", "tile"), None, None, None),
        P(),
        P(),
        P(),
        P(),
        P(),
        P(),
        P(),
        P(),
        P(),
        P(("img", "tile"), None),
        P("img", "tile", None),
        P("img", "tile", None, None),
    )
    return jax.shard_map(
        on_device,
        mesh=mesh,
        in_specs=placed,
        out_specs=(P("img", "tile", None, None), P(("img", "tile"), None)),
        check_vma=False,
    )
```

```python
import functools

import jax
import jax.numpy as jnp
from jax import lax
from jax.experimental import pallas as pl
from jax.experimental.pallas import tpu as pltpu
from jax.sharding import PartitionSpec as P

F32 = jnp.float32
BF16 = jnp.bfloat16
I32 = jnp.int32
VMEM_BYTES = 50 * 1024 * 1024
LANES = (((1,), (1,)), ((), ()))
ROWS = (((0,), (0,)), ((), ()))


def params():
    return pltpu.CompilerParams(vmem_limit_bytes=VMEM_BYTES)


def index_kernel(peers, cap, rows_held, ids_ref, req_ref, own_ref, rank_ref):
    tiles, length = ids_ref.shape
    earlier = lax.broadcasted_iota(I32, (length, length), 0)
    later = lax.broadcasted_iota(I32, (length, length), 1)
    upper = (earlier < later).astype(BF16)
    every = jnp.ones((length, length), BF16)
    peer_id = lax.broadcasted_iota(I32, (peers, length), 0)
    slot_id = lax.broadcasted_iota(I32, (cap, length), 0)
    hots = []
    for t in range(tiles):
        owner = ids_ref[t : t + 1, :] // rows_held
        own_ref[t : t + 1, :] = owner.astype(F32).astype(BF16)
        hots.append((jnp.broadcast_to(owner, (peers, length)) == peer_id).astype(F32))
    stack = jnp.concatenate(hots, 0).astype(BF16)
    within = jnp.dot(stack, upper, preferred_element_type=F32)
    totals = jnp.dot(stack, every, preferred_element_type=F32)
    offset = jnp.zeros((peers, length), F32)
    found = jnp.zeros((2 * peers, cap), F32)
    for t in range(tiles):
        own_rows = slice(t * peers, (t + 1) * peers)
        rank = jnp.sum(hots[t] * (within[own_rows] + offset), axis=0, keepdims=True).astype(I32)
        offset = offset + totals[own_rows]
        rank_ref[t : t + 1, :] = rank.astype(F32).astype(BF16)
        ids = ids_ref[t : t + 1, :]
        row = ids - (ids // rows_held) * rows_held + 1
        high = (row >> 6).astype(F32)
        low = (row & 63).astype(F32)
        digits = jnp.concatenate([hots[t] * high, hots[t] * low], 0).astype(BF16)
        slots = (jnp.broadcast_to(rank, (cap, length)) == slot_id).astype(F32).astype(BF16)
        found = found + lax.dot_general(digits, slots, LANES, preferred_element_type=F32)
    req_ref[...] = (found[:peers] * 64.0 + found[peers:]).astype(I32) - 1


def index(ids, peers, cap, rows_held):
    like = jax.ShapeDtypeStruct(ids.shape, BF16)
    return pl.pallas_call(
        functools.partial(index_kernel, peers, cap, rows_held),
        out_shape=(jax.ShapeDtypeStruct((peers, cap), I32), like, like),
        compiler_params=params(),
        cost_estimate=pl.CostEstimate(flops=10**9, bytes_accessed=10**7, transcendentals=0),
        name="index",
    )(ids)


def weights_kernel(alpha_ref, out_ref):
    alpha = alpha_ref[...]
    length = alpha.shape[1]
    logs = jnp.log1p(-alpha)
    earlier = lax.broadcasted_iota(I32, (length, length), 0)
    later = lax.broadcasted_iota(I32, (length, length), 1)
    upper = (earlier < later).astype(F32)
    before = jnp.dot(logs, upper, preferred_element_type=F32, precision=lax.Precision.HIGHEST)
    out_ref[...] = (alpha * jnp.exp(before)).astype(BF16)


def weights(alphas):
    return pl.pallas_call(
        weights_kernel,
        out_shape=jax.ShapeDtypeStruct(alphas.shape, BF16),
        compiler_params=params(),
        cost_estimate=pl.CostEstimate(flops=10**8, bytes_accessed=10**6, transcendentals=0),
        name="weights",
    )(alphas)


def spread_kernel(near, cap, base_ref, own_ref, rank_ref, weight_ref, out_ref):
    tiles, length = own_ref.shape
    cells = weight_ref.shape[0] // tiles
    slot_id = lax.broadcasted_iota(I32, (cap, length), 0)
    for t in range(tiles):
        own = own_ref[t : t + 1, :].astype(I32)
        rank = rank_ref[t : t + 1, :].astype(I32)
        here = slice(t * cells, (t + 1) * cells)
        weight = weight_ref[here, :].astype(F32)
        by_owner = [jnp.where(own == base_ref[o], weight, 0.0) for o in range(near)]
        slots = (jnp.broadcast_to(rank, (cap, length)) == slot_id).astype(F32).astype(BF16)
        moved = lax.dot_general(
            jnp.concatenate(by_owner, 0).astype(BF16), slots, LANES, preferred_element_type=F32
        ).astype(BF16)
        if cap % 128 == 0:
            for o in range(near):
                out_ref[here, o * cap : (o + 1) * cap] = moved[o * cells : (o + 1) * cells]
        else:
            out_ref[here, :] = jnp.concatenate([moved[o * cells : (o + 1) * cells] for o in range(near)], 1)


def spread(owners, own, rank, weight, cap):
    tiles, length = own.shape
    cells = weight.shape[0] // tiles
    near = owners.shape[0]
    step = 16
    lists = pl.BlockSpec((step, length), lambda t: (t, 0))
    return pl.pallas_call(
        functools.partial(spread_kernel, near, cap),
        grid=(tiles // step,),
        in_specs=[pl.BlockSpec(memory_space=pltpu.SMEM), lists, lists, pl.BlockSpec((step * cells, length), lambda t: (t, 0))],
        out_specs=pl.BlockSpec((step * cells, near * cap), lambda t: (t, 0)),
        out_shape=jax.ShapeDtypeStruct((weight.shape[0], near * cap), BF16),
        compiler_params=params(),
        cost_estimate=pl.CostEstimate(flops=10**8, bytes_accessed=10**6, transcendentals=0),
        name="spread",
    )(owners, own, rank, weight)


def gather_kernel(group, cap, asked_ref, rows_ref, out_ref):
    first = pl.program_id(0) * group
    asked = asked_ref[...]
    peer = lax.broadcasted_iota(I32, asked.shape, 1)
    held = rows_ref.shape[0]
    row_id = lax.broadcasted_iota(I32, (cap, held), 1)
    picks = []
    for q in range(group):
        column = jnp.sum(jnp.where(peer == first + q, asked, 0), axis=1, keepdims=True)
        picks.append((jnp.broadcast_to(column, (cap, held)) == row_id).astype(F32).astype(BF16))
    pick = jnp.concatenate(picks, 0)
    out_ref[...] = jnp.dot(pick, rows_ref[...], preferred_element_type=F32).astype(BF16)


def gather(asked, rows):
    near, cap = asked.shape
    held, feat = rows.shape
    group = max(1, min(near, 1024 // cap))
    return pl.pallas_call(
        functools.partial(gather_kernel, group, cap),
        grid=(near // group,),
        in_specs=[pl.BlockSpec((cap, near), lambda i: (0, 0)), pl.BlockSpec((held, feat), lambda i: (0, 0))],
        out_specs=pl.BlockSpec((group * cap, feat), lambda i: (i, 0)),
        out_shape=jax.ShapeDtypeStruct((near * cap, feat), BF16),
        compiler_params=params(),
        cost_estimate=pl.CostEstimate(flops=10**8, bytes_accessed=10**6, transcendentals=0),
        name="gather",
    )(asked.T, rows)


def blend_kernel(n_parts, weight_ref, rows_ref, *rest):
    color = jnp.dot(weight_ref[...], rows_ref[...], preferred_element_type=F32)
    for part_ref in rest[:n_parts]:
        color = color + part_ref[...].astype(F32)
    rest[n_parts][...] = color.astype(BF16)


def last_blend_kernel(n_parts, place_ref, weight_ref, rows_ref, *rest):
    parts, target_ref = rest[:n_parts], rest[n_parts]
    color_ref, diff_ref = rest[-2:]
    color = jnp.dot(weight_ref[...], rows_ref[...], preferred_element_type=F32)
    for part_ref in parts:
        color = color + part_ref[...].astype(F32)
    color_ref[...] = color.astype(BF16)
    cells = target_ref.shape[1]
    per_step = color.shape[0] // cells
    for k in range(per_step):
        at = place_ref[pl.program_id(0) * per_step + k]
        here = slice(k * cells, (k + 1) * cells)
        diff_ref[here, :] = (color[here] - target_ref[at].astype(F32)).astype(BF16)


def blend(weight, rows, parts=(), place=None, target=None):
    cells, slots = weight.shape
    feat = rows.shape[1]
    block = min(cells, 256)
    cell_block = pl.BlockSpec((block, feat), lambda i: (i, 0))
    out = jax.ShapeDtypeStruct((cells, feat), BF16)
    last = place is not None
    in_specs = [pl.BlockSpec((block, slots), lambda i: (i, 0)), pl.BlockSpec((slots, feat), lambda i: (0, 0))]
    in_specs += [cell_block] * len(parts)
    args = [weight, rows, *parts]
    if last:
        in_specs = [pl.BlockSpec(memory_space=pltpu.SMEM)] + in_specs + [pl.BlockSpec(target.shape, lambda i: (0, 0, 0))]
        args = [place, *args, target]
    return pl.pallas_call(
        functools.partial(last_blend_kernel if last else blend_kernel, len(parts)),
        grid=(cells // block,),
        in_specs=in_specs,
        out_specs=(cell_block, cell_block) if last else cell_block,
        out_shape=(out, out) if last else out,
        compiler_params=params(),
        cost_estimate=pl.CostEstimate(flops=4 * 10**9, bytes_accessed=10**7, transcendentals=0),
        name="blend",
    )(*args)


def terms_kernel(weight_ref, *refs):
    diff = refs[0][...]
    for more_ref in refs[1:-1]:
        diff = diff + more_ref[...]
    refs[-1][...] = lax.dot_general(weight_ref[...], diff, ROWS, preferred_element_type=F32).astype(BF16)


def terms(weight, *diffs):
    cells, slots = weight.shape
    feat = diffs[0].shape[1]
    block = min(slots, 1024)
    return pl.pallas_call(
        terms_kernel,
        grid=(slots // block,),
        in_specs=[pl.BlockSpec((cells, block), lambda i: (0, i))]
        + [pl.BlockSpec((cells, feat), lambda i: (0, 0))] * len(diffs),
        out_specs=pl.BlockSpec((block, feat), lambda i: (i, 0)),
        out_shape=jax.ShapeDtypeStruct((slots, feat), BF16),
        compiler_params=params(),
        cost_estimate=pl.CostEstimate(flops=10**11, bytes_accessed=10**7, transcendentals=0),
        name="terms",
    )(weight, *diffs)


def add_rows_kernel(count, *refs):
    out_ref = refs[-1]
    block = out_ref.shape[0]
    total = None if len(refs) == 2 * count + 1 else refs[2 * count][...]
    for n in range(count):
        asked_ref, terms_ref = refs[n], refs[count + n]
        near, cap = asked_ref.shape
        row_id = lax.broadcasted_iota(I32, (block, cap), 0) + pl.program_id(0) * block
        picks = []
        for o in range(near):
            asked = jnp.broadcast_to(asked_ref[o : o + 1, :], (block, cap))
            picks.append((asked == row_id).astype(F32).astype(BF16))
        got = jnp.dot(jnp.concatenate(picks, 1), terms_ref[...], preferred_element_type=F32)
        total = got if total is None else total + got
    out_ref[...] = total


def add_rows(askeds, arrivals, held, before=None):
    near, cap = askeds[0].shape
    feat = arrivals[0].shape[1]
    count = len(askeds)
    block = min(held, 512)
    row_block = pl.BlockSpec((block, feat), lambda i: (i, 0))
    more = before is not None
    in_specs = [pl.BlockSpec((near, cap), lambda i: (0, 0))] * count
    in_specs += [pl.BlockSpec((near * cap, feat), lambda i: (0, 0))] * count
    return pl.pallas_call(
        functools.partial(add_rows_kernel, count),
        grid=(held // block,),
        in_specs=in_specs + [row_block] * more,
        out_specs=row_block,
        out_shape=jax.ShapeDtypeStruct((held, feat), F32),
        compiler_params=params(),
        cost_estimate=pl.CostEstimate(flops=5 * count * 10**9, bytes_accessed=10**7, transcendentals=0),
        name="add_rows",
    )(*askeds, *arrivals, *((before,) if more else ()))


def layer_norm(rows, gain, bias):
    mean = jnp.mean(rows, axis=-1, keepdims=True)
    centred = rows - mean
    var = jnp.mean(centred * centred, axis=-1, keepdims=True)
    return centred * lax.rsqrt(var + 1e-05) * gain + bias


def encode_kernel(strips, *refs):
    gain, bias, up, up_bias, down, down_bias, last_gain, last_bias, head = refs[strips:-1]
    out_ref = refs[-1]
    hidden = up.shape[1]
    step = 768 if hidden % 768 == 0 else hidden
    group = max(1, strips // 2)
    for first in range(0, strips, group):
        wide = jnp.concatenate([ref[...] for ref in refs[first : first + group]], 0).astype(F32)
        normed = layer_norm(wide, gain[...], bias[...]).astype(BF16)
        block_out = wide + down_bias[...]
        for k in range(0, hidden, step):
            inner = jnp.dot(normed, up[:, k : k + step], preferred_element_type=F32) + up_bias[:, k : k + step]
            act = (inner * jax.nn.sigmoid(1.702 * inner)).astype(BF16)
            block_out = block_out + jnp.dot(act, down[k : k + step, :], preferred_element_type=F32)
        final = layer_norm(block_out, last_gain[...], last_bias[...]).astype(BF16)
        embed = jnp.dot(final, head[...], preferred_element_type=F32)
        scale = lax.rsqrt(jnp.mean(embed * embed, axis=-1, keepdims=True) + 1e-06)
        target = (embed * scale).astype(BF16)
        cells = target.shape[0] // group
        for n in range(group):
            out_ref[first + n] = target[n * cells : (n + 1) * cells]


def encode(strips, *weights_and_biases):
    args = [w.reshape(1, -1) if w.ndim == 1 else w for w in weights_and_biases]
    cells = strips[0].shape[0]
    return pl.pallas_call(
        functools.partial(encode_kernel, len(strips)),
        out_shape=jax.ShapeDtypeStruct((len(strips), cells, args[-1].shape[1]), BF16),
        compiler_params=params(),
        cost_estimate=pl.CostEstimate(flops=10**11, bytes_accessed=10**7, transcendentals=0),
        name="encode",
    )(*strips, *args)


def on_device(
    patches,
    norm_gain,
    norm_bias,
    up_weight,
    up_bias,
    down_weight,
    down_bias,
    final_gain,
    final_bias,
    head_weight,
    gauss_rows,
    tile_lists,
    alphas,
):
    view_count, tiles_view, cells, width = patches.shape
    feat = head_weight.shape[1]
    n_img = lax.axis_size("img")
    n_tile = lax.axis_size("tile")
    peers = n_img * n_tile
    both = ("img", "tile")
    held = gauss_rows.shape[0]
    group_views, strip_tiles, list_len = tile_lists.shape
    tiles = group_views * strip_tiles
    cap = 2 * tiles * list_len // peers

    wide_layer = n_tile // 4
    near = n_img * wide_layer
    tile = lax.axis_index("tile")
    layer = tile // wide_layer
    low = layer < 2
    outer = (layer == 0) | (layer == 3)
    groups = [[i * n_tile + z * wide_layer + k for i in range(n_img) for k in range(wide_layer)] for z in range(4)]

    def moves(*pairs):
        return [(a * wide_layer + k, b * wide_layer + k) for a, b in pairs for k in range(wide_layer)]

    beside = moves((0, 1), (1, 0), (2, 3), (3, 2))
    middle = moves((1, 2), (2, 1))
    inwards = moves((0, 1), (3, 2))
    outwards = moves((1, 0), (2, 3))

    def move(x, pairs):
        return lax.ppermute(x, "tile", pairs)

    def exchange(x):
        return lax.all_to_all(x, both, split_axis=0, concat_axis=0, axis_index_groups=groups, tiled=True)

    def tie(*values):
        return lax.optimization_barrier(values)

    request, own, rank = index(tile_lists.reshape(tiles, list_len), peers, cap, held)
    weight = weights(alphas.reshape(tiles * cells, list_len))
    packed = jnp.concatenate([weight, own, rank], 0)
    request, patches = tie(request, patches)
    asked = lax.all_to_all(request, both, split_axis=0, concat_axis=0, tiled=True)
    chips = n_tile // 2
    core = tile % 2
    chip = tile // 2
    patches = patches.reshape(chips, 2, -1, width)
    others = lax.dynamic_index_in_dim(patches, 1 - core, 1, keepdims=False)
    others = move(others, [(a, a ^ 1) for a in range(n_tile)])
    asked, others, packed = tie(asked, others, packed)
    far_to_outer = move(packed, moves((0, 3), (3, 0)))
    far_to_inner = move(packed, moves((0, 2), (3, 1)))
    pairs = jnp.concatenate([lax.dynamic_index_in_dim(patches, core, 1, keepdims=False), others], 1)
    strips = []
    for n in range(chips):
        pair = lax.dynamic_index_in_dim(pairs, lax.rem(chip + n, chips), 0, keepdims=False)
        strips.append(move(pair, [(a, (a + 2 * n) % n_tile) for a in range(n_tile)]) if n else pair)
    view = jnp.arange(n_tile, dtype=I32)
    place = lax.rem(chip + chips - view // 2, chips) * 2 + (view % 2 != core).astype(I32)
    asked = asked.reshape(n_img, 4, wide_layer, cap)
    sets = (jnp.where(low, 3, 0), jnp.where(low, 2, 1), layer ^ 1, layer)
    lists = [lax.dynamic_index_in_dim(asked, s, 1, keepdims=False).reshape(near, cap) for s in sets]
    owners = (
        jnp.arange(n_img, dtype=I32)[:, None] * n_tile
        + layer * wide_layer
        + jnp.arange(wide_layer, dtype=I32)[None, :]
    ).reshape(near)

    def spread_of(pack):
        n_cells = tiles * cells
        return spread(owners, pack[n_cells : n_cells + tiles], pack[n_cells + tiles :], pack[:n_cells], cap)

    looked, lists[1] = tie(gather(lists[0], gauss_rows), lists[1])
    rows_1 = exchange(looked)
    looked_2 = gather(lists[1], gauss_rows)
    looked_2, lists[2] = tie(looked_2, lists[2])
    spread_1 = spread_of(jnp.where(outer, far_to_outer, far_to_inner))
    looked_3 = gather(lists[2], gauss_rows)
    looked_2, looked_3, spread_1, rows_1, packed = tie(looked_2, looked_3, spread_1, rows_1, packed)

    rows_2 = exchange(looked_2)
    part_1 = blend(spread_1, rows_1)
    moved_1 = move(part_1, inwards)
    near_to_outer = move(packed, moves((1, 3), (2, 0)))
    near_to_inner = move(packed, middle)
    from_beside = move(packed, beside)
    part_1, *strips = tie(part_1, *strips)
    target = encode(
        strips, norm_gain, norm_bias, up_weight, up_bias, down_weight, down_bias, final_gain, final_bias, head_weight
    )
    looked_3, rows_2, part_1, target, lists[3], near_to_outer, near_to_inner, from_beside = tie(
        looked_3, rows_2, part_1, target, lists[3], near_to_outer, near_to_inner, from_beside
    )

    rows_3 = exchange(looked_3)
    far = move(part_1 + moved_1, middle)
    spread_2 = spread_of(jnp.where(outer, near_to_outer, near_to_inner))
    part_2 = blend(spread_2, rows_2)
    moved_2 = move(part_2, inwards)
    part_2, lists[3], from_beside = tie(part_2, lists[3], from_beside)
    looked_4 = gather(lists[3], gauss_rows)
    spread_3 = spread_of(from_beside)
    looked_4, rows_3, far, spread_3, packed = tie(looked_4, rows_3, far, spread_3, packed)

    rows_4 = exchange(looked_4)
    part_3 = blend(spread_3, rows_3, (far,))
    beside_part = move(part_3, beside)
    part_2, moved_2, part_3, packed = tie(part_2, moved_2, part_3, packed)
    middle_part = move(part_2 + moved_2, middle)
    spread_4 = spread_of(packed)
    color, diff = blend(spread_4, rows_4, (beside_part, middle_part), place, target.reshape(n_tile, -1, feat))
    spreads = (spread_1, spread_2, spread_3, spread_4)

    diff_beside = move(diff, beside)
    diff_middle = move(diff, middle)
    far_middle = move(diff_beside, middle)
    diff_out = move(diff_middle, outwards)
    far_out = move(far_middle, outwards)
    back = []
    for n, diffs in ((3, (diff,)), (2, (diff_beside,)), (1, (diff_middle, diff_out)), (0, (far_middle, far_out))):
        term = terms(spreads[n], *diffs)
        if back:
            term, back[-1] = lax.optimization_barrier((term, back[-1]))
        back.append(exchange(term))
    grad = add_rows([lists[3], lists[2], lists[1]], back[:3], held)
    grad = add_rows([lists[0]], back[3:], held, grad)
    return (color.reshape(group_views, strip_tiles, cells, feat), grad)


def solution(mesh):
    placed = (
        P(("img", "tile"), None, None, None),
        P(),
        P(),
        P(),
        P(),
        P(),
        P(),
        P(),
        P(),
        P(),
        P(("img", "tile"), None),
        P("img", "tile", None),
        P("img", "tile", None, None),
    )
    return jax.shard_map(
        on_device,
        mesh=mesh,
        in_specs=placed,
        out_specs=(P("img", "tile", None, None), P(("img", "tile"), None)),
        check_vma=False,
    )
```

```python
import functools

import jax
import jax.numpy as jnp
from jax import lax
from jax.experimental import pallas as pl
from jax.experimental.pallas import tpu as pltpu
from jax.sharding import PartitionSpec as P

F32 = jnp.float32
BF16 = jnp.bfloat16
I32 = jnp.int32
VMEM_BYTES = 50 * 1024 * 1024
LANES = (((1,), (1,)), ((), ()))
ROWS = (((0,), (0,)), ((), ()))


def params():
    return pltpu.CompilerParams(vmem_limit_bytes=VMEM_BYTES)


def index_kernel(peers, cap, rows_held, ids_ref, req_ref, own_ref, rank_ref):
    tiles, length = ids_ref.shape
    earlier = lax.broadcasted_iota(I32, (length, length), 0)
    later = lax.broadcasted_iota(I32, (length, length), 1)
    upper = (earlier < later).astype(BF16)
    every = jnp.ones((length, length), BF16)
    peer_id = lax.broadcasted_iota(I32, (peers, length), 0)
    slot_id = lax.broadcasted_iota(I32, (cap, length), 0)
    hots = []
    for t in range(tiles):
        owner = ids_ref[t : t + 1, :] // rows_held
        own_ref[t : t + 1, :] = owner.astype(F32).astype(BF16)
        hots.append((jnp.broadcast_to(owner, (peers, length)) == peer_id).astype(F32))
    stack = jnp.concatenate(hots, 0).astype(BF16)
    within = jnp.dot(stack, upper, preferred_element_type=F32)
    totals = jnp.dot(stack, every, preferred_element_type=F32)
    offset = jnp.zeros((peers, length), F32)
    found = jnp.zeros((2 * peers, cap), F32)
    for t in range(tiles):
        own_rows = slice(t * peers, (t + 1) * peers)
        rank = jnp.sum(hots[t] * (within[own_rows] + offset), axis=0, keepdims=True).astype(I32)
        offset = offset + totals[own_rows]
        rank_ref[t : t + 1, :] = rank.astype(F32).astype(BF16)
        ids = ids_ref[t : t + 1, :]
        row = ids - (ids // rows_held) * rows_held + 1
        high = (row >> 6).astype(F32)
        low = (row & 63).astype(F32)
        digits = jnp.concatenate([hots[t] * high, hots[t] * low], 0).astype(BF16)
        slots = (jnp.broadcast_to(rank, (cap, length)) == slot_id).astype(F32).astype(BF16)
        found = found + lax.dot_general(digits, slots, LANES, preferred_element_type=F32)
    req_ref[...] = (found[:peers] * 64.0 + found[peers:]).astype(I32) - 1


def index(ids, peers, cap, rows_held):
    like = jax.ShapeDtypeStruct(ids.shape, BF16)
    return pl.pallas_call(
        functools.partial(index_kernel, peers, cap, rows_held),
        out_shape=(jax.ShapeDtypeStruct((peers, cap), I32), like, like),
        compiler_params=params(),
        cost_estimate=pl.CostEstimate(flops=10**9, bytes_accessed=10**7, transcendentals=0),
        name="index",
    )(ids)


def weights_kernel(alpha_ref, out_ref):
    alpha = alpha_ref[...]
    length = alpha.shape[1]
    logs = jnp.log1p(-alpha)
    earlier = lax.broadcasted_iota(I32, (length, length), 0)
    later = lax.broadcasted_iota(I32, (length, length), 1)
    upper = (earlier < later).astype(F32)
    before = jnp.dot(logs, upper, preferred_element_type=F32, precision=lax.Precision.HIGHEST)
    out_ref[...] = (alpha * jnp.exp(before)).astype(BF16)


def weights(alphas):
    return pl.pallas_call(
        weights_kernel,
        out_shape=jax.ShapeDtypeStruct(alphas.shape, BF16),
        compiler_params=params(),
        cost_estimate=pl.CostEstimate(flops=10**8, bytes_accessed=10**6, transcendentals=0),
        name="weights",
    )(alphas)


def spread_kernel(near, cap, packs, base_ref, *refs):
    out_ref = refs[-1]
    own_all, rank_all, weight_all = (sum(ref[...].astype(F32) for ref in refs[k : 3 * packs : 3]) for k in range(3))
    tiles, length = own_all.shape
    cells = weight_all.shape[0] // tiles
    slot_id = lax.broadcasted_iota(I32, (cap, length), 0)
    for t in range(tiles):
        own = own_all[t : t + 1, :].astype(I32)
        rank = rank_all[t : t + 1, :].astype(I32)
        here = slice(t * cells, (t + 1) * cells)
        weight = weight_all[here, :]
        by_owner = [jnp.where(own == base_ref[o], weight, 0.0) for o in range(near)]
        slots = (jnp.broadcast_to(rank, (cap, length)) == slot_id).astype(F32).astype(BF16)
        moved = lax.dot_general(
            jnp.concatenate(by_owner, 0).astype(BF16), slots, LANES, preferred_element_type=F32
        ).astype(BF16)
        if cap % 128 == 0:
            for o in range(near):
                out_ref[here, o * cap : (o + 1) * cap] = moved[o * cells : (o + 1) * cells]
        else:
            out_ref[here, :] = jnp.concatenate([moved[o * cells : (o + 1) * cells] for o in range(near)], 1)


def spread(owners, packs, tiles, cells, cap):
    length = packs[0].shape[1]
    near = owners.shape[0]
    step = 16
    first = tiles * cells // step
    specs = [
        pl.BlockSpec((step, length), lambda t: (first + t, 0)),
        pl.BlockSpec((step, length), lambda t: (first + tiles // step + t, 0)),
        pl.BlockSpec((step * cells, length), lambda t: (t, 0)),
    ]
    return pl.pallas_call(
        functools.partial(spread_kernel, near, cap, len(packs)),
        grid=(tiles // step,),
        in_specs=[pl.BlockSpec(memory_space=pltpu.SMEM)] + specs * len(packs),
        out_specs=pl.BlockSpec((step * cells, near * cap), lambda t: (t, 0)),
        out_shape=jax.ShapeDtypeStruct((tiles * cells, near * cap), BF16),
        compiler_params=params(),
        cost_estimate=pl.CostEstimate(flops=10**8, bytes_accessed=10**6, transcendentals=0),
        name="spread",
    )(owners, *[pack for pack in packs for _ in range(3)])


def gather_kernel(group, cap, asked_ref, rows_ref, out_ref):
    first = pl.program_id(0) * group
    asked = asked_ref[...]
    peer = lax.broadcasted_iota(I32, asked.shape, 1)
    held = rows_ref.shape[0]
    row_id = lax.broadcasted_iota(I32, (cap, held), 1)
    picks = []
    for q in range(group):
        column = jnp.sum(jnp.where(peer == first + q, asked, 0), axis=1, keepdims=True)
        picks.append((jnp.broadcast_to(column, (cap, held)) == row_id).astype(F32).astype(BF16))
    pick = jnp.concatenate(picks, 0)
    out_ref[...] = jnp.dot(pick, rows_ref[...], preferred_element_type=F32).astype(BF16)


def gather(asked, rows):
    near, cap = asked.shape
    held, feat = rows.shape
    group = max(1, min(near, 1024 // cap))
    return pl.pallas_call(
        functools.partial(gather_kernel, group, cap),
        grid=(near // group,),
        in_specs=[pl.BlockSpec((cap, near), lambda i: (0, 0)), pl.BlockSpec((held, feat), lambda i: (0, 0))],
        out_specs=pl.BlockSpec((group * cap, feat), lambda i: (i, 0)),
        out_shape=jax.ShapeDtypeStruct((near * cap, feat), BF16),
        compiler_params=params(),
        cost_estimate=pl.CostEstimate(flops=10**8, bytes_accessed=10**6, transcendentals=0),
        name="gather",
    )(asked.T, rows)


def blend_kernel(n_parts, weight_ref, rows_ref, *rest):
    color = jnp.dot(weight_ref[...], rows_ref[...], preferred_element_type=F32)
    for part_ref in rest[:n_parts]:
        color = color + part_ref[...].astype(F32)
    rest[n_parts][...] = color.astype(BF16)


def last_blend_kernel(n_parts, place_ref, weight_ref, rows_ref, *rest):
    parts, target_ref = rest[:n_parts], rest[n_parts]
    color_ref, diff_ref = rest[-2:]
    color = jnp.dot(weight_ref[...], rows_ref[...], preferred_element_type=F32)
    for part_ref in parts:
        color = color + part_ref[...].astype(F32)
    color_ref[...] = color.astype(BF16)
    cells = target_ref.shape[1]
    per_step = color.shape[0] // cells
    for k in range(per_step):
        at = place_ref[pl.program_id(0) * per_step + k]
        here = slice(k * cells, (k + 1) * cells)
        diff_ref[here, :] = (color[here] - target_ref[at].astype(F32)).astype(BF16)


def blend(weight, rows, parts=(), place=None, target=None):
    cells, slots = weight.shape
    feat = rows.shape[1]
    block = min(cells, 256)
    cell_block = pl.BlockSpec((block, feat), lambda i: (i, 0))
    out = jax.ShapeDtypeStruct((cells, feat), BF16)
    last = place is not None
    in_specs = [pl.BlockSpec((block, slots), lambda i: (i, 0)), pl.BlockSpec((slots, feat), lambda i: (0, 0))]
    in_specs += [cell_block] * len(parts)
    args = [weight, rows, *parts]
    if last:
        in_specs = [pl.BlockSpec(memory_space=pltpu.SMEM)] + in_specs + [pl.BlockSpec(target.shape, lambda i: (0, 0, 0))]
        args = [place, *args, target]
    return pl.pallas_call(
        functools.partial(last_blend_kernel if last else blend_kernel, len(parts)),
        grid=(cells // block,),
        in_specs=in_specs,
        out_specs=(cell_block, cell_block) if last else cell_block,
        out_shape=(out, out) if last else out,
        compiler_params=params(),
        cost_estimate=pl.CostEstimate(flops=4 * 10**9, bytes_accessed=10**7, transcendentals=0),
        name="blend",
    )(*args)


def terms_kernel(weight_ref, *refs):
    diff = refs[0][...]
    for more_ref in refs[1:-1]:
        diff = diff + more_ref[...]
    refs[-1][...] = lax.dot_general(weight_ref[...], diff, ROWS, preferred_element_type=F32).astype(BF16)


def terms(weight, *diffs):
    cells, slots = weight.shape
    feat = diffs[0].shape[1]
    block = min(slots, 1024)
    return pl.pallas_call(
        terms_kernel,
        grid=(slots // block,),
        in_specs=[pl.BlockSpec((cells, block), lambda i: (0, i))]
        + [pl.BlockSpec((cells, feat), lambda i: (0, 0))] * len(diffs),
        out_specs=pl.BlockSpec((block, feat), lambda i: (i, 0)),
        out_shape=jax.ShapeDtypeStruct((slots, feat), BF16),
        compiler_params=params(),
        cost_estimate=pl.CostEstimate(flops=10**11, bytes_accessed=10**7, transcendentals=0),
        name="terms",
    )(weight, *diffs)


def add_rows_kernel(count, *refs):
    out_ref = refs[-1]
    block = out_ref.shape[0]
    total = None if len(refs) == 2 * count + 1 else refs[2 * count][...]
    for n in range(count):
        asked_ref, terms_ref = refs[n], refs[count + n]
        near, cap = asked_ref.shape
        row_id = lax.broadcasted_iota(I32, (block, cap), 0) + pl.program_id(0) * block
        picks = []
        for o in range(near):
            asked = jnp.broadcast_to(asked_ref[o : o + 1, :], (block, cap))
            picks.append((asked == row_id).astype(F32).astype(BF16))
        got = jnp.dot(jnp.concatenate(picks, 1), terms_ref[...], preferred_element_type=F32)
        total = got if total is None else total + got
    out_ref[...] = total


def add_rows(askeds, arrivals, held, before=None):
    near, cap = askeds[0].shape
    feat = arrivals[0].shape[1]
    count = len(askeds)
    block = min(held, 512)
    row_block = pl.BlockSpec((block, feat), lambda i: (i, 0))
    more = before is not None
    in_specs = [pl.BlockSpec((near, cap), lambda i: (0, 0))] * count
    in_specs += [pl.BlockSpec((near * cap, feat), lambda i: (0, 0))] * count
    return pl.pallas_call(
        functools.partial(add_rows_kernel, count),
        grid=(held // block,),
        in_specs=in_specs + [row_block] * more,
        out_specs=row_block,
        out_shape=jax.ShapeDtypeStruct((held, feat), F32),
        compiler_params=params(),
        cost_estimate=pl.CostEstimate(flops=5 * count * 10**9, bytes_accessed=10**7, transcendentals=0),
        name="add_rows",
    )(*askeds, *arrivals, *((before,) if more else ()))


def layer_norm(rows, gain, bias):
    mean = jnp.mean(rows, axis=-1, keepdims=True)
    centred = rows - mean
    var = jnp.mean(centred * centred, axis=-1, keepdims=True)
    return centred * lax.rsqrt(var + 1e-05) * gain + bias


def encode_kernel(strips, *refs):
    gain, bias, up, up_bias, down, down_bias, last_gain, last_bias, head = refs[strips:-1]
    out_ref = refs[-1]
    hidden = up.shape[1]
    step = 768 if hidden % 768 == 0 else hidden
    group = max(1, strips // 2)
    for first in range(0, strips, group):
        wide = jnp.concatenate([ref[...] for ref in refs[first : first + group]], 0).astype(F32)
        normed = layer_norm(wide, gain[...], bias[...]).astype(BF16)
        block_out = wide + down_bias[...]
        for k in range(0, hidden, step):
            inner = jnp.dot(normed, up[:, k : k + step], preferred_element_type=F32) + up_bias[k : k + step]
            act = (inner * jax.nn.sigmoid(1.702 * inner)).astype(BF16)
            block_out = block_out + jnp.dot(act, down[k : k + step, :], preferred_element_type=F32)
        final = layer_norm(block_out, last_gain[...], last_bias[...]).astype(BF16)
        embed = jnp.dot(final, head[...], preferred_element_type=F32)
        scale = lax.rsqrt(jnp.mean(embed * embed, axis=-1, keepdims=True) + 1e-06)
        target = (embed * scale).astype(BF16)
        cells = target.shape[0] // group
        for n in range(group):
            out_ref[first + n] = target[n * cells : (n + 1) * cells]


def encode(strips, *weights_and_biases):
    cells = strips[0].shape[0]
    return pl.pallas_call(
        functools.partial(encode_kernel, len(strips)),
        out_shape=jax.ShapeDtypeStruct((len(strips), cells, weights_and_biases[-1].shape[1]), BF16),
        compiler_params=params(),
        cost_estimate=pl.CostEstimate(flops=10**11, bytes_accessed=10**7, transcendentals=0),
        name="encode",
    )(*strips, *weights_and_biases)


def on_device(
    patches,
    norm_gain,
    norm_bias,
    up_weight,
    up_bias,
    down_weight,
    down_bias,
    final_gain,
    final_bias,
    head_weight,
    gauss_rows,
    tile_lists,
    alphas,
):
    view_count, tiles_view, cells, width = patches.shape
    feat = head_weight.shape[1]
    n_img = lax.axis_size("img")
    n_tile = lax.axis_size("tile")
    peers = n_img * n_tile
    both = ("img", "tile")
    held = gauss_rows.shape[0]
    group_views, strip_tiles, list_len = tile_lists.shape
    tiles = group_views * strip_tiles
    cap = 2 * tiles * list_len // peers

    wide_layer = n_tile // 4
    near = n_img * wide_layer
    tile = lax.axis_index("tile")
    layer = tile // wide_layer
    low = layer < 2
    groups = [[i * n_tile + z * wide_layer + k for i in range(n_img) for k in range(wide_layer)] for z in range(4)]

    def moves(*pairs):
        return [(a * wide_layer + k, b * wide_layer + k) for a, b in pairs for k in range(wide_layer)]

    beside = moves((0, 1), (1, 0), (2, 3), (3, 2))
    middle = moves((1, 2), (2, 1))
    inwards = moves((0, 1), (3, 2))
    outwards = moves((1, 0), (2, 3))

    def move(x, pairs):
        return lax.ppermute(x, "tile", pairs)

    def exchange(x):
        return lax.all_to_all(x, both, split_axis=0, concat_axis=0, axis_index_groups=groups, tiled=True)

    def tie(*values):
        return lax.optimization_barrier(values)

    request, own, rank = index(tile_lists.reshape(tiles, list_len), peers, cap, held)
    weight = weights(alphas.reshape(tiles * cells, list_len))
    packed = jnp.concatenate([weight, own, rank], 0)
    request, patches = tie(request, patches)
    asked = lax.all_to_all(request, both, split_axis=0, concat_axis=0, tiled=True)
    chips = n_tile // 2
    core = tile % 2
    chip = tile // 2
    patches = patches.reshape(chips, 2, -1, width)
    others = lax.dynamic_index_in_dim(patches, 1 - core, 1, keepdims=False)
    others = move(others, [(a, a ^ 1) for a in range(n_tile)])
    asked, others, packed = tie(asked, others, packed)
    far_to_outer = move(packed, moves((0, 3), (3, 0)))
    far_to_inner = move(packed, moves((0, 2), (3, 1)))
    pairs = jnp.concatenate([lax.dynamic_index_in_dim(patches, core, 1, keepdims=False), others], 1)
    strips = []
    for n in range(chips):
        pair = lax.dynamic_index_in_dim(pairs, lax.rem(chip + n, chips), 0, keepdims=False)
        strips.append(move(pair, [(a, (a + 2 * n) % n_tile) for a in range(n_tile)]) if n else pair)
    view = jnp.arange(n_tile, dtype=I32)
    place = lax.rem(chip + chips - view // 2, chips) * 2 + (view % 2 != core).astype(I32)
    asked = asked.reshape(n_img, 4, wide_layer, cap)
    sets = (jnp.where(low, 3, 0), jnp.where(low, 2, 1), layer ^ 1, layer)
    lists = [lax.dynamic_index_in_dim(asked, s, 1, keepdims=False).reshape(near, cap) for s in sets]
    owners = (
        jnp.arange(n_img, dtype=I32)[:, None] * n_tile
        + layer * wide_layer
        + jnp.arange(wide_layer, dtype=I32)[None, :]
    ).reshape(near)

    def spread_of(*packs):
        return spread(owners, packs, tiles, cells, cap)

    looked, lists[1] = tie(gather(lists[0], gauss_rows), lists[1])
    rows_1 = exchange(looked)
    looked_2 = gather(lists[1], gauss_rows)
    looked_2, lists[2] = tie(looked_2, lists[2])
    spread_1 = spread_of(far_to_outer, far_to_inner)
    looked_3 = gather(lists[2], gauss_rows)
    looked_2, looked_3, spread_1, rows_1, packed = tie(looked_2, looked_3, spread_1, rows_1, packed)

    rows_2 = exchange(looked_2)
    part_1 = blend(spread_1, rows_1)
    moved_1 = move(part_1, inwards)
    near_to_outer = move(packed, moves((1, 3), (2, 0)))
    near_to_inner = move(packed, middle)
    from_beside = move(packed, beside)
    part_1, *strips = tie(part_1, *strips)
    target = encode(
        strips, norm_gain, norm_bias, up_weight, up_bias, down_weight, down_bias, final_gain, final_bias, head_weight
    )
    looked_3, rows_2, part_1, target, lists[3], near_to_outer, near_to_inner, from_beside = tie(
        looked_3, rows_2, part_1, target, lists[3], near_to_outer, near_to_inner, from_beside
    )

    rows_3 = exchange(looked_3)
    far = move(part_1 + moved_1, middle)
    spread_2 = spread_of(near_to_outer, near_to_inner)
    part_2 = blend(spread_2, rows_2)
    moved_2 = move(part_2, inwards)
    part_2, lists[3], from_beside = tie(part_2, lists[3], from_beside)
    looked_4 = gather(lists[3], gauss_rows)
    spread_3 = spread_of(from_beside)
    looked_4, rows_3, far, spread_3, packed = tie(looked_4, rows_3, far, spread_3, packed)

    rows_4 = exchange(looked_4)
    part_3 = blend(spread_3, rows_3, (far,))
    beside_part = move(part_3, beside)
    part_2, moved_2, part_3, packed = tie(part_2, moved_2, part_3, packed)
    middle_part = move(part_2 + moved_2, middle)
    spread_4 = spread_of(packed)
    color, diff = blend(spread_4, rows_4, (beside_part, middle_part), place, target.reshape(n_tile, -1, feat))
    spreads = (spread_1, spread_2, spread_3, spread_4)

    diff_beside = move(diff, beside)
    diff_middle = move(diff, middle)
    far_middle = move(diff_beside, middle)
    diff_out = move(diff_middle, outwards)
    far_out = move(far_middle, outwards)
    back = []
    for n, diffs in ((3, (diff,)), (2, (diff_beside,)), (1, (diff_middle, diff_out)), (0, (far_middle, far_out))):
        term = terms(spreads[n], *diffs)
        if back:
            term, back[-1] = lax.optimization_barrier((term, back[-1]))
        back.append(exchange(term))
    grad = add_rows([lists[3], lists[2], lists[1]], back[:3], held)
    grad = add_rows([lists[0]], back[3:], held, grad)
    return (color.reshape(group_views, strip_tiles, cells, feat), grad)


def solution(mesh):
    placed = (
        P(("img", "tile"), None, None, None),
        P(),
        P(),
        P(),
        P(),
        P(),
        P(),
        P(),
        P(),
        P(),
        P(("img", "tile"), None),
        P("img", "tile", None),
        P("img", "tile", None, None),
    )
    return jax.shard_map(
        on_device,
        mesh=mesh,
        in_specs=placed,
        out_specs=(P("img", "tile", None, None), P(("img", "tile"), None)),
        check_vma=False,
    )
```

```python
import functools

import jax
import jax.numpy as jnp
from jax import lax
from jax.experimental import pallas as pl
from jax.experimental.pallas import tpu as pltpu
from jax.sharding import PartitionSpec as P

F32 = jnp.float32
BF16 = jnp.bfloat16
I32 = jnp.int32
VMEM_BYTES = 50 * 1024 * 1024
LANES = (((1,), (1,)), ((), ()))
ROWS = (((0,), (0,)), ((), ()))


def params():
    return pltpu.CompilerParams(vmem_limit_bytes=VMEM_BYTES)


def index_kernel(peers, cap, rows_held, ids_ref, req_ref, own_ref, rank_ref):
    tiles, length = ids_ref.shape
    earlier = lax.broadcasted_iota(I32, (length, length), 0)
    later = lax.broadcasted_iota(I32, (length, length), 1)
    upper = (earlier < later).astype(BF16)
    every = jnp.ones((length, length), BF16)
    peer_id = lax.broadcasted_iota(I32, (peers, length), 0)
    slot_id = lax.broadcasted_iota(I32, (cap, length), 0)
    hots = []
    for t in range(tiles):
        owner = ids_ref[t : t + 1, :] // rows_held
        own_ref[t : t + 1, :] = owner.astype(F32).astype(BF16)
        hots.append((jnp.broadcast_to(owner, (peers, length)) == peer_id).astype(F32))
    stack = jnp.concatenate(hots, 0).astype(BF16)
    within = jnp.dot(stack, upper, preferred_element_type=F32)
    totals = jnp.dot(stack, every, preferred_element_type=F32)
    offset = jnp.zeros((peers, length), F32)
    found = jnp.zeros((2 * peers, cap), F32)
    for t in range(tiles):
        own_rows = slice(t * peers, (t + 1) * peers)
        rank = jnp.sum(hots[t] * (within[own_rows] + offset), axis=0, keepdims=True).astype(I32)
        offset = offset + totals[own_rows]
        rank_ref[t : t + 1, :] = rank.astype(F32).astype(BF16)
        ids = ids_ref[t : t + 1, :]
        row = ids - (ids // rows_held) * rows_held + 1
        high = (row >> 6).astype(F32)
        low = (row & 63).astype(F32)
        digits = jnp.concatenate([hots[t] * high, hots[t] * low], 0).astype(BF16)
        slots = (jnp.broadcast_to(rank, (cap, length)) == slot_id).astype(F32).astype(BF16)
        found = found + lax.dot_general(digits, slots, LANES, preferred_element_type=F32)
    req_ref[...] = (found[:peers] * 64.0 + found[peers:]).astype(I32) - 1


def index(ids, peers, cap, rows_held):
    like = jax.ShapeDtypeStruct(ids.shape, BF16)
    return pl.pallas_call(
        functools.partial(index_kernel, peers, cap, rows_held),
        out_shape=(jax.ShapeDtypeStruct((peers, cap), I32), like, like),
        compiler_params=params(),
        cost_estimate=pl.CostEstimate(flops=10**9, bytes_accessed=10**7, transcendentals=0),
        name="index",
    )(ids)


def weights_kernel(alpha_ref, out_ref):
    alpha = alpha_ref[...]
    length = alpha.shape[1]
    logs = jnp.log1p(-alpha)
    earlier = lax.broadcasted_iota(I32, (length, length), 0)
    later = lax.broadcasted_iota(I32, (length, length), 1)
    upper = (earlier < later).astype(F32)
    before = jnp.dot(logs, upper, preferred_element_type=F32, precision=lax.Precision.HIGHEST)
    out_ref[...] = (alpha * jnp.exp(before)).astype(BF16)


def weights(alphas):
    return pl.pallas_call(
        weights_kernel,
        out_shape=jax.ShapeDtypeStruct(alphas.shape, BF16),
        compiler_params=params(),
        cost_estimate=pl.CostEstimate(flops=10**8, bytes_accessed=10**6, transcendentals=0),
        name="weights",
    )(alphas)


def spread_kernel(near, cap, packs, base_ref, *refs):
    out_ref = refs[-1]
    own_all, rank_all, weight_all = (sum(ref[...].astype(F32) for ref in refs[k : 3 * packs : 3]) for k in range(3))
    tiles, length = own_all.shape
    cells = weight_all.shape[0] // tiles
    slot_id = lax.broadcasted_iota(I32, (cap, length), 0)
    for t in range(tiles):
        own = own_all[t : t + 1, :].astype(I32)
        rank = rank_all[t : t + 1, :].astype(I32)
        here = slice(t * cells, (t + 1) * cells)
        weight = weight_all[here, :]
        by_owner = [jnp.where(own == base_ref[o], weight, 0.0) for o in range(near)]
        slots = (jnp.broadcast_to(rank, (cap, length)) == slot_id).astype(F32).astype(BF16)
        moved = lax.dot_general(
            jnp.concatenate(by_owner, 0).astype(BF16), slots, LANES, preferred_element_type=F32
        ).astype(BF16)
        if cap % 128 == 0:
            for o in range(near):
                out_ref[here, o * cap : (o + 1) * cap] = moved[o * cells : (o + 1) * cells]
        else:
            out_ref[here, :] = jnp.concatenate([moved[o * cells : (o + 1) * cells] for o in range(near)], 1)


def spread(owners, packs, tiles, cells, cap):
    length = packs[0].shape[1]
    near = owners.shape[0]
    step = 16
    first = tiles * cells // step
    specs = [
        pl.BlockSpec((step, length), lambda t: (first + t, 0)),
        pl.BlockSpec((step, length), lambda t: (first + tiles // step + t, 0)),
        pl.BlockSpec((step * cells, length), lambda t: (t, 0)),
    ]
    return pl.pallas_call(
        functools.partial(spread_kernel, near, cap, len(packs)),
        grid=(tiles // step,),
        in_specs=[pl.BlockSpec(memory_space=pltpu.SMEM)] + specs * len(packs),
        out_specs=pl.BlockSpec((step * cells, near * cap), lambda t: (t, 0)),
        out_shape=jax.ShapeDtypeStruct((tiles * cells, near * cap), BF16),
        compiler_params=params(),
        cost_estimate=pl.CostEstimate(flops=10**8, bytes_accessed=10**6, transcendentals=0),
        name="spread",
    )(owners, *[pack for pack in packs for _ in range(3)])


def gather_kernel(group, cap, asked_ref, rows_ref, out_ref):
    first = pl.program_id(0) * group
    asked = asked_ref[...]
    peer = lax.broadcasted_iota(I32, asked.shape, 1)
    held = rows_ref.shape[0]
    row_id = lax.broadcasted_iota(I32, (cap, held), 1)
    picks = []
    for q in range(group):
        column = jnp.sum(jnp.where(peer == first + q, asked, 0), axis=1, keepdims=True)
        picks.append((jnp.broadcast_to(column, (cap, held)) == row_id).astype(F32).astype(BF16))
    pick = jnp.concatenate(picks, 0)
    out_ref[...] = jnp.dot(pick, rows_ref[...], preferred_element_type=F32).astype(BF16)


def gather(asked, rows, flops=10**8):
    near, cap = asked.shape
    held, feat = rows.shape
    group = max(1, min(near, 1024 // cap))
    return pl.pallas_call(
        functools.partial(gather_kernel, group, cap),
        grid=(near // group,),
        in_specs=[pl.BlockSpec((cap, near), lambda i: (0, 0)), pl.BlockSpec((held, feat), lambda i: (0, 0))],
        out_specs=pl.BlockSpec((group * cap, feat), lambda i: (i, 0)),
        out_shape=jax.ShapeDtypeStruct((near * cap, feat), BF16),
        compiler_params=params(),
        cost_estimate=pl.CostEstimate(flops=flops, bytes_accessed=10**6, transcendentals=0),
        name="gather",
    )(asked.T, rows)


def blend_kernel(n_parts, weight_ref, rows_ref, *rest):
    color = jnp.dot(weight_ref[...], rows_ref[...], preferred_element_type=F32)
    for part_ref in rest[:n_parts]:
        color = color + part_ref[...].astype(F32)
    rest[n_parts][...] = color.astype(BF16)


def last_blend_kernel(n_parts, place_ref, weight_ref, rows_ref, *rest):
    parts, target_ref = rest[:n_parts], rest[n_parts]
    color_ref, diff_ref = rest[-2:]
    color = jnp.dot(weight_ref[...], rows_ref[...], preferred_element_type=F32)
    for part_ref in parts:
        color = color + part_ref[...].astype(F32)
    color_ref[...] = color.astype(BF16)
    cells = target_ref.shape[1]
    per_step = color.shape[0] // cells
    for k in range(per_step):
        at = place_ref[pl.program_id(0) * per_step + k]
        here = slice(k * cells, (k + 1) * cells)
        diff_ref[here, :] = (color[here] - target_ref[at].astype(F32)).astype(BF16)


def blend(weight, rows, parts=(), place=None, target=None):
    cells, slots = weight.shape
    feat = rows.shape[1]
    block = min(cells, 256)
    cell_block = pl.BlockSpec((block, feat), lambda i: (i, 0))
    out = jax.ShapeDtypeStruct((cells, feat), BF16)
    last = place is not None
    in_specs = [pl.BlockSpec((block, slots), lambda i: (i, 0)), pl.BlockSpec((slots, feat), lambda i: (0, 0))]
    in_specs += [cell_block] * len(parts)
    args = [weight, rows, *parts]
    if last:
        in_specs = [pl.BlockSpec(memory_space=pltpu.SMEM)] + in_specs + [pl.BlockSpec(target.shape, lambda i: (0, 0, 0))]
        args = [place, *args, target]
    return pl.pallas_call(
        functools.partial(last_blend_kernel if last else blend_kernel, len(parts)),
        grid=(cells // block,),
        in_specs=in_specs,
        out_specs=(cell_block, cell_block) if last else cell_block,
        out_shape=(out, out) if last else out,
        compiler_params=params(),
        cost_estimate=pl.CostEstimate(flops=4 * 10**9, bytes_accessed=10**7, transcendentals=0),
        name="blend",
    )(*args)


def terms_kernel(weight_ref, *refs):
    diff = refs[0][...]
    for more_ref in refs[1:-1]:
        diff = diff + more_ref[...]
    refs[-1][...] = lax.dot_general(weight_ref[...], diff, ROWS, preferred_element_type=F32).astype(BF16)


def terms(weight, *diffs):
    cells, slots = weight.shape
    feat = diffs[0].shape[1]
    block = min(slots, 1024)
    return pl.pallas_call(
        terms_kernel,
        grid=(slots // block,),
        in_specs=[pl.BlockSpec((cells, block), lambda i: (0, i))]
        + [pl.BlockSpec((cells, feat), lambda i: (0, 0))] * len(diffs),
        out_specs=pl.BlockSpec((block, feat), lambda i: (i, 0)),
        out_shape=jax.ShapeDtypeStruct((slots, feat), BF16),
        compiler_params=params(),
        cost_estimate=pl.CostEstimate(flops=10**11, bytes_accessed=10**7, transcendentals=0),
        name="terms",
    )(weight, *diffs)


def add_rows_kernel(count, *refs):
    out_ref = refs[-1]
    block = out_ref.shape[0]
    total = None if len(refs) == 2 * count + 1 else refs[2 * count][...]
    for n in range(count):
        asked_ref, terms_ref = refs[n], refs[count + n]
        near, cap = asked_ref.shape
        row_id = lax.broadcasted_iota(I32, (block, cap), 0) + pl.program_id(0) * block
        picks = []
        for o in range(near):
            asked = jnp.broadcast_to(asked_ref[o : o + 1, :], (block, cap))
            picks.append((asked == row_id).astype(F32).astype(BF16))
        got = jnp.dot(jnp.concatenate(picks, 1), terms_ref[...], preferred_element_type=F32)
        total = got if total is None else total + got
    out_ref[...] = total


def add_rows(askeds, arrivals, held, before=None):
    near, cap = askeds[0].shape
    feat = arrivals[0].shape[1]
    count = len(askeds)
    block = min(held, 512)
    row_block = pl.BlockSpec((block, feat), lambda i: (i, 0))
    more = before is not None
    in_specs = [pl.BlockSpec((near, cap), lambda i: (0, 0))] * count
    in_specs += [pl.BlockSpec((near * cap, feat), lambda i: (0, 0))] * count
    return pl.pallas_call(
        functools.partial(add_rows_kernel, count),
        grid=(held // block,),
        in_specs=in_specs + [row_block] * more,
        out_specs=row_block,
        out_shape=jax.ShapeDtypeStruct((held, feat), F32),
        compiler_params=params(),
        cost_estimate=pl.CostEstimate(flops=5 * count * 10**9, bytes_accessed=10**7, transcendentals=0),
        name="add_rows",
    )(*askeds, *arrivals, *((before,) if more else ()))


def layer_norm(rows, gain, bias):
    mean = jnp.mean(rows, axis=-1, keepdims=True)
    centred = rows - mean
    var = jnp.mean(centred * centred, axis=-1, keepdims=True)
    return centred * lax.rsqrt(var + 1e-05) * gain + bias


def encode_kernel(strips, *refs):
    gain, bias, up, up_bias, down, down_bias, last_gain, last_bias, head = refs[strips:-1]
    out_ref = refs[-1]
    hidden = up.shape[1]
    step = 768 if hidden % 768 == 0 else hidden
    group = max(1, strips // 2)
    for first in range(0, strips, group):
        wide = jnp.concatenate([ref[...] for ref in refs[first : first + group]], 0).astype(F32)
        normed = layer_norm(wide, gain[...], bias[...]).astype(BF16)
        block_out = wide + down_bias[...]
        for k in range(0, hidden, step):
            inner = jnp.dot(normed, up[:, k : k + step], preferred_element_type=F32) + up_bias[k : k + step]
            act = (inner * jax.nn.sigmoid(1.702 * inner)).astype(BF16)
            block_out = block_out + jnp.dot(act, down[k : k + step, :], preferred_element_type=F32)
        final = layer_norm(block_out, last_gain[...], last_bias[...]).astype(BF16)
        embed = jnp.dot(final, head[...], preferred_element_type=F32)
        scale = lax.rsqrt(jnp.mean(embed * embed, axis=-1, keepdims=True) + 1e-06)
        target = (embed * scale).astype(BF16)
        cells = target.shape[0] // group
        for n in range(group):
            out_ref[first + n] = target[n * cells : (n + 1) * cells]


def encode(strips, *weights_and_biases):
    cells = strips[0].shape[0]
    return pl.pallas_call(
        functools.partial(encode_kernel, len(strips)),
        out_shape=jax.ShapeDtypeStruct((len(strips), cells, weights_and_biases[-1].shape[1]), BF16),
        compiler_params=params(),
        cost_estimate=pl.CostEstimate(flops=15 * 10**9, bytes_accessed=10**7, transcendentals=0),
        name="encode",
    )(*strips, *weights_and_biases)


def on_device(
    patches,
    norm_gain,
    norm_bias,
    up_weight,
    up_bias,
    down_weight,
    down_bias,
    final_gain,
    final_bias,
    head_weight,
    gauss_rows,
    tile_lists,
    alphas,
):
    view_count, tiles_view, cells, width = patches.shape
    feat = head_weight.shape[1]
    n_img = lax.axis_size("img")
    n_tile = lax.axis_size("tile")
    peers = n_img * n_tile
    both = ("img", "tile")
    held = gauss_rows.shape[0]
    group_views, strip_tiles, list_len = tile_lists.shape
    tiles = group_views * strip_tiles
    cap = 2 * tiles * list_len // peers

    wide_layer = n_tile // 4
    near = n_img * wide_layer
    tile = lax.axis_index("tile")
    layer = tile // wide_layer
    low = layer < 2
    groups = [[i * n_tile + z * wide_layer + k for i in range(n_img) for k in range(wide_layer)] for z in range(4)]

    def moves(*pairs):
        return [(a * wide_layer + k, b * wide_layer + k) for a, b in pairs for k in range(wide_layer)]

    beside = moves((0, 1), (1, 0), (2, 3), (3, 2))
    middle = moves((1, 2), (2, 1))
    inwards = moves((0, 1), (3, 2))
    outwards = moves((1, 0), (2, 3))

    def move(x, pairs):
        return lax.ppermute(x, "tile", pairs)

    def exchange(x):
        return lax.all_to_all(x, both, split_axis=0, concat_axis=0, axis_index_groups=groups, tiled=True)

    def tie(*values):
        return lax.optimization_barrier(values)

    request, own, rank = index(tile_lists.reshape(tiles, list_len), peers, cap, held)
    weight = weights(alphas.reshape(tiles * cells, list_len))
    packed = jnp.concatenate([weight, own, rank], 0)
    request, patches = tie(request, patches)
    asked = lax.all_to_all(request, both, split_axis=0, concat_axis=0, tiled=True)
    chips = n_tile // 2
    core = tile % 2
    chip = tile // 2
    patches = patches.reshape(chips, 2, -1, width)
    others = lax.dynamic_index_in_dim(patches, 1 - core, 1, keepdims=False)
    others = move(others, [(a, a ^ 1) for a in range(n_tile)])
    asked, others, packed = tie(asked, others, packed)
    far_to_outer = move(packed, moves((0, 3), (3, 0)))
    far_to_inner = move(packed, moves((0, 2), (3, 1)))
    pairs = jnp.concatenate([lax.dynamic_index_in_dim(patches, core, 1, keepdims=False), others], 1)
    strips = []
    for n in range(chips):
        pair = lax.dynamic_index_in_dim(pairs, lax.rem(chip + n, chips), 0, keepdims=False)
        strips.append(move(pair, [(a, (a + 2 * n) % n_tile) for a in range(n_tile)]) if n else pair)
    view = jnp.arange(n_tile, dtype=I32)
    place = lax.rem(chip + chips - view // 2, chips) * 2 + (view % 2 != core).astype(I32)
    asked = asked.reshape(n_img, 4, wide_layer, cap)
    sets = (jnp.where(low, 3, 0), jnp.where(low, 2, 1), layer ^ 1, layer)
    lists = [lax.dynamic_index_in_dim(asked, s, 1, keepdims=False).reshape(near, cap) for s in sets]
    owners = (
        jnp.arange(n_img, dtype=I32)[:, None] * n_tile
        + layer * wide_layer
        + jnp.arange(wide_layer, dtype=I32)[None, :]
    ).reshape(near)

    def spread_of(*packs):
        return spread(owners, packs, tiles, cells, cap)

    looked, lists[1] = tie(gather(lists[0], gauss_rows), lists[1])
    rows_1 = exchange(looked)
    looked_2 = gather(lists[1], gauss_rows)
    spread_1 = spread_of(far_to_outer, far_to_inner)
    looked_2, spread_1, rows_1, packed, lists[2], *strips[1::2] = tie(
        looked_2, spread_1, rows_1, packed, lists[2], *strips[1::2]
    )

    rows_2 = exchange(looked_2)
    part_1 = blend(spread_1, rows_1)
    moved_1 = move(part_1, inwards)
    near_to_outer = move(packed, moves((1, 3), (2, 0)))
    near_to_inner = move(packed, middle)
    from_beside = move(packed, beside)
    part_1, lists[2], *strips = tie(part_1, lists[2], *strips)
    looked_3 = gather(lists[2], gauss_rows, 15 * 10**9)
    spread_2 = spread_of(near_to_outer, near_to_inner)
    looked_3, rows_2, part_1, lists[3], spread_2, from_beside = tie(
        looked_3, rows_2, part_1, lists[3], spread_2, from_beside
    )

    rows_3 = exchange(looked_3)
    far = move(part_1 + moved_1, middle)
    part_2 = blend(spread_2, rows_2)
    moved_2 = move(part_2, inwards)
    part_2, lists[3], from_beside = tie(part_2, lists[3], from_beside)
    looked_4 = gather(lists[3], gauss_rows)
    spread_3 = spread_of(from_beside)
    looked_4, rows_3, far, spread_3, packed = tie(looked_4, rows_3, far, spread_3, packed)

    rows_4 = exchange(looked_4)
    part_3 = blend(spread_3, rows_3, (far,))
    beside_part = move(part_3, beside)
    part_2, moved_2, part_3, packed, *strips = tie(part_2, moved_2, part_3, packed, *strips)
    middle_part = move(part_2 + moved_2, middle)
    spread_4 = spread_of(packed)
    target = encode(
        strips, norm_gain, norm_bias, up_weight, up_bias, down_weight, down_bias, final_gain, final_bias, head_weight
    )
    color, diff = blend(
        spread_4, rows_4, (beside_part, middle_part), place, target.reshape(n_tile, -1, feat)
    )
    spreads = (spread_1, spread_2, spread_3, spread_4)

    diff_beside = move(diff, beside)
    diff_middle = move(diff, middle)
    far_middle = move(diff_beside, middle)
    diff_out = move(diff_middle, outwards)
    far_out = move(far_middle, outwards)
    back = []
    for n, diffs in ((3, (diff,)), (2, (diff_beside,)), (1, (diff_middle, diff_out)), (0, (far_middle, far_out))):
        term = terms(spreads[n], *diffs)
        if back:
            term, back[-1] = lax.optimization_barrier((term, back[-1]))
        back.append(exchange(term))
    grad = add_rows([lists[3], lists[2], lists[1]], back[:3], held)
    grad = add_rows([lists[0]], back[3:], held, grad)
    return (color.reshape(group_views, strip_tiles, cells, feat), grad)


def solution(mesh):
    placed = (
        P(("img", "tile"), None, None, None),
        P(),
        P(),
        P(),
        P(),
        P(),
        P(),
        P(),
        P(),
        P(),
        P(("img", "tile"), None),
        P("img", "tile", None),
        P("img", "tile", None, None),
    )
    return jax.shard_map(
        on_device,
        mesh=mesh,
        in_specs=placed,
        out_specs=(P("img", "tile", None, None), P(("img", "tile"), None)),
        check_vma=False,
    )
```

```python
import functools

import jax
import jax.numpy as jnp
from jax import lax
from jax.experimental import pallas as pl
from jax.experimental.pallas import tpu as pltpu
from jax.sharding import PartitionSpec as P

F32 = jnp.float32
BF16 = jnp.bfloat16
I32 = jnp.int32
VMEM_BYTES = 50 * 1024 * 1024
LANES = (((1,), (1,)), ((), ()))
ROWS = (((0,), (0,)), ((), ()))


def params():
    return pltpu.CompilerParams(vmem_limit_bytes=VMEM_BYTES)


def index_kernel(peers, cap, rows_held, ids_ref, req_ref, own_ref, rank_ref):
    tiles, length = ids_ref.shape
    earlier = lax.broadcasted_iota(I32, (length, length), 0)
    later = lax.broadcasted_iota(I32, (length, length), 1)
    upper = (earlier < later).astype(BF16)
    every = jnp.ones((length, length), BF16)
    peer_id = lax.broadcasted_iota(I32, (peers, length), 0)
    slot_id = lax.broadcasted_iota(I32, (cap, length), 0)
    hots = []
    for t in range(tiles):
        owner = ids_ref[t : t + 1, :] // rows_held
        own_ref[t : t + 1, :] = owner.astype(F32).astype(BF16)
        hots.append((jnp.broadcast_to(owner, (peers, length)) == peer_id).astype(F32))
    stack = jnp.concatenate(hots, 0).astype(BF16)
    within = jnp.dot(stack, upper, preferred_element_type=F32)
    totals = jnp.dot(stack, every, preferred_element_type=F32)
    offset = jnp.zeros((peers, length), F32)
    found = jnp.zeros((2 * peers, cap), F32)
    for t in range(tiles):
        own_rows = slice(t * peers, (t + 1) * peers)
        rank = jnp.sum(hots[t] * (within[own_rows] + offset), axis=0, keepdims=True).astype(I32)
        offset = offset + totals[own_rows]
        rank_ref[t : t + 1, :] = rank.astype(F32).astype(BF16)
        ids = ids_ref[t : t + 1, :]
        row = ids - (ids // rows_held) * rows_held + 1
        high = (row >> 6).astype(F32)
        low = (row & 63).astype(F32)
        digits = jnp.concatenate([hots[t] * high, hots[t] * low], 0).astype(BF16)
        slots = (jnp.broadcast_to(rank, (cap, length)) == slot_id).astype(F32).astype(BF16)
        found = found + lax.dot_general(digits, slots, LANES, preferred_element_type=F32)
    req_ref[...] = (found[:peers] * 64.0 + found[peers:]).astype(I32) - 1


def index(ids, peers, cap, rows_held):
    like = jax.ShapeDtypeStruct(ids.shape, BF16)
    return pl.pallas_call(
        functools.partial(index_kernel, peers, cap, rows_held),
        out_shape=(jax.ShapeDtypeStruct((peers, cap), I32), like, like),
        compiler_params=params(),
        cost_estimate=pl.CostEstimate(flops=10**9, bytes_accessed=10**7, transcendentals=0),
        name="index",
    )(ids)


def weights_kernel(alpha_ref, out_ref):
    alpha = alpha_ref[...]
    length = alpha.shape[1]
    logs = jnp.log1p(-alpha)
    earlier = lax.broadcasted_iota(I32, (length, length), 0)
    later = lax.broadcasted_iota(I32, (length, length), 1)
    upper = (earlier < later).astype(F32)
    before = jnp.dot(logs, upper, preferred_element_type=F32, precision=lax.Precision.HIGHEST)
    out_ref[...] = (alpha * jnp.exp(before)).astype(BF16)


def weights(alphas):
    return pl.pallas_call(
        weights_kernel,
        out_shape=jax.ShapeDtypeStruct(alphas.shape, BF16),
        compiler_params=params(),
        cost_estimate=pl.CostEstimate(flops=10**8, bytes_accessed=10**6, transcendentals=0),
        name="weights",
    )(alphas)


def spread_kernel(near, cap, packs, base_ref, *refs):
    out_ref = refs[-1]
    own_all, rank_all, weight_all = (sum(ref[...].astype(F32) for ref in refs[k : 3 * packs : 3]) for k in range(3))
    tiles, length = own_all.shape
    cells = weight_all.shape[0] // tiles
    slot_id = lax.broadcasted_iota(I32, (cap, length), 0)
    for t in range(tiles):
        own = own_all[t : t + 1, :].astype(I32)
        rank = rank_all[t : t + 1, :].astype(I32)
        here = slice(t * cells, (t + 1) * cells)
        weight = weight_all[here, :]
        by_owner = [jnp.where(own == base_ref[o], weight, 0.0) for o in range(near)]
        slots = (jnp.broadcast_to(rank, (cap, length)) == slot_id).astype(F32).astype(BF16)
        moved = lax.dot_general(
            jnp.concatenate(by_owner, 0).astype(BF16), slots, LANES, preferred_element_type=F32
        ).astype(BF16)
        if cap % 128 == 0:
            for o in range(near):
                out_ref[here, o * cap : (o + 1) * cap] = moved[o * cells : (o + 1) * cells]
        else:
            out_ref[here, :] = jnp.concatenate([moved[o * cells : (o + 1) * cells] for o in range(near)], 1)


def spread(owners, packs, tiles, cells, cap):
    length = packs[0].shape[1]
    near = owners.shape[0]
    step = 16
    first = tiles * cells // step
    specs = [
        pl.BlockSpec((step, length), lambda t: (first + t, 0)),
        pl.BlockSpec((step, length), lambda t: (first + tiles // step + t, 0)),
        pl.BlockSpec((step * cells, length), lambda t: (t, 0)),
    ]
    return pl.pallas_call(
        functools.partial(spread_kernel, near, cap, len(packs)),
        grid=(tiles // step,),
        in_specs=[pl.BlockSpec(memory_space=pltpu.SMEM)] + specs * len(packs),
        out_specs=pl.BlockSpec((step * cells, near * cap), lambda t: (t, 0)),
        out_shape=jax.ShapeDtypeStruct((tiles * cells, near * cap), BF16),
        compiler_params=params(),
        cost_estimate=pl.CostEstimate(flops=10**8, bytes_accessed=10**6, transcendentals=0),
        name="spread",
    )(owners, *[pack for pack in packs for _ in range(3)])


def gather_kernel(group, cap, asked_ref, rows_ref, out_ref):
    first = pl.program_id(0) * group
    asked = asked_ref[...]
    peer = lax.broadcasted_iota(I32, asked.shape, 1)
    held = rows_ref.shape[0]
    row_id = lax.broadcasted_iota(I32, (cap, held), 1)
    picks = []
    for q in range(group):
        column = jnp.sum(jnp.where(peer == first + q, asked, 0), axis=1, keepdims=True)
        picks.append((jnp.broadcast_to(column, (cap, held)) == row_id).astype(F32).astype(BF16))
    pick = jnp.concatenate(picks, 0)
    out_ref[...] = jnp.dot(pick, rows_ref[...], preferred_element_type=F32).astype(BF16)


def gather(asked, rows, flops=10**8):
    near, cap = asked.shape
    held, feat = rows.shape
    group = max(1, min(near, 1024 // cap))
    return pl.pallas_call(
        functools.partial(gather_kernel, group, cap),
        grid=(near // group,),
        in_specs=[pl.BlockSpec((cap, near), lambda i: (0, 0)), pl.BlockSpec((held, feat), lambda i: (0, 0))],
        out_specs=pl.BlockSpec((group * cap, feat), lambda i: (i, 0)),
        out_shape=jax.ShapeDtypeStruct((near * cap, feat), BF16),
        compiler_params=params(),
        cost_estimate=pl.CostEstimate(flops=flops, bytes_accessed=10**6, transcendentals=0),
        name="gather",
    )(asked.T, rows)


def blend_kernel(n_parts, weight_ref, rows_ref, *rest):
    color = jnp.dot(weight_ref[...], rows_ref[...], preferred_element_type=F32)
    for part_ref in rest[:n_parts]:
        color = color + part_ref[...].astype(F32)
    rest[n_parts][...] = color.astype(BF16)


def last_blend_kernel(n_parts, place_ref, weight_ref, rows_ref, *rest):
    parts, target_ref = rest[:n_parts], rest[n_parts]
    color_ref, diff_ref = rest[-2:]
    color = jnp.dot(weight_ref[...], rows_ref[...], preferred_element_type=F32)
    for part_ref in parts:
        color = color + part_ref[...].astype(F32)
    color_ref[...] = color.astype(BF16)
    cells = target_ref.shape[1]
    per_step = color.shape[0] // cells
    for k in range(per_step):
        at = place_ref[pl.program_id(0) * per_step + k]
        here = slice(k * cells, (k + 1) * cells)
        diff_ref[here, :] = (color[here] - target_ref[at].astype(F32)).astype(BF16)


def blend(weight, rows, parts=(), place=None, target=None):
    cells, slots = weight.shape
    feat = rows.shape[1]
    block = min(cells, 256)
    cell_block = pl.BlockSpec((block, feat), lambda i: (i, 0))
    out = jax.ShapeDtypeStruct((cells, feat), BF16)
    last = place is not None
    in_specs = [pl.BlockSpec((block, slots), lambda i: (i, 0)), pl.BlockSpec((slots, feat), lambda i: (0, 0))]
    in_specs += [cell_block] * len(parts)
    args = [weight, rows, *parts]
    if last:
        in_specs = [pl.BlockSpec(memory_space=pltpu.SMEM)] + in_specs + [pl.BlockSpec(target.shape, lambda i: (0, 0, 0))]
        args = [place, *args, target]
    return pl.pallas_call(
        functools.partial(last_blend_kernel if last else blend_kernel, len(parts)),
        grid=(cells // block,),
        in_specs=in_specs,
        out_specs=(cell_block, cell_block) if last else cell_block,
        out_shape=(out, out) if last else out,
        compiler_params=params(),
        cost_estimate=pl.CostEstimate(flops=4 * 10**9, bytes_accessed=10**7, transcendentals=0),
        name="blend",
    )(*args)


def terms_kernel(weight_ref, *refs):
    diff = refs[0][...]
    for more_ref in refs[1:-1]:
        diff = diff + more_ref[...]
    refs[-1][...] = lax.dot_general(weight_ref[...], diff, ROWS, preferred_element_type=F32).astype(BF16)


def terms(weight, *diffs):
    cells, slots = weight.shape
    feat = diffs[0].shape[1]
    block = min(slots, 1024)
    return pl.pallas_call(
        terms_kernel,
        grid=(slots // block,),
        in_specs=[pl.BlockSpec((cells, block), lambda i: (0, i))]
        + [pl.BlockSpec((cells, feat), lambda i: (0, 0))] * len(diffs),
        out_specs=pl.BlockSpec((block, feat), lambda i: (i, 0)),
        out_shape=jax.ShapeDtypeStruct((slots, feat), BF16),
        compiler_params=params(),
        cost_estimate=pl.CostEstimate(flops=10**11, bytes_accessed=10**7, transcendentals=0),
        name="terms",
    )(weight, *diffs)


def add_rows_kernel(count, *refs):
    out_ref = refs[-1]
    block = out_ref.shape[0]
    total = None if len(refs) == 2 * count + 1 else refs[2 * count][...]
    for n in range(count):
        asked_ref, terms_ref = refs[n], refs[count + n]
        near, cap = asked_ref.shape
        row_id = lax.broadcasted_iota(I32, (block, cap), 0) + pl.program_id(0) * block
        picks = []
        for o in range(near):
            asked = jnp.broadcast_to(asked_ref[o : o + 1, :], (block, cap))
            picks.append((asked == row_id).astype(F32).astype(BF16))
        got = jnp.dot(jnp.concatenate(picks, 1), terms_ref[...], preferred_element_type=F32)
        total = got if total is None else total + got
    out_ref[...] = total


def add_rows(askeds, arrivals, held, before=None):
    near, cap = askeds[0].shape
    feat = arrivals[0].shape[1]
    count = len(askeds)
    block = min(held, 512)
    row_block = pl.BlockSpec((block, feat), lambda i: (i, 0))
    more = before is not None
    in_specs = [pl.BlockSpec((near, cap), lambda i: (0, 0))] * count
    in_specs += [pl.BlockSpec((near * cap, feat), lambda i: (0, 0))] * count
    return pl.pallas_call(
        functools.partial(add_rows_kernel, count),
        grid=(held // block,),
        in_specs=in_specs + [row_block] * more,
        out_specs=row_block,
        out_shape=jax.ShapeDtypeStruct((held, feat), F32),
        compiler_params=params(),
        cost_estimate=pl.CostEstimate(flops=5 * count * 10**9, bytes_accessed=10**7, transcendentals=0),
        name="add_rows",
    )(*askeds, *arrivals, *((before,) if more else ()))


def layer_norm(rows, gain, bias):
    mean = jnp.mean(rows, axis=-1, keepdims=True)
    centred = rows - mean
    var = jnp.mean(centred * centred, axis=-1, keepdims=True)
    return centred * lax.rsqrt(var + 1e-05) * gain + bias


def encode_kernel(strips, *refs):
    gain, bias, up, up_bias, down, down_bias, last_gain, last_bias, head = refs[strips:-1]
    out_ref = refs[-1]
    hidden = up.shape[1]
    step = 768 if hidden % 768 == 0 else hidden
    group = max(1, strips // 2)
    for first in range(0, strips, group):
        wide = jnp.concatenate([ref[...] for ref in refs[first : first + group]], 0).astype(F32)
        normed = layer_norm(wide, gain[...], bias[...]).astype(BF16)
        block_out = wide + down_bias[...]
        for k in range(0, hidden, step):
            inner = jnp.dot(normed, up[:, k : k + step], preferred_element_type=F32) + up_bias[k : k + step]
            act = (inner * jax.nn.sigmoid(1.702 * inner)).astype(BF16)
            block_out = block_out + jnp.dot(act, down[k : k + step, :], preferred_element_type=F32)
        final = layer_norm(block_out, last_gain[...], last_bias[...]).astype(BF16)
        embed = jnp.dot(final, head[...], preferred_element_type=F32)
        scale = lax.rsqrt(jnp.mean(embed * embed, axis=-1, keepdims=True) + 1e-06)
        target = (embed * scale).astype(BF16)
        cells = target.shape[0] // group
        for n in range(group):
            out_ref[first + n] = target[n * cells : (n + 1) * cells]


def encode(strips, *weights_and_biases):
    cells = strips[0].shape[0]
    return pl.pallas_call(
        functools.partial(encode_kernel, len(strips)),
        out_shape=jax.ShapeDtypeStruct((len(strips), cells, weights_and_biases[-1].shape[1]), BF16),
        compiler_params=params(),
        cost_estimate=pl.CostEstimate(flops=15 * 10**9, bytes_accessed=10**7, transcendentals=0),
        name="encode",
    )(*strips, *weights_and_biases)


def on_device(
    patches,
    norm_gain,
    norm_bias,
    up_weight,
    up_bias,
    down_weight,
    down_bias,
    final_gain,
    final_bias,
    head_weight,
    gauss_rows,
    tile_lists,
    alphas,
):
    view_count, tiles_view, cells, width = patches.shape
    feat = head_weight.shape[1]
    n_img = lax.axis_size("img")
    n_tile = lax.axis_size("tile")
    peers = n_img * n_tile
    both = ("img", "tile")
    held = gauss_rows.shape[0]
    group_views, strip_tiles, list_len = tile_lists.shape
    tiles = group_views * strip_tiles
    cap = 2 * tiles * list_len // peers

    wide_layer = n_tile // 4
    near = n_img * wide_layer
    tile = lax.axis_index("tile")
    layer = tile // wide_layer
    low = layer < 2
    groups = [[i * n_tile + z * wide_layer + k for i in range(n_img) for k in range(wide_layer)] for z in range(4)]

    def moves(*pairs):
        return [(a * wide_layer + k, b * wide_layer + k) for a, b in pairs for k in range(wide_layer)]

    beside = moves((0, 1), (1, 0), (2, 3), (3, 2))
    middle = moves((1, 2), (2, 1))
    inwards = moves((0, 1), (3, 2))
    outwards = moves((1, 0), (2, 3))

    def move(x, pairs):
        return lax.ppermute(x, "tile", pairs)

    def exchange(x):
        return lax.all_to_all(x, both, split_axis=0, concat_axis=0, axis_index_groups=groups, tiled=True)

    def tie(*values):
        return lax.optimization_barrier(values)

    request, own, rank = index(tile_lists.reshape(tiles, list_len), peers, cap, held)
    weight = weights(alphas.reshape(tiles * cells, list_len))
    packed = jnp.concatenate([weight, own, rank], 0)
    request, patches = tie(request, patches)
    asked = lax.all_to_all(request, both, split_axis=0, concat_axis=0, tiled=True)
    chips = n_tile // 2
    core = tile % 2
    chip = tile // 2
    patches = patches.reshape(chips, 2, -1, width)
    others = lax.dynamic_index_in_dim(patches, 1 - core, 1, keepdims=False)
    others = move(others, [(a, a ^ 1) for a in range(n_tile)])
    asked, others, packed = tie(asked, others, packed)
    far_to_outer = move(packed, moves((0, 3), (3, 0)))
    far_to_inner = move(packed, moves((0, 2), (3, 1)))
    pairs = jnp.concatenate([lax.dynamic_index_in_dim(patches, core, 1, keepdims=False), others], 1)

    def strip(pairs, n):
        pair = lax.dynamic_index_in_dim(pairs, lax.rem(chip + n, chips), 0, keepdims=False)
        return move(pair, [(a, (a + 2 * n) % n_tile) for a in range(n_tile)]) if n else pair

    view = jnp.arange(n_tile, dtype=I32)
    place = lax.rem(chip + chips - view // 2, chips) * 2 + (view % 2 != core).astype(I32)
    asked = asked.reshape(n_img, 4, wide_layer, cap)
    sets = (jnp.where(low, 3, 0), jnp.where(low, 2, 1), layer ^ 1, layer)
    lists = [lax.dynamic_index_in_dim(asked, s, 1, keepdims=False).reshape(near, cap) for s in sets]
    owners = (
        jnp.arange(n_img, dtype=I32)[:, None] * n_tile
        + layer * wide_layer
        + jnp.arange(wide_layer, dtype=I32)[None, :]
    ).reshape(near)

    def spread_of(*packs):
        return spread(owners, packs, tiles, cells, cap)

    looked, lists[1] = tie(gather(lists[0], gauss_rows), lists[1])
    rows_1 = exchange(looked)
    looked_2 = gather(lists[1], gauss_rows)
    far_to_outer, far_to_inner, pairs, looked_2 = tie(far_to_outer, far_to_inner, pairs, looked_2)
    strips = [strip(pairs, n) for n in range(2)]
    spread_1 = spread_of(far_to_outer, far_to_inner)
    looked_2, spread_1, rows_1, *strips = tie(looked_2, spread_1, rows_1, *strips)

    rows_2 = exchange(looked_2)
    part_1 = blend(spread_1, rows_1)
    moved_1 = move(part_1, inwards)
    part_1, lists[2], packed, pairs = tie(part_1, lists[2], packed, pairs)
    near_to_outer = move(packed, moves((1, 3), (2, 0)))
    near_to_inner = move(packed, middle)
    strips += [strip(pairs, n) for n in range(2, chips)]
    looked_3 = gather(lists[2], gauss_rows, 15 * 10**9)
    spread_2 = spread_of(near_to_outer, near_to_inner)
    looked_3, rows_2, part_1, lists[3], spread_2, packed, *strips = tie(
        looked_3, rows_2, part_1, lists[3], spread_2, packed, *strips
    )

    rows_3 = exchange(looked_3)
    from_beside = move(packed, beside)
    far = move(part_1 + moved_1, middle)
    part_2 = blend(spread_2, rows_2)
    moved_2 = move(part_2, inwards)
    part_2, lists[3] = tie(part_2, lists[3])
    looked_4 = gather(lists[3], gauss_rows)
    spread_3 = spread_of(from_beside)
    looked_4, rows_3, far, spread_3, packed = tie(looked_4, rows_3, far, spread_3, packed)

    rows_4 = exchange(looked_4)
    part_3 = blend(spread_3, rows_3, (far,))
    beside_part = move(part_3, beside)
    part_2, moved_2, part_3, packed, *strips = tie(part_2, moved_2, part_3, packed, *strips)
    middle_part = move(part_2 + moved_2, middle)
    spread_4 = spread_of(packed)
    target = encode(
        strips, norm_gain, norm_bias, up_weight, up_bias, down_weight, down_bias, final_gain, final_bias, head_weight
    )
    color, diff = blend(
        spread_4, rows_4, (beside_part, middle_part), place, target.reshape(n_tile, -1, feat)
    )
    spreads = (spread_1, spread_2, spread_3, spread_4)

    diff_beside = move(diff, beside)
    diff_middle = move(diff, middle)
    far_middle = move(diff_beside, middle)
    diff_out = move(diff_middle, outwards)
    far_out = move(far_middle, outwards)
    back = []
    for n, diffs in ((3, (diff,)), (2, (diff_beside,)), (1, (diff_middle, diff_out)), (0, (far_middle, far_out))):
        term = terms(spreads[n], *diffs)
        if back:
            term, back[-1] = lax.optimization_barrier((term, back[-1]))
        back.append(exchange(term))
    grad = add_rows([lists[3], lists[2], lists[1]], back[:3], held)
    grad = add_rows([lists[0]], back[3:], held, grad)
    return (color.reshape(group_views, strip_tiles, cells, feat), grad)


def solution(mesh):
    placed = (
        P(("img", "tile"), None, None, None),
        P(),
        P(),
        P(),
        P(),
        P(),
        P(),
        P(),
        P(),
        P(),
        P(("img", "tile"), None),
        P("img", "tile", None),
        P("img", "tile", None, None),
    )
    return jax.shard_map(
        on_device,
        mesh=mesh,
        in_specs=placed,
        out_specs=(P("img", "tile", None, None), P(("img", "tile"), None)),
        check_vma=False,
    )
```

```python
import functools

import jax
import jax.numpy as jnp
from jax import lax
from jax.experimental import pallas as pl
from jax.experimental.pallas import tpu as pltpu
from jax.sharding import PartitionSpec as P

F32 = jnp.float32
BF16 = jnp.bfloat16
I32 = jnp.int32
VMEM_BYTES = 50 * 1024 * 1024
LANES = (((1,), (1,)), ((), ()))
ROWS = (((0,), (0,)), ((), ()))


def params():
    return pltpu.CompilerParams(vmem_limit_bytes=VMEM_BYTES)


def index_kernel(peers, cap, rows_held, ids_ref, req_ref, own_ref, rank_ref):
    tiles, length = ids_ref.shape
    earlier = lax.broadcasted_iota(I32, (length, length), 0)
    later = lax.broadcasted_iota(I32, (length, length), 1)
    upper = (earlier < later).astype(BF16)
    every = jnp.ones((length, length), BF16)
    peer_id = lax.broadcasted_iota(I32, (peers, length), 0)
    slot_id = lax.broadcasted_iota(I32, (cap, length), 0)
    hots = []
    for t in range(tiles):
        owner = ids_ref[t : t + 1, :] // rows_held
        own_ref[t : t + 1, :] = owner.astype(F32).astype(BF16)
        hots.append((jnp.broadcast_to(owner, (peers, length)) == peer_id).astype(F32))
    stack = jnp.concatenate(hots, 0).astype(BF16)
    within = jnp.dot(stack, upper, preferred_element_type=F32)
    totals = jnp.dot(stack, every, preferred_element_type=F32)
    offset = jnp.zeros((peers, length), F32)
    found = jnp.zeros((2 * peers, cap), F32)
    for t in range(tiles):
        own_rows = slice(t * peers, (t + 1) * peers)
        rank = jnp.sum(hots[t] * (within[own_rows] + offset), axis=0, keepdims=True).astype(I32)
        offset = offset + totals[own_rows]
        rank_ref[t : t + 1, :] = rank.astype(F32).astype(BF16)
        ids = ids_ref[t : t + 1, :]
        row = ids - (ids // rows_held) * rows_held + 1
        high = (row >> 6).astype(F32)
        low = (row & 63).astype(F32)
        digits = jnp.concatenate([hots[t] * high, hots[t] * low], 0).astype(BF16)
        slots = (jnp.broadcast_to(rank, (cap, length)) == slot_id).astype(F32).astype(BF16)
        found = found + lax.dot_general(digits, slots, LANES, preferred_element_type=F32)
    req_ref[...] = (found[:peers] * 64.0 + found[peers:]).astype(I32) - 1


def index(ids, peers, cap, rows_held):
    like = jax.ShapeDtypeStruct(ids.shape, BF16)
    return pl.pallas_call(
        functools.partial(index_kernel, peers, cap, rows_held),
        out_shape=(jax.ShapeDtypeStruct((peers, cap), I32), like, like),
        compiler_params=params(),
        cost_estimate=pl.CostEstimate(flops=10**9, bytes_accessed=10**7, transcendentals=0),
        name="index",
    )(ids)


def weights_kernel(alpha_ref, out_ref):
    alpha = alpha_ref[...]
    length = alpha.shape[1]
    logs = jnp.log1p(-alpha)
    earlier = lax.broadcasted_iota(I32, (length, length), 0)
    later = lax.broadcasted_iota(I32, (length, length), 1)
    upper = (earlier < later).astype(F32)
    before = jnp.dot(logs, upper, preferred_element_type=F32, precision=lax.Precision.HIGHEST)
    out_ref[...] = (alpha * jnp.exp(before)).astype(BF16)


def weights(alphas):
    return pl.pallas_call(
        weights_kernel,
        out_shape=jax.ShapeDtypeStruct(alphas.shape, BF16),
        compiler_params=params(),
        cost_estimate=pl.CostEstimate(flops=10**8, bytes_accessed=10**6, transcendentals=0),
        name="weights",
    )(alphas)


def spread_kernel(near, cap, packs, base_ref, *refs):
    out_ref = refs[-1]
    own_all, rank_all, weight_all = (sum(ref[...].astype(F32) for ref in refs[k : 3 * packs : 3]) for k in range(3))
    tiles, length = own_all.shape
    cells = weight_all.shape[0] // tiles
    slot_id = lax.broadcasted_iota(I32, (cap, length), 0)
    for t in range(tiles):
        own = own_all[t : t + 1, :].astype(I32)
        rank = rank_all[t : t + 1, :].astype(I32)
        here = slice(t * cells, (t + 1) * cells)
        weight = weight_all[here, :]
        by_owner = [jnp.where(own == base_ref[o], weight, 0.0) for o in range(near)]
        slots = (jnp.broadcast_to(rank, (cap, length)) == slot_id).astype(F32).astype(BF16)
        moved = lax.dot_general(
            jnp.concatenate(by_owner, 0).astype(BF16), slots, LANES, preferred_element_type=F32
        ).astype(BF16)
        if cap % 128 == 0:
            for o in range(near):
                out_ref[here, o * cap : (o + 1) * cap] = moved[o * cells : (o + 1) * cells]
        else:
            out_ref[here, :] = jnp.concatenate([moved[o * cells : (o + 1) * cells] for o in range(near)], 1)


def spread(owners, packs, tiles, cells, cap):
    length = packs[0].shape[1]
    near = owners.shape[0]
    step = 16
    first = tiles * cells // step
    specs = [
        pl.BlockSpec((step, length), lambda t: (first + t, 0)),
        pl.BlockSpec((step, length), lambda t: (first + tiles // step + t, 0)),
        pl.BlockSpec((step * cells, length), lambda t: (t, 0)),
    ]
    return pl.pallas_call(
        functools.partial(spread_kernel, near, cap, len(packs)),
        grid=(tiles // step,),
        in_specs=[pl.BlockSpec(memory_space=pltpu.SMEM)] + specs * len(packs),
        out_specs=pl.BlockSpec((step * cells, near * cap), lambda t: (t, 0)),
        out_shape=jax.ShapeDtypeStruct((tiles * cells, near * cap), BF16),
        compiler_params=params(),
        cost_estimate=pl.CostEstimate(flops=10**8, bytes_accessed=10**6, transcendentals=0),
        name="spread",
    )(owners, *[pack for pack in packs for _ in range(3)])


def gather_kernel(group, cap, asked_ref, rows_ref, out_ref):
    first = pl.program_id(0) * group
    asked = asked_ref[...]
    peer = lax.broadcasted_iota(I32, asked.shape, 1)
    held = rows_ref.shape[0]
    row_id = lax.broadcasted_iota(I32, (cap, held), 1)
    picks = []
    for q in range(group):
        column = jnp.sum(jnp.where(peer == first + q, asked, 0), axis=1, keepdims=True)
        picks.append((jnp.broadcast_to(column, (cap, held)) == row_id).astype(F32).astype(BF16))
    pick = jnp.concatenate(picks, 0)
    out_ref[...] = jnp.dot(pick, rows_ref[...], preferred_element_type=F32).astype(BF16)


def gather(asked, rows):
    near, cap = asked.shape
    held, feat = rows.shape
    group = max(1, min(near, 1024 // cap))
    return pl.pallas_call(
        functools.partial(gather_kernel, group, cap),
        grid=(near // group,),
        in_specs=[pl.BlockSpec((cap, near), lambda i: (0, 0)), pl.BlockSpec((held, feat), lambda i: (0, 0))],
        out_specs=pl.BlockSpec((group * cap, feat), lambda i: (i, 0)),
        out_shape=jax.ShapeDtypeStruct((near * cap, feat), BF16),
        compiler_params=params(),
        cost_estimate=pl.CostEstimate(flops=10**8, bytes_accessed=10**6, transcendentals=0),
        name="gather",
    )(asked.T, rows)


def blend_kernel(n_parts, weight_ref, rows_ref, *rest):
    color = jnp.dot(weight_ref[...], rows_ref[...], preferred_element_type=F32)
    for part_ref in rest[:n_parts]:
        color = color + part_ref[...].astype(F32)
    rest[n_parts][...] = color.astype(BF16)


def last_blend_kernel(n_parts, place_ref, weight_ref, rows_ref, *rest):
    parts, target_ref = rest[:n_parts], rest[n_parts]
    color_ref, diff_ref = rest[-2:]
    color = jnp.dot(weight_ref[...], rows_ref[...], preferred_element_type=F32)
    for part_ref in parts:
        color = color + part_ref[...].astype(F32)
    color_ref[...] = color.astype(BF16)
    cells = target_ref.shape[1]
    per_step = color.shape[0] // cells
    for k in range(per_step):
        at = place_ref[pl.program_id(0) * per_step + k]
        here = slice(k * cells, (k + 1) * cells)
        diff_ref[here, :] = (color[here] - target_ref[at].astype(F32)).astype(BF16)


def blend(weight, rows, parts=(), place=None, target=None):
    cells, slots = weight.shape
    feat = rows.shape[1]
    block = min(cells, 256)
    cell_block = pl.BlockSpec((block, feat), lambda i: (i, 0))
    out = jax.ShapeDtypeStruct((cells, feat), BF16)
    last = place is not None
    in_specs = [pl.BlockSpec((block, slots), lambda i: (i, 0)), pl.BlockSpec((slots, feat), lambda i: (0, 0))]
    in_specs += [cell_block] * len(parts)
    args = [weight, rows, *parts]
    if last:
        in_specs = [pl.BlockSpec(memory_space=pltpu.SMEM)] + in_specs + [pl.BlockSpec(target.shape, lambda i: (0, 0, 0))]
        args = [place, *args, target]
    return pl.pallas_call(
        functools.partial(last_blend_kernel if last else blend_kernel, len(parts)),
        grid=(cells // block,),
        in_specs=in_specs,
        out_specs=(cell_block, cell_block) if last else cell_block,
        out_shape=(out, out) if last else out,
        compiler_params=params(),
        cost_estimate=pl.CostEstimate(flops=4 * 10**9, bytes_accessed=10**7, transcendentals=0),
        name="blend",
    )(*args)


def terms_kernel(weight_ref, *refs):
    diff = refs[0][...]
    for more_ref in refs[1:-1]:
        diff = diff + more_ref[...]
    refs[-1][...] = lax.dot_general(weight_ref[...], diff, ROWS, preferred_element_type=F32).astype(BF16)


def terms(weight, *diffs):
    cells, slots = weight.shape
    feat = diffs[0].shape[1]
    block = min(slots, 1024)
    return pl.pallas_call(
        terms_kernel,
        grid=(slots // block,),
        in_specs=[pl.BlockSpec((cells, block), lambda i: (0, i))]
        + [pl.BlockSpec((cells, feat), lambda i: (0, 0))] * len(diffs),
        out_specs=pl.BlockSpec((block, feat), lambda i: (i, 0)),
        out_shape=jax.ShapeDtypeStruct((slots, feat), BF16),
        compiler_params=params(),
        cost_estimate=pl.CostEstimate(flops=10**11, bytes_accessed=10**7, transcendentals=0),
        name="terms",
    )(weight, *diffs)


def add_rows_kernel(count, *refs):
    out_ref = refs[-1]
    block = out_ref.shape[0]
    total = None if len(refs) == 2 * count + 1 else refs[2 * count][...]
    for n in range(count):
        asked_ref, terms_ref = refs[n], refs[count + n]
        near, cap = asked_ref.shape
        row_id = lax.broadcasted_iota(I32, (block, cap), 0) + pl.program_id(0) * block
        picks = []
        for o in range(near):
            asked = jnp.broadcast_to(asked_ref[o : o + 1, :], (block, cap))
            picks.append((asked == row_id).astype(F32).astype(BF16))
        got = jnp.dot(jnp.concatenate(picks, 1), terms_ref[...], preferred_element_type=F32)
        total = got if total is None else total + got
    out_ref[...] = total


def add_rows(askeds, arrivals, held, before=None):
    near, cap = askeds[0].shape
    feat = arrivals[0].shape[1]
    count = len(askeds)
    block = min(held, 512)
    row_block = pl.BlockSpec((block, feat), lambda i: (i, 0))
    more = before is not None
    in_specs = [pl.BlockSpec((near, cap), lambda i: (0, 0))] * count
    in_specs += [pl.BlockSpec((near * cap, feat), lambda i: (0, 0))] * count
    return pl.pallas_call(
        functools.partial(add_rows_kernel, count),
        grid=(held // block,),
        in_specs=in_specs + [row_block] * more,
        out_specs=row_block,
        out_shape=jax.ShapeDtypeStruct((held, feat), F32),
        compiler_params=params(),
        cost_estimate=pl.CostEstimate(flops=5 * count * 10**9, bytes_accessed=10**7, transcendentals=0),
        name="add_rows",
    )(*askeds, *arrivals, *((before,) if more else ()))


def layer_norm(rows, gain, bias):
    mean = jnp.mean(rows, axis=-1, keepdims=True)
    centred = rows - mean
    var = jnp.mean(centred * centred, axis=-1, keepdims=True)
    return centred * lax.rsqrt(var + 1e-05) * gain + bias


def encode_kernel(strips, *refs):
    gain, bias, up, up_bias, down, down_bias, last_gain, last_bias, head = refs[strips:-1]
    out_ref = refs[-1]
    hidden = up.shape[1]
    step = 768 if hidden % 768 == 0 else hidden
    group = max(1, strips // 2)
    for first in range(0, strips, group):
        wide = jnp.concatenate([ref[...] for ref in refs[first : first + group]], 0).astype(F32)
        normed = layer_norm(wide, gain[...], bias[...]).astype(BF16)
        block_out = wide + down_bias[...]
        for k in range(0, hidden, step):
            inner = jnp.dot(normed, up[:, k : k + step], preferred_element_type=F32) + up_bias[k : k + step]
            act = (inner * jax.nn.sigmoid(1.702 * inner)).astype(BF16)
            block_out = block_out + jnp.dot(act, down[k : k + step, :], preferred_element_type=F32)
        final = layer_norm(block_out, last_gain[...], last_bias[...]).astype(BF16)
        embed = jnp.dot(final, head[...], preferred_element_type=F32)
        scale = lax.rsqrt(jnp.mean(embed * embed, axis=-1, keepdims=True) + 1e-06)
        target = (embed * scale).astype(BF16)
        cells = target.shape[0] // group
        for n in range(group):
            out_ref[first + n] = target[n * cells : (n + 1) * cells]


def encode(strips, *weights_and_biases):
    cells = strips[0].shape[0]
    return pl.pallas_call(
        functools.partial(encode_kernel, len(strips)),
        out_shape=jax.ShapeDtypeStruct((len(strips), cells, weights_and_biases[-1].shape[1]), BF16),
        compiler_params=params(),
        cost_estimate=pl.CostEstimate(flops=10**11, bytes_accessed=10**7, transcendentals=0),
        name="encode",
    )(*strips, *weights_and_biases)


def on_device(
    patches,
    norm_gain,
    norm_bias,
    up_weight,
    up_bias,
    down_weight,
    down_bias,
    final_gain,
    final_bias,
    head_weight,
    gauss_rows,
    tile_lists,
    alphas,
):
    view_count, tiles_view, cells, width = patches.shape
    feat = head_weight.shape[1]
    n_img = lax.axis_size("img")
    n_tile = lax.axis_size("tile")
    peers = n_img * n_tile
    both = ("img", "tile")
    held = gauss_rows.shape[0]
    group_views, strip_tiles, list_len = tile_lists.shape
    tiles = group_views * strip_tiles
    cap = 2 * tiles * list_len // peers

    wide_layer = n_tile // 4
    near = n_img * wide_layer
    tile = lax.axis_index("tile")
    layer = tile // wide_layer
    low = layer < 2
    groups = [[i * n_tile + z * wide_layer + k for i in range(n_img) for k in range(wide_layer)] for z in range(4)]

    def moves(*pairs):
        return [(a * wide_layer + k, b * wide_layer + k) for a, b in pairs for k in range(wide_layer)]

    beside = moves((0, 1), (1, 0), (2, 3), (3, 2))
    middle = moves((1, 2), (2, 1))
    inwards = moves((0, 1), (3, 2))
    outwards = moves((1, 0), (2, 3))

    def move(x, pairs):
        return lax.ppermute(x, "tile", pairs)

    def exchange(x):
        return lax.all_to_all(x, both, split_axis=0, concat_axis=0, axis_index_groups=groups, tiled=True)

    def tie(*values):
        return lax.optimization_barrier(values)

    request, own, rank = index(tile_lists.reshape(tiles, list_len), peers, cap, held)
    weight = weights(alphas.reshape(tiles * cells, list_len))
    packed = jnp.concatenate([weight, own, rank], 0)
    request, patches = tie(request, patches)
    asked = lax.all_to_all(request, both, split_axis=0, concat_axis=0, tiled=True)
    chips = n_tile // 2
    core = tile % 2
    chip = tile // 2
    patches = patches.reshape(chips, 2, -1, width)
    others = lax.dynamic_index_in_dim(patches, 1 - core, 1, keepdims=False)
    others = move(others, [(a, a ^ 1) for a in range(n_tile)])
    asked, others, packed = tie(asked, others, packed)
    far_to_outer = move(packed, moves((0, 3), (3, 0)))
    far_to_inner = move(packed, moves((0, 2), (3, 1)))
    pairs = jnp.concatenate([lax.dynamic_index_in_dim(patches, core, 1, keepdims=False), others], 1)
    strips = []
    for n in range(chips):
        pair = lax.dynamic_index_in_dim(pairs, lax.rem(chip + n, chips), 0, keepdims=False)
        strips.append(move(pair, [(a, (a + 2 * n) % n_tile) for a in range(n_tile)]) if n else pair)
    view = jnp.arange(n_tile, dtype=I32)
    place = lax.rem(chip + chips - view // 2, chips) * 2 + (view % 2 != core).astype(I32)
    asked = asked.reshape(n_img, 4, wide_layer, cap)
    sets = (jnp.where(low, 3, 0), jnp.where(low, 2, 1), layer ^ 1, layer)
    lists = [lax.dynamic_index_in_dim(asked, s, 1, keepdims=False).reshape(near, cap) for s in sets]
    owners = (
        jnp.arange(n_img, dtype=I32)[:, None] * n_tile
        + layer * wide_layer
        + jnp.arange(wide_layer, dtype=I32)[None, :]
    ).reshape(near)

    def spread_of(*packs):
        return spread(owners, packs, tiles, cells, cap)

    looked, lists[1] = tie(gather(lists[0], gauss_rows), lists[1])
    rows_1 = exchange(looked)
    looked_2 = gather(lists[1], gauss_rows)
    looked_2, lists[2] = tie(looked_2, lists[2])
    spread_1 = spread_of(far_to_outer, far_to_inner)
    looked_3 = gather(lists[2], gauss_rows)
    looked_2, looked_3, spread_1, rows_1, packed = tie(looked_2, looked_3, spread_1, rows_1, packed)

    rows_2 = exchange(looked_2)
    part_1 = blend(spread_1, rows_1)
    moved_1 = move(part_1, inwards)
    near_to_outer = move(packed, moves((1, 3), (2, 0)))
    near_to_inner = move(packed, middle)
    from_beside = move(packed, beside)
    part_1, *strips = tie(part_1, *strips)
    target = encode(
        strips, norm_gain, norm_bias, up_weight, up_bias, down_weight, down_bias, final_gain, final_bias, head_weight
    )
    looked_3, rows_2, part_1, target, lists[3], near_to_outer, near_to_inner, from_beside = tie(
        looked_3, rows_2, part_1, target, lists[3], near_to_outer, near_to_inner, from_beside
    )

    rows_3 = exchange(looked_3)
    spread_2 = spread_of(near_to_outer, near_to_inner)
    part_1, moved_1, spread_2 = tie(part_1, moved_1, spread_2)
    far = move(part_1 + moved_1, middle)
    part_2 = blend(spread_2, rows_2)
    moved_2 = move(part_2, inwards)
    part_2, lists[3], from_beside = tie(part_2, lists[3], from_beside)
    looked_4 = gather(lists[3], gauss_rows)
    spread_3 = spread_of(from_beside)
    looked_4, rows_3, far, spread_3, packed = tie(looked_4, rows_3, far, spread_3, packed)

    rows_4 = exchange(looked_4)
    part_3 = blend(spread_3, rows_3, (far,))
    beside_part = move(part_3, beside)
    part_2, moved_2, part_3, packed = tie(part_2, moved_2, part_3, packed)
    middle_part = move(part_2 + moved_2, middle)
    spread_4 = spread_of(packed)
    color, diff = blend(spread_4, rows_4, (beside_part, middle_part), place, target.reshape(n_tile, -1, feat))
    spreads = (spread_1, spread_2, spread_3, spread_4)

    diff_beside = move(diff, beside)
    diff_middle = move(diff, middle)
    far_middle = move(diff_beside, middle)
    diff_out = move(diff_middle, outwards)
    far_out = move(far_middle, outwards)
    back = []
    for n, diffs in ((3, (diff,)), (2, (diff_beside,)), (1, (diff_middle, diff_out)), (0, (far_middle, far_out))):
        term = terms(spreads[n], *diffs)
        if back:
            term, back[-1] = lax.optimization_barrier((term, back[-1]))
        back.append(exchange(term))
    grad = add_rows([lists[3], lists[2], lists[1]], back[:3], held)
    grad = add_rows([lists[0]], back[3:], held, grad)
    return (color.reshape(group_views, strip_tiles, cells, feat), grad)


def solution(mesh):
    placed = (
        P(("img", "tile"), None, None, None),
        P(),
        P(),
        P(),
        P(),
        P(),
        P(),
        P(),
        P(),
        P(),
        P(("img", "tile"), None),
        P("img", "tile", None),
        P("img", "tile", None, None),
    )
    return jax.shard_map(
        on_device,
        mesh=mesh,
        in_specs=placed,
        out_specs=(P("img", "tile", None, None), P(("img", "tile"), None)),
        check_vma=False,
    )
```

```python
import functools

import jax
import jax.numpy as jnp
from jax import lax
from jax.experimental import pallas as pl
from jax.experimental.pallas import tpu as pltpu
from jax.sharding import PartitionSpec as P

F32 = jnp.float32
BF16 = jnp.bfloat16
I32 = jnp.int32
VMEM_BYTES = 50 * 1024 * 1024
LANES = (((1,), (1,)), ((), ()))
ROWS = (((0,), (0,)), ((), ()))


def params():
    return pltpu.CompilerParams(vmem_limit_bytes=VMEM_BYTES)


def index_kernel(peers, cap, rows_held, ids_ref, req_ref, own_ref, rank_ref):
    tiles, length = ids_ref.shape
    earlier = lax.broadcasted_iota(I32, (length, length), 0)
    later = lax.broadcasted_iota(I32, (length, length), 1)
    upper = (earlier < later).astype(BF16)
    every = jnp.ones((length, length), BF16)
    peer_id = lax.broadcasted_iota(I32, (peers, length), 0)
    slot_id = lax.broadcasted_iota(I32, (cap, length), 0)
    hots, owners, ranks = [], [], []
    for t in range(tiles):
        owner = ids_ref[t : t + 1, :] // rows_held
        owners.append(owner.astype(F32))
        hots.append((jnp.broadcast_to(owner, (peers, length)) == peer_id).astype(F32))
    stack = jnp.concatenate(hots, 0).astype(BF16)
    within = jnp.dot(stack, upper, preferred_element_type=F32)
    totals = jnp.dot(stack, every, preferred_element_type=F32)
    offset = jnp.zeros((peers, length), F32)
    found = jnp.zeros((2 * peers, cap), F32)
    for t in range(tiles):
        own_rows = slice(t * peers, (t + 1) * peers)
        rank = jnp.sum(hots[t] * (within[own_rows] + offset), axis=0, keepdims=True).astype(I32)
        offset = offset + totals[own_rows]
        ranks.append(rank.astype(F32))
        ids = ids_ref[t : t + 1, :]
        row = ids - (ids // rows_held) * rows_held + 1
        high = (row >> 6).astype(F32)
        low = (row & 63).astype(F32)
        digits = jnp.concatenate([hots[t] * high, hots[t] * low], 0).astype(BF16)
        slots = (jnp.broadcast_to(rank, (cap, length)) == slot_id).astype(F32).astype(BF16)
        found = found + lax.dot_general(digits, slots, LANES, preferred_element_type=F32)
    own_ref[...] = jnp.concatenate(owners, 0).astype(BF16)
    rank_ref[...] = jnp.concatenate(ranks, 0).astype(BF16)
    req_ref[...] = (found[:peers] * 64.0 + found[peers:]).astype(I32) - 1


def index(ids, peers, cap, rows_held):
    like = jax.ShapeDtypeStruct(ids.shape, BF16)
    return pl.pallas_call(
        functools.partial(index_kernel, peers, cap, rows_held),
        out_shape=(jax.ShapeDtypeStruct((peers, cap), I32), like, like),
        compiler_params=params(),
        cost_estimate=pl.CostEstimate(flops=10**9, bytes_accessed=10**7, transcendentals=0),
        name="index",
    )(ids)


def weights_kernel(alpha_ref, out_ref):
    alpha = alpha_ref[...]
    length = alpha.shape[1]
    logs = jnp.log1p(-alpha)
    earlier = lax.broadcasted_iota(I32, (length, length), 0)
    later = lax.broadcasted_iota(I32, (length, length), 1)
    upper = (earlier < later).astype(F32)
    before = jnp.dot(logs, upper, preferred_element_type=F32, precision=lax.Precision.HIGHEST)
    out_ref[...] = (alpha * jnp.exp(before)).astype(BF16)


def weights(alphas):
    return pl.pallas_call(
        weights_kernel,
        out_shape=jax.ShapeDtypeStruct(alphas.shape, BF16),
        compiler_params=params(),
        cost_estimate=pl.CostEstimate(flops=10**8, bytes_accessed=10**6, transcendentals=0),
        name="weights",
    )(alphas)


def spread_kernel(near, cap, packs, base_ref, *refs):
    out_ref = refs[-1]
    own_all, rank_all, weight_all = (sum(ref[...].astype(F32) for ref in refs[k : 3 * packs : 3]) for k in range(3))
    tiles, length = own_all.shape
    cells = weight_all.shape[0] // tiles
    slot_id = lax.broadcasted_iota(I32, (cap, length), 0)
    for t in range(tiles):
        own = own_all[t : t + 1, :].astype(I32)
        rank = rank_all[t : t + 1, :].astype(I32)
        here = slice(t * cells, (t + 1) * cells)
        weight = weight_all[here, :]
        by_owner = [jnp.where(own == base_ref[o], weight, 0.0) for o in range(near)]
        slots = (jnp.broadcast_to(rank, (cap, length)) == slot_id).astype(F32).astype(BF16)
        moved = lax.dot_general(
            jnp.concatenate(by_owner, 0).astype(BF16), slots, LANES, preferred_element_type=F32
        ).astype(BF16)
        if cap % 128 == 0:
            for o in range(near):
                out_ref[here, o * cap : (o + 1) * cap] = moved[o * cells : (o + 1) * cells]
        else:
            out_ref[here, :] = jnp.concatenate([moved[o * cells : (o + 1) * cells] for o in range(near)], 1)


def spread(owners, packs, tiles, cells, cap):
    length = packs[0].shape[1]
    near = owners.shape[0]
    step = 16
    first = tiles * cells // step
    specs = [
        pl.BlockSpec((step, length), lambda t: (first + t, 0)),
        pl.BlockSpec((step, length), lambda t: (first + tiles // step + t, 0)),
        pl.BlockSpec((step * cells, length), lambda t: (t, 0)),
    ]
    return pl.pallas_call(
        functools.partial(spread_kernel, near, cap, len(packs)),
        grid=(tiles // step,),
        in_specs=[pl.BlockSpec(memory_space=pltpu.SMEM)] + specs * len(packs),
        out_specs=pl.BlockSpec((step * cells, near * cap), lambda t: (t, 0)),
        out_shape=jax.ShapeDtypeStruct((tiles * cells, near * cap), BF16),
        compiler_params=params(),
        cost_estimate=pl.CostEstimate(flops=10**8, bytes_accessed=10**6, transcendentals=0),
        name="spread",
    )(owners, *[pack for pack in packs for _ in range(3)])


def gather_kernel(group, cap, asked_ref, rows_ref, out_ref):
    first = pl.program_id(0) * group
    asked = asked_ref[...]
    peer = lax.broadcasted_iota(I32, asked.shape, 1)
    held = rows_ref.shape[0]
    row_id = lax.broadcasted_iota(I32, (cap, held), 1)
    picks = []
    for q in range(group):
        column = jnp.sum(jnp.where(peer == first + q, asked, 0), axis=1, keepdims=True)
        picks.append((jnp.broadcast_to(column, (cap, held)) == row_id).astype(F32).astype(BF16))
    pick = jnp.concatenate(picks, 0)
    out_ref[...] = jnp.dot(pick, rows_ref[...], preferred_element_type=F32).astype(BF16)


def gather(asked, rows):
    near, cap = asked.shape
    held, feat = rows.shape
    group = max(1, min(near, 1024 // cap))
    return pl.pallas_call(
        functools.partial(gather_kernel, group, cap),
        grid=(near // group,),
        in_specs=[pl.BlockSpec((cap, near), lambda i: (0, 0)), pl.BlockSpec((held, feat), lambda i: (0, 0))],
        out_specs=pl.BlockSpec((group * cap, feat), lambda i: (i, 0)),
        out_shape=jax.ShapeDtypeStruct((near * cap, feat), BF16),
        compiler_params=params(),
        cost_estimate=pl.CostEstimate(flops=10**8, bytes_accessed=10**6, transcendentals=0),
        name="gather",
    )(asked.T, rows)


def blend_kernel(n_parts, weight_ref, rows_ref, *rest):
    color = jnp.dot(weight_ref[...], rows_ref[...], preferred_element_type=F32)
    for part_ref in rest[:n_parts]:
        color = color + part_ref[...].astype(F32)
    rest[n_parts][...] = color.astype(BF16)


def last_blend_kernel(n_parts, place_ref, weight_ref, rows_ref, *rest):
    parts, target_ref = rest[:n_parts], rest[n_parts]
    color_ref, diff_ref = rest[-2:]
    color = jnp.dot(weight_ref[...], rows_ref[...], preferred_element_type=F32)
    for part_ref in parts:
        color = color + part_ref[...].astype(F32)
    color_ref[...] = color.astype(BF16)
    cells = target_ref.shape[1]
    per_step = color.shape[0] // cells
    for k in range(per_step):
        at = place_ref[pl.program_id(0) * per_step + k]
        here = slice(k * cells, (k + 1) * cells)
        diff_ref[here, :] = (color[here] - target_ref[at].astype(F32)).astype(BF16)


def blend(weight, rows, parts=(), place=None, target=None):
    cells, slots = weight.shape
    feat = rows.shape[1]
    block = min(cells, 256)
    cell_block = pl.BlockSpec((block, feat), lambda i: (i, 0))
    out = jax.ShapeDtypeStruct((cells, feat), BF16)
    last = place is not None
    in_specs = [pl.BlockSpec((block, slots), lambda i: (i, 0)), pl.BlockSpec((slots, feat), lambda i: (0, 0))]
    in_specs += [cell_block] * len(parts)
    args = [weight, rows, *parts]
    if last:
        in_specs = [pl.BlockSpec(memory_space=pltpu.SMEM)] + in_specs + [pl.BlockSpec(target.shape, lambda i: (0, 0, 0))]
        args = [place, *args, target]
    return pl.pallas_call(
        functools.partial(last_blend_kernel if last else blend_kernel, len(parts)),
        grid=(cells // block,),
        in_specs=in_specs,
        out_specs=(cell_block, cell_block) if last else cell_block,
        out_shape=(out, out) if last else out,
        compiler_params=params(),
        cost_estimate=pl.CostEstimate(flops=4 * 10**9, bytes_accessed=10**7, transcendentals=0),
        name="blend",
    )(*args)


def terms_kernel(weight_ref, *refs):
    diff = refs[0][...]
    for more_ref in refs[1:-1]:
        diff = diff + more_ref[...]
    refs[-1][...] = lax.dot_general(weight_ref[...], diff, ROWS, preferred_element_type=F32).astype(BF16)


def terms(weight, *diffs):
    cells, slots = weight.shape
    feat = diffs[0].shape[1]
    block = min(slots, 1024)
    return pl.pallas_call(
        terms_kernel,
        grid=(slots // block,),
        in_specs=[pl.BlockSpec((cells, block), lambda i: (0, i))]
        + [pl.BlockSpec((cells, feat), lambda i: (0, 0))] * len(diffs),
        out_specs=pl.BlockSpec((block, feat), lambda i: (i, 0)),
        out_shape=jax.ShapeDtypeStruct((slots, feat), BF16),
        compiler_params=params(),
        cost_estimate=pl.CostEstimate(flops=10**11, bytes_accessed=10**7, transcendentals=0),
        name="terms",
    )(weight, *diffs)


def add_rows_kernel(count, *refs):
    out_ref = refs[-1]
    block = out_ref.shape[0]
    total = None if len(refs) == 2 * count + 1 else refs[2 * count][...]
    for n in range(count):
        asked_ref, terms_ref = refs[n], refs[count + n]
        near, cap = asked_ref.shape
        row_id = lax.broadcasted_iota(I32, (block, cap), 0) + pl.program_id(0) * block
        picks = []
        for o in range(near):
            asked = jnp.broadcast_to(asked_ref[o : o + 1, :], (block, cap))
            picks.append((asked == row_id).astype(F32).astype(BF16))
        got = jnp.dot(jnp.concatenate(picks, 1), terms_ref[...], preferred_element_type=F32)
        total = got if total is None else total + got
    out_ref[...] = total


def add_rows(askeds, arrivals, held, before=None):
    near, cap = askeds[0].shape
    feat = arrivals[0].shape[1]
    count = len(askeds)
    block = min(held, 512)
    row_block = pl.BlockSpec((block, feat), lambda i: (i, 0))
    more = before is not None
    in_specs = [pl.BlockSpec((near, cap), lambda i: (0, 0))] * count
    in_specs += [pl.BlockSpec((near * cap, feat), lambda i: (0, 0))] * count
    return pl.pallas_call(
        functools.partial(add_rows_kernel, count),
        grid=(held // block,),
        in_specs=in_specs + [row_block] * more,
        out_specs=row_block,
        out_shape=jax.ShapeDtypeStruct((held, feat), F32),
        compiler_params=params(),
        cost_estimate=pl.CostEstimate(flops=5 * count * 10**9, bytes_accessed=10**7, transcendentals=0),
        name="add_rows",
    )(*askeds, *arrivals, *((before,) if more else ()))


def layer_norm(rows, gain, bias):
    mean = jnp.mean(rows, axis=-1, keepdims=True)
    centred = rows - mean
    var = jnp.mean(centred * centred, axis=-1, keepdims=True)
    return centred * lax.rsqrt(var + 1e-05) * gain + bias


def encode_kernel(strips, *refs):
    gain, bias, up, up_bias, down, down_bias, last_gain, last_bias, head = refs[strips:-1]
    out_ref = refs[-1]
    hidden = up.shape[1]
    step = 768 if hidden % 768 == 0 else hidden
    group = max(1, strips // 2)
    for first in range(0, strips, group):
        wide = jnp.concatenate([ref[...] for ref in refs[first : first + group]], 0).astype(F32)
        normed = layer_norm(wide, gain[...], bias[...]).astype(BF16)
        block_out = wide + down_bias[...]
        for k in range(0, hidden, step):
            inner = jnp.dot(normed, up[:, k : k + step], preferred_element_type=F32) + up_bias[k : k + step]
            act = (inner * jax.nn.sigmoid(1.702 * inner)).astype(BF16)
            block_out = block_out + jnp.dot(act, down[k : k + step, :], preferred_element_type=F32)
        final = layer_norm(block_out, last_gain[...], last_bias[...]).astype(BF16)
        embed = jnp.dot(final, head[...], preferred_element_type=F32)
        scale = lax.rsqrt(jnp.mean(embed * embed, axis=-1, keepdims=True) + 1e-06)
        target = (embed * scale).astype(BF16)
        cells = target.shape[0] // group
        for n in range(group):
            out_ref[first + n] = target[n * cells : (n + 1) * cells]


def encode(strips, *weights_and_biases):
    cells = strips[0].shape[0]
    return pl.pallas_call(
        functools.partial(encode_kernel, len(strips)),
        out_shape=jax.ShapeDtypeStruct((len(strips), cells, weights_and_biases[-1].shape[1]), BF16),
        compiler_params=params(),
        cost_estimate=pl.CostEstimate(flops=10**11, bytes_accessed=10**7, transcendentals=0),
        name="encode",
    )(*strips, *weights_and_biases)


def on_device(
    patches,
    norm_gain,
    norm_bias,
    up_weight,
    up_bias,
    down_weight,
    down_bias,
    final_gain,
    final_bias,
    head_weight,
    gauss_rows,
    tile_lists,
    alphas,
):
    view_count, tiles_view, cells, width = patches.shape
    feat = head_weight.shape[1]
    n_img = lax.axis_size("img")
    n_tile = lax.axis_size("tile")
    peers = n_img * n_tile
    both = ("img", "tile")
    held = gauss_rows.shape[0]
    group_views, strip_tiles, list_len = tile_lists.shape
    tiles = group_views * strip_tiles
    cap = 2 * tiles * list_len // peers

    wide_layer = n_tile // 4
    near = n_img * wide_layer
    tile = lax.axis_index("tile")
    layer = tile // wide_layer
    low = layer < 2
    groups = [[i * n_tile + z * wide_layer + k for i in range(n_img) for k in range(wide_layer)] for z in range(4)]

    def moves(*pairs):
        return [(a * wide_layer + k, b * wide_layer + k) for a, b in pairs for k in range(wide_layer)]

    beside = moves((0, 1), (1, 0), (2, 3), (3, 2))
    middle = moves((1, 2), (2, 1))
    inwards = moves((0, 1), (3, 2))
    outwards = moves((1, 0), (2, 3))

    def move(x, pairs):
        return lax.ppermute(x, "tile", pairs)

    def exchange(x):
        return lax.all_to_all(x, both, split_axis=0, concat_axis=0, axis_index_groups=groups, tiled=True)

    def tie(*values):
        return lax.optimization_barrier(values)

    request, own, rank = index(tile_lists.reshape(tiles, list_len), peers, cap, held)
    weight = weights(alphas.reshape(tiles * cells, list_len))
    packed = jnp.concatenate([weight, own, rank], 0)
    request, patches = tie(request, patches)
    asked = lax.all_to_all(request, both, split_axis=0, concat_axis=0, tiled=True)
    chips = n_tile // 2
    core = tile % 2
    chip = tile // 2
    patches = patches.reshape(chips, 2, -1, width)
    others = lax.dynamic_index_in_dim(patches, 1 - core, 1, keepdims=False)
    others = move(others, [(a, a ^ 1) for a in range(n_tile)])
    asked, others, packed = tie(asked, others, packed)
    far_to_outer = move(packed, moves((0, 3), (3, 0)))
    far_to_inner = move(packed, moves((0, 2), (3, 1)))
    pairs = jnp.concatenate([lax.dynamic_index_in_dim(patches, core, 1, keepdims=False), others], 1)
    strips = []
    for n in range(chips):
        pair = lax.dynamic_index_in_dim(pairs, lax.rem(chip + n, chips), 0, keepdims=False)
        strips.append(move(pair, [(a, (a + 2 * n) % n_tile) for a in range(n_tile)]) if n else pair)
    view = jnp.arange(n_tile, dtype=I32)
    place = lax.rem(chip + chips - view // 2, chips) * 2 + (view % 2 != core).astype(I32)
    asked = asked.reshape(n_img, 4, wide_layer, cap)
    sets = (jnp.where(low, 3, 0), jnp.where(low, 2, 1), layer ^ 1, layer)
    lists = [lax.dynamic_index_in_dim(asked, s, 1, keepdims=False).reshape(near, cap) for s in sets]
    owners = (
        jnp.arange(n_img, dtype=I32)[:, None] * n_tile
        + layer * wide_layer
        + jnp.arange(wide_layer, dtype=I32)[None, :]
    ).reshape(near)

    def spread_of(*packs):
        return spread(owners, packs, tiles, cells, cap)

    looked, lists[1] = tie(gather(lists[0], gauss_rows), lists[1])
    rows_1 = exchange(looked)
    looked_2 = gather(lists[1], gauss_rows)
    looked_2, lists[2] = tie(looked_2, lists[2])
    spread_1 = spread_of(far_to_outer, far_to_inner)
    looked_3 = gather(lists[2], gauss_rows)
    looked_2, looked_3, spread_1, rows_1, packed = tie(looked_2, looked_3, spread_1, rows_1, packed)

    rows_2 = exchange(looked_2)
    part_1 = blend(spread_1, rows_1)
    moved_1 = move(part_1, inwards)
    near_to_outer = move(packed, moves((1, 3), (2, 0)))
    near_to_inner = move(packed, middle)
    from_beside = move(packed, beside)
    part_1, *strips = tie(part_1, *strips)
    target = encode(
        strips, norm_gain, norm_bias, up_weight, up_bias, down_weight, down_bias, final_gain, final_bias, head_weight
    )
    looked_3, rows_2, part_1, target, lists[3], near_to_outer, near_to_inner, from_beside = tie(
        looked_3, rows_2, part_1, target, lists[3], near_to_outer, near_to_inner, from_beside
    )

    rows_3 = exchange(looked_3)
    far = move(part_1 + moved_1, middle)
    spread_2 = spread_of(near_to_outer, near_to_inner)
    part_2 = blend(spread_2, rows_2)
    moved_2 = move(part_2, inwards)
    part_2, lists[3], from_beside = tie(part_2, lists[3], from_beside)
    looked_4 = gather(lists[3], gauss_rows)
    spread_3 = spread_of(from_beside)
    looked_4, rows_3, far, spread_3, packed = tie(looked_4, rows_3, far, spread_3, packed)

    rows_4 = exchange(looked_4)
    part_3 = blend(spread_3, rows_3, (far,))
    beside_part = move(part_3, beside)
    part_2, moved_2, part_3, packed = tie(part_2, moved_2, part_3, packed)
    middle_part = move(part_2 + moved_2, middle)
    spread_4 = spread_of(packed)
    color, diff = blend(spread_4, rows_4, (beside_part, middle_part), place, target.reshape(n_tile, -1, feat))
    spreads = (spread_1, spread_2, spread_3, spread_4)

    diff_beside = move(diff, beside)
    diff_middle = move(diff, middle)
    far_middle = move(diff_beside, middle)
    diff_out = move(diff_middle, outwards)
    far_out = move(far_middle, outwards)
    back = []
    for n, diffs in ((3, (diff,)), (2, (diff_beside,)), (1, (diff_middle, diff_out)), (0, (far_middle, far_out))):
        term = terms(spreads[n], *diffs)
        if back:
            term, back[-1] = lax.optimization_barrier((term, back[-1]))
        back.append(exchange(term))
    grad = add_rows([lists[3], lists[2], lists[1]], back[:3], held)
    grad = add_rows([lists[0]], back[3:], held, grad)
    return (color.reshape(group_views, strip_tiles, cells, feat), grad)


def solution(mesh):
    placed = (
        P(("img", "tile"), None, None, None),
        P(),
        P(),
        P(),
        P(),
        P(),
        P(),
        P(),
        P(),
        P(),
        P(("img", "tile"), None),
        P("img", "tile", None),
        P("img", "tile", None, None),
    )
    return jax.shard_map(
        on_device,
        mesh=mesh,
        in_specs=placed,
        out_specs=(P("img", "tile", None, None), P(("img", "tile"), None)),
        check_vma=False,
    )
```
